128 devices in a mesh: blocks: 32 (over z, x, core), chan: 4 (over y).
Axes of the slice: x: 4, y: 4, z: 4, core: 2. Of those that a mesh axis runs over, the one named last changes fastest.
Arguments:
- feats: bfloat16 [1024, 256, 512], P('blocks', 'chan')
- conv_weights: bfloat16 [3, 7, 256, 256], P(None, None, 'chan'), may hold values from -0.125 to 0.125
- norm_gain: float32 [3, 256], P(None, 'chan'), may hold values from 0.25 to 1.75
- norm_bias: float32 [3, 256], P(None, 'chan'), may hold values from -3 to 3
- time_bias: float32 [256], P('chan'), may hold values from -4 to 4
- local_nbr: int32 [1024, 6], P('blocks'), may hold values from 0 to 32, as said below
- face_links: int32 [32, 32, 2], P('blocks'), may hold values from 0 to 192, as said below
- coarse_send: int32 [32, 32, 2], P('blocks'), may hold values from 0 to 32, as said below
- coarse_recv: int32 [32, 32, 2], P('blocks'), may hold values from 0 to 64, as said below
Outputs:
- updated: bfloat16 [1024, 256, 512], P('blocks', 'chan')
The draws below stay inside these ranges and needn't reach their ends.
Inputs may be any that keep to these rules, and one draw needn't show every extreme that they name: local_nbr[s * 32 + b, f] is a slot of device s other than b, or 32 for none; the relation is mutual across faces f and f XOR 1. face_links[s, p, k] = 6 b + f names slot b and face f of device s for the k-th link of the pair s, p, and face_links[p, s, k] names the block and face f XOR 1 on p; 192 marks an unused link, at the same k on both sides and always for p = s; no face of a block appears twice on a device or also has a neighbour in local_nbr; some pair uses all 2 links. coarse_send[s, p, k] is a slot of device s sent to device p, or 32 for an unused place; every slot of every device appears exactly once; some pair uses all 2 places. coarse_recv[p, s, k] = 8 t + o is a tile and octant of device p, and equals 64 exactly where coarse_send[s, p, k] is 32; no code appears twice on a device; some device fills all 64 codes.
All inputs are finite; a program needn't handle non-finite values.
Results may differ from the reference program's by a relative error of at most 0.0029.
Values may be sent and summed in bfloat16 or wider, within the bound.
No kernel may reach another device: no remote copies, remote signals or barrier semaphores. Data moves between devices by JAX's collectives and lax.ppermute only.
A program may use at most 320 MiB of HBM per device.

```python
import math
import jax
import jax.numpy as jnp
from jax import lax

C = 256
GROUP = 8
SIDE = 8
BLK_DEV = 32
FACE_CAP = 2
TILE_DEV = 8
PIECE_CAP = 2
BLOCKS = 1024
VOX = 512
HALF_VOX = 64
N_BLOCKS = 32


def face_plan(key):
    devices = N_BLOCKS
    per_device = BLK_DEV
    order_keys = jax.random.split(jax.random.fold_in(key, 11), devices * 3)
    orders = jax.vmap(lambda sub_key: jax.random.permutation(sub_key, per_device))(order_keys)
    orders = orders.reshape(devices, 3, per_device).astype(jnp.int32)
    device_ids = jnp.arange(devices, dtype=jnp.int32)
    distance = jnp.abs(device_ids[:, None] - device_ids[None, :])
    near_counts = jax.random.randint(jax.random.fold_in(key, 12), (devices, devices), 0, 3).astype(jnp.int32)
    far_draws = jax.random.randint(jax.random.fold_in(key, 13), (devices, devices), 0, 16).astype(jnp.int32)
    far_counts = (far_draws == 0).astype(jnp.int32)
    drawn_counts = jnp.where(distance <= 4, near_counts, far_counts)
    upper_part = jnp.triu(drawn_counts, 1)
    pair_counts = upper_part + upper_part.T
    half_pair = (device_ids[:, None] == 0) & (device_ids[None, :] == devices // 2) | (device_ids[None, :] == 0) & (device_ids[:, None] == devices // 2)
    pair_counts = jnp.where(half_pair, jnp.maximum(pair_counts, 1), pair_counts)
    pair_counts = jnp.where(distance == 1, 2, pair_counts)
    pair_counts = jnp.where(distance == 0, 0, pair_counts)
    direction = (device_ids[:, None] + device_ids[None, :]) % 3
    above_peer = device_ids[None, :, None] > device_ids[:, None, None]
    above_other = device_ids[None, None, :] > device_ids[:, None, None]
    before = device_ids[None, None, :] < device_ids[None, :, None]
    matching = (direction[:, None, :] == direction[:, :, None]) & (above_peer == above_other) & before
    offsets = jnp.sum(jnp.where(matching, pair_counts[:, None, :], 0), axis=2)
    link_ids = jnp.arange(FACE_CAP, dtype=jnp.int32)
    position = offsets[:, :, None] + link_ids[None, None, :]
    in_use = link_ids[None, None, :] < pair_counts[:, :, None]
    upward = jnp.broadcast_to(device_ids[None, :, None] > device_ids[:, None, None], position.shape)
    remain = position % 3
    low_rank = 4 * (position // 3) + jnp.where(remain == 0, 0, jnp.where(remain == 1, 2, 3))
    high_rank = 4 * (position // 3) + remain + 1
    rank_in = jnp.minimum(jnp.where(upward, high_rank, low_rank), per_device - 1)
    axis_ids = jnp.broadcast_to(direction[:, :, None], position.shape)
    owners = jnp.broadcast_to(device_ids[:, None, None], position.shape)
    slot_ids = orders[owners, axis_ids, rank_in]
    face_ids = 2 * axis_ids + upward.astype(jnp.int32)
    link_codes = jnp.where(in_use, slot_ids * 6 + face_ids, 6 * per_device).astype(jnp.int32)
    lower_slots = orders[:, :, 0::4]
    upper_slots = orders[:, :, 1::4]
    device_index = jnp.broadcast_to(device_ids[:, None, None], lower_slots.shape)
    axis_index = jnp.broadcast_to(jnp.arange(3, dtype=jnp.int32)[None, :, None], lower_slots.shape)
    neighbours = jnp.full((devices, per_device, 6), per_device, jnp.int32)
    neighbours = neighbours.at[device_index, lower_slots, 2 * axis_index + 1].set(upper_slots)
    neighbours = neighbours.at[device_index, upper_slots, 2 * axis_index].set(lower_slots)
    return (neighbours.reshape(devices * per_device, 6), link_codes)


def coarse_plan(key):
    devices = N_BLOCKS
    per_device = BLK_DEV
    share = per_device // devices
    code_count = 8 * TILE_DEV
    device_ids = jnp.arange(devices, dtype=jnp.int32)
    popularity = jax.random.permutation(jax.random.fold_in(key, 21), devices).astype(jnp.int32)
    jitter = jax.random.randint(jax.random.fold_in(key, 22), (devices, devices), 0, devices // 2).astype(jnp.int32)
    scores = jnp.where(popularity[None, :] == 0, -1, popularity[None, :] + jitter)
    scores = scores * devices + device_ids[None, :]
    ranking = jnp.argsort(scores, axis=1, stable=True).astype(jnp.int32)
    placing = jnp.argsort(ranking, axis=1, stable=True).astype(jnp.int32)
    pair_counts = jnp.where(placing < devices // 4, 2 * share, jnp.where(placing < 3 * devices // 4, share, 0)).astype(jnp.int32)
    send_start = jnp.cumsum(pair_counts, axis=1) - pair_counts
    recv_start = jnp.cumsum(pair_counts, axis=0) - pair_counts
    piece_ids = jnp.arange(PIECE_CAP, dtype=jnp.int32)
    in_use = piece_ids[None, None, :] < pair_counts[:, :, None]
    slot_perm = jax.vmap(lambda sub_key: jax.random.permutation(sub_key, per_device))(jax.random.split(jax.random.fold_in(key, 23), devices)).astype(jnp.int32)
    code_perm = jax.vmap(lambda sub_key: jax.random.permutation(sub_key, code_count))(jax.random.split(jax.random.fold_in(key, 24), devices)).astype(jnp.int32)
    senders = jnp.broadcast_to(device_ids[:, None, None], in_use.shape)
    receivers = jnp.broadcast_to(device_ids[None, :, None], in_use.shape)
    send_rank = jnp.minimum(send_start[:, :, None] + piece_ids[None, None, :], per_device - 1)
    recv_rank = jnp.minimum(recv_start[:, :, None] + piece_ids[None, None, :], code_count - 1)
    sending = jnp.where(in_use, slot_perm[senders, send_rank], per_device).astype(jnp.int32)
    arriving = jnp.where(in_use, code_perm[receivers, recv_rank], code_count).astype(jnp.int32)
    return (sending, jnp.transpose(arriving, (1, 0, 2)))


def draw_local_nbr(key, part):
    return face_plan(key)[0]


def draw_face_links(key, part):
    return face_plan(key)[1]


def draw_coarse_send(key, part):
    return coarse_plan(key)[0]


def draw_coarse_recv(key, part):
    return coarse_plan(key)[1]


def draw_feats(key, part):
    key = jax.random.fold_in(key, 3)
    key_noise, key_channel = jax.random.split(key, 2)
    slot_ids = jnp.arange(BLOCKS, dtype=jnp.float32)
    ramp = 1.0 + 2.0 * slot_ids / (BLOCKS - 1)
    noise = jax.random.normal(key_noise, (BLOCKS, C, VOX), jnp.float32)
    channel_scale = jnp.exp(jax.random.uniform(key_channel, (C,), jnp.float32, math.log(0.5), math.log(2.0)))
    return (noise * channel_scale[None, :, None] * ramp[:, None, None]).astype(jnp.bfloat16)


def level_of(rng, shape, cuts, low, top_value):
    def one(dim, shards_of):
        heights = jax.random.uniform(jax.random.fold_in(jax.random.fold_in(rng, 6), dim), (shards_of,), jnp.float32, low / len(cuts), top_value / len(cuts))
        return jnp.repeat(jnp.exp(heights), shape[dim] // shards_of).reshape((-1,) + (1,) * (len(shape) - dim - 1))

    factor_of = one(*cuts[0])
    for cut in cuts[1:]:
        factor_of = factor_of * one(*cut)
    return factor_of


def gaussian(rng, shape, scale, reach, cuts=(), held_as=jnp.bfloat16):
    values = scale * jax.random.normal(rng, shape, jnp.float32)
    if cuts:
        values = values * level_of(rng, shape, cuts, -0.22, 0.18)
    return jnp.clip(values, -reach, reach).astype(held_as)


def setup_inputs(seed: int = 0) -> dict:
    streams_of = jax.random.split(jax.random.key(seed), 10)
    feats = draw_feats(jax.random.fold_in(streams_of[9], 71), 0)
    conv_weights = gaussian(streams_of[1], (3, 7, C, C), (7 * C) ** -0.5, 0.125, ((2, 4),))
    norm_gain = jnp.clip(1.0 + 0.15 * jax.random.normal(streams_of[2], (3, C), jnp.float32), 0.25, 1.75)
    norm_bias = gaussian(streams_of[3], (3, C), 0.5, 3.0, ((1, 4),), jnp.float32)
    time_bias = gaussian(streams_of[4], (C,), 1.0, 4.0, ((0, 4),), jnp.float32)
    local_nbr = draw_local_nbr(jax.random.fold_in(streams_of[9], 71), 0)
    face_links = draw_face_links(jax.random.fold_in(streams_of[9], 71), 0)
    coarse_send = draw_coarse_send(jax.random.fold_in(streams_of[9], 71), 0)
    coarse_recv = draw_coarse_recv(jax.random.fold_in(streams_of[9], 71), 0)
    return {"feats": feats, "conv_weights": conv_weights, "norm_gain": norm_gain, "norm_bias": norm_bias, "time_bias": time_bias, "local_nbr": local_nbr, "face_links": face_links, "coarse_send": coarse_send, "coarse_recv": coarse_recv}


EPS = 1e-05
OPPOSITE = (1, 0, 3, 2, 5, 4)

def face_layers(volume):
    return jnp.stack([volume[:, :, 0], volume[:, :, -1], volume[:, :, :, 0], volume[:, :, :, -1], volume[:, :, :, :, 0], volume[:, :, :, :, -1]], axis=1)

def tap_input(volume, border, which_face):
    along_axis = 2 + which_face // 2
    extent = volume.shape[along_axis]
    planes = jnp.expand_dims(border[:, which_face], along_axis)
    if which_face % 2 == 1:
        return jnp.concatenate([lax.slice_in_dim(volume, 1, extent, axis=along_axis), planes], axis=along_axis)
    return jnp.concatenate([planes, lax.slice_in_dim(volume, 0, extent - 1, axis=along_axis)], axis=along_axis)

def cross_conv(volume, border, weights):
    blocks_here, channels = (volume.shape[0], volume.shape[1])
    kernels = weights.astype(jnp.float32)
    running = jnp.einsum('oc,bcv->bov', kernels[0], volume.reshape(blocks_here, channels, -1).astype(jnp.float32), precision=lax.Precision.HIGHEST)
    for which_face in range(6):
        moved = tap_input(volume, border, which_face).reshape(blocks_here, channels, -1).astype(jnp.float32)
        running = running + jnp.einsum('oc,bcv->bov', kernels[1 + which_face], moved, precision=lax.Precision.HIGHEST)
    return running

def inverse_index(indices, extent, default_value):
    flat_codes = indices.reshape(-1).astype(jnp.int32)
    lookup = jnp.full((extent + 1,), default_value, jnp.int32)
    lookup = lookup.at[flat_codes].set(jnp.arange(flat_codes.shape[0], dtype=jnp.int32))
    return lookup[:extent]

def group_terms(values):
    rows, channels, cells = values.shape
    grouped = values.reshape(rows, channels // GROUP, GROUP, cells)
    return jnp.stack([lax.optimization_barrier(jnp.sum(grouped, axis=(0, 2, 3))), lax.optimization_barrier(jnp.sum(grouped * grouped, axis=(0, 2, 3)))])

def normalize_silu(values, totals, squares, entries, gain_row, bias_row):
    average = totals / entries
    spread = squares / entries - average * average
    inverse = lax.rsqrt(spread + EPS)
    average_full = jnp.repeat(average, GROUP)
    inverse_full = jnp.repeat(inverse, GROUP) * gain_row
    return jax.nn.silu((values - average_full[None, :, None]) * inverse_full[None, :, None] + bias_row[None, :, None])

def face_conv_all(activation, weights, local_src, remote_src, face_links):
    volumes = activation.reshape(N_BLOCKS, BLK_DEV, C, SIDE, SIDE, SIDE)
    layers = jax.vmap(face_layers)(volumes).reshape(N_BLOCKS, BLK_DEV * 6, C, SIDE, SIDE)
    padded = jnp.concatenate([layers, jnp.zeros((N_BLOCKS, 1, C, SIDE, SIDE), activation.dtype)], axis=1)
    device_ids = jnp.arange(N_BLOCKS, dtype=jnp.int32)
    blank = jnp.zeros((1, C, SIDE, SIDE), activation.dtype)

    def one_device(device):
        incoming = padded[device_ids[:, None], face_links[:, device, :]].reshape(N_BLOCKS * FACE_CAP, C, SIDE, SIDE)
        nearby = padded[device][local_src[device]]
        distant = jnp.concatenate([incoming, blank], axis=0)[remote_src[device]]
        border = (nearby + distant).reshape(BLK_DEV, 6, C, SIDE, SIDE)
        return cross_conv(volumes[device], border, weights)
    return lax.map(one_device, device_ids)

def assemble(octants, tile_count):
    channels = octants.shape[1]
    half_side = SIDE // 2
    arranged = octants.reshape(tile_count, 2, 2, 2, channels, half_side, half_side, half_side)
    arranged = jnp.transpose(arranged, (0, 4, 1, 5, 2, 6, 3, 7))
    return arranged.reshape(tile_count, channels, SIDE, SIDE, SIDE)

def split_octants(volume):
    tile_count, channels = (volume.shape[0], volume.shape[1])
    half_side = SIDE // 2
    arranged = volume.reshape(tile_count, channels, 2, half_side, 2, half_side, 2, half_side)
    arranged = jnp.transpose(arranged, (0, 2, 4, 6, 1, 3, 5, 7))
    return arranged.reshape(tile_count * 8, channels, half_side ** 3)

def upsample(pieces):
    blocks_here, channels = (pieces.shape[0], pieces.shape[1])
    half_side = SIDE // 2
    spread_out = pieces.reshape(blocks_here, channels, half_side, 1, half_side, 1, half_side, 1)
    spread_out = jnp.broadcast_to(spread_out, (blocks_here, channels, half_side, 2, half_side, 2, half_side, 2))
    return spread_out.reshape(blocks_here, channels, SIDE * SIDE * SIDE)

def reference(feats, conv_weights, norm_gain, norm_bias, time_bias, local_nbr, face_links, coarse_send, coarse_recv):
    half_side = SIDE // 2
    by_device = feats.reshape(N_BLOCKS, BLK_DEV, C, VOX)
    device_ids = jnp.arange(N_BLOCKS, dtype=jnp.int32)
    fine_entries = float(BLOCKS * VOX * GROUP)
    coarse_entries = float(BLOCKS * HALF_VOX * GROUP)
    opposite = jnp.array(OPPOSITE, jnp.int32)
    local_src = jnp.where(local_nbr < BLK_DEV, local_nbr * 6 + opposite[None, :], 6 * BLK_DEV).reshape(N_BLOCKS, BLK_DEV * 6).astype(jnp.int32)
    remote_src = jax.vmap(lambda indices: inverse_index(indices, 6 * BLK_DEV, N_BLOCKS * FACE_CAP))(face_links)
    first_stats = lax.optimization_barrier(jnp.sum(lax.map(lambda portion: group_terms(portion.astype(jnp.float32)), by_device), axis=0))
    first_act = lax.map(lambda portion: normalize_silu(portion.astype(jnp.float32), first_stats[0], first_stats[1], fine_entries, norm_gain[0], norm_bias[0]).astype(jnp.bfloat16), by_device)
    hidden = face_conv_all(first_act, conv_weights[0], local_src, remote_src, face_links) + time_bias[None, None, :, None]
    second_stats = lax.optimization_barrier(jnp.sum(lax.map(group_terms, hidden), axis=0))
    second_act = lax.map(lambda portion: normalize_silu(portion, second_stats[0], second_stats[1], fine_entries, norm_gain[1], norm_bias[1]).astype(jnp.bfloat16), hidden)
    branch = face_conv_all(second_act, conv_weights[1], local_src, remote_src, face_links)

    def pool(portion):
        cells = portion.astype(jnp.float32).reshape(BLK_DEV, C, half_side, 2, half_side, 2, half_side, 2)
        return lax.optimization_barrier(jnp.mean(cells, axis=(3, 5, 7))).reshape(BLK_DEV, C, HALF_VOX).astype(jnp.bfloat16)
    pooled = lax.map(pool, by_device)
    third_stats = lax.optimization_barrier(jnp.sum(lax.map(lambda portion: group_terms(portion.astype(jnp.float32)), pooled), axis=0))
    pooled_ext = jnp.concatenate([pooled.reshape(N_BLOCKS, BLK_DEV, C * HALF_VOX), jnp.zeros((N_BLOCKS, 1, C * HALF_VOX), jnp.bfloat16)], axis=1)
    tile_src = jax.vmap(lambda indices: inverse_index(indices, 8 * TILE_DEV, N_BLOCKS * PIECE_CAP))(coarse_recv)
    block_src = jax.vmap(lambda indices: inverse_index(indices, BLK_DEV, N_BLOCKS * PIECE_CAP))(coarse_send)
    blank_row = jnp.zeros((1, C * HALF_VOX), jnp.bfloat16)

    def tile_device(device):
        incoming = pooled_ext[device_ids[:, None], coarse_send[:, device, :]].reshape(N_BLOCKS * PIECE_CAP, C * HALF_VOX)
        rows_in = jnp.concatenate([incoming, blank_row], axis=0)[tile_src[device]]
        filled = (tile_src[device] < N_BLOCKS * PIECE_CAP).astype(jnp.float32)
        values = rows_in.reshape(8 * TILE_DEV, C, HALF_VOX).astype(jnp.float32)
        third_act = (normalize_silu(values, third_stats[0], third_stats[1], coarse_entries, norm_gain[2], norm_bias[2]) * filled[:, None, None]).astype(jnp.bfloat16)
        volume = assemble(third_act, TILE_DEV)
        border = jnp.zeros((TILE_DEV, 6, C, SIDE, SIDE), jnp.bfloat16)
        result = cross_conv(volume, border, conv_weights[2]).astype(jnp.bfloat16)
        return split_octants(result.reshape(TILE_DEV, C, SIDE, SIDE, SIDE)).reshape(8 * TILE_DEV, C * HALF_VOX)
    coarse = lax.map(tile_device, device_ids)
    coarse_ext = jnp.concatenate([coarse, jnp.zeros((N_BLOCKS, 1, C * HALF_VOX), jnp.bfloat16)], axis=1)

    def return_device(device):
        incoming = coarse_ext[device_ids[:, None], coarse_recv[:, device, :]].reshape(N_BLOCKS * PIECE_CAP, C * HALF_VOX)
        returned = incoming[block_src[device]].reshape(BLK_DEV, C, HALF_VOX)
        return upsample(returned)
    lifted = lax.map(return_device, device_ids)
    merged = by_device.astype(jnp.float32) + branch + lifted.astype(jnp.float32)
    return merged.astype(jnp.bfloat16).reshape(BLOCKS, C, VOX)
```

```python
import functools

import jax
import jax.numpy as jnp
import numpy as np
from jax import lax
from jax.experimental import pallas as pl
from jax.experimental.pallas import tpu as pltpu
from jax.sharding import PartitionSpec as P

GROUP = 8
SIDE = 8
VOX = 512
SLOTS = 32
DEVS = 32
QUART = 8
TILES = 2
FACES = 6 * SLOTS
CODES = 64
EPS = 1e-05
F32 = jnp.float32
BF16 = jnp.bfloat16
HIGH = lax.Precision.HIGHEST
NT = (((1,), (1,)), ((), ()))
NN = (((1,), (0,)), ((), ()))
VMEM = pl.BlockSpec(memory_space=pltpu.VMEM)
SMEM = pl.BlockSpec(memory_space=pltpu.SMEM)
LIMIT = 56 * 1024 * 1024


def tables():
    places = np.arange(VOX)
    coords = (places // 64, places // 8 % 8, places % 8)
    extract = np.zeros((7 * 64, VOX), np.float32)
    for face in range(6):
        along = face // 2
        others = [coords[k] for k in range(3) if k != along]
        chosen = coords[along] == (0 if face % 2 == 0 else SIDE - 1)
        extract[face * 64 + (8 * others[0] + others[1])[chosen], places[chosen]] = 1.0
    x, y, z = coords
    coarse = x // 2 * 16 + y // 2 * 4 + z // 2
    extract[384 + coarse, places] = 0.125
    lift = np.zeros((VOX, 64), np.float32)
    lift[places, coarse] = 1.0
    octant = x // 4 * 4 + y // 4 * 2 + z // 4
    inner = x % 4 * 16 + y % 4 * 4 + z % 4
    place = np.zeros((VOX, VOX), np.float32)
    place[places, octant * 64 + inner] = 1.0
    return extract, lift, place


def lanes(rows):
    return lax.broadcasted_iota(jnp.int32, (rows, 128), 1)


def terms(value):
    high = value.astype(BF16).astype(F32)
    rest = value - high
    middle = rest.astype(BF16).astype(F32)
    return high, middle, rest - middle


def joined(block, row):
    return (block[row + 2 : row + 3] + block[row + 1 : row + 2]) + block[row : row + 1]


def put_terms(ref, row, value):
    for k, part in enumerate(terms(value)):
        ref[row + k : row + k + 1, :] = part


def silu(u):
    return u * (1.0 / (1.0 + jnp.exp(-u)))


def group_matrix():
    row = lax.broadcasted_iota(jnp.int32, (128, 128), 0) % 64 // GROUP
    col = lax.broadcasted_iota(jnp.int32, (128, 128), 1) % 64 // GROUP
    return (row == col).astype(F32)


def group_sum(row):
    wide = jnp.broadcast_to(row, (8, 128))
    return lax.dot_general(wide, group_matrix(), NN, precision=HIGH, preferred_element_type=F32)[0:1]


def norm_rows(total, square, entries, gain):
    mean = total * (1.0 / entries)
    spread = square * (1.0 / entries) - mean * mean
    return mean, lax.rsqrt(spread + EPS) * gain


def invert(codes_ref, count, limit, out_ref, extent):
    def clear(i, _):
        out_ref[i] = 0
        return 0

    lax.fori_loop(0, extent, clear, 0)

    def mark(i, _):
        code = codes_ref[i]

        @pl.when(code < limit)
        def _():
            out_ref[code] = i + 1

        return 0

    lax.fori_loop(0, count, mark, 0)


def unpack(parts):
    left = lanes(32) < 64
    low, high = [], []
    for a, b in ((parts[0], parts[1]), (parts[2], parts[3])):
        low.append(jnp.where(left, a, pltpu.roll(b, 64, 1)))
        high.append(jnp.where(left, pltpu.roll(a, 64, 1), b))
    return jnp.concatenate(
        [jnp.concatenate(low, axis=1), jnp.concatenate(high, axis=1)], axis=0
    )


def pack(cells):
    left = lanes(32) < 64
    parts = []
    for half in range(2):
        low = cells[0:32, 128 * half : 128 * half + 128]
        high = cells[32:64, 128 * half : 128 * half + 128]
        parts.append(jnp.where(left, low, pltpu.roll(high, 64, 1)))
        parts.append(jnp.where(left, pltpu.roll(low, 64, 1), high))
    return parts


def spread_row(row):
    left = lanes(1) < 64
    parts = []
    for half in range(2):
        part = row[:, 128 * half : 128 * half + 128]
        turned = pltpu.roll(jnp.broadcast_to(part, (8, 128)), 64, 1)[0:1]
        parts.append(jnp.where(left, part, turned))
        parts.append(jnp.where(left, turned, part))
    return parts


def gather_row(rows):
    left = lanes(1) < 64
    return jnp.concatenate(
        [jnp.where(left, rows[0], rows[1]), jnp.where(left, rows[2], rows[3])], axis=1
    )


def extract_kernel(links, csend, feats, table, faces, out, pooled, stat):
    left = lanes(32) < 64

    def step(j, carry):
        s, q, ps, pq = carry
        rows = []
        for k in range(4):
            x = feats[4 * j + k]
            rows += [x, x]
            wide = x.astype(F32)
            for v in range(4):
                piece = wide[:, 128 * v : 128 * v + 128]
                s = s + piece
                q = q + piece * piece
        layers = lax.dot_general(
            table[...], jnp.concatenate(rows, axis=0), NT, preferred_element_type=F32
        )
        for k in range(4):
            for f in range(7):
                low = layers[64 * f : 64 * f + 32, 128 * k : 128 * k + 128]
                high = layers[64 * f + 32 : 64 * f + 64, 128 * k : 128 * k + 128]
                unit = jnp.where(left, low, high).astype(BF16)
                if f < 6:
                    faces[(4 * j + k) * 6 + f] = unit
                else:
                    pooled[4 * j + k] = unit
                    wide = unit.astype(F32)
                    ps = ps + wide
                    pq = pq + wide * wide
        return s, q, ps, pq

    zero = jnp.zeros((64, 128), F32)
    small = jnp.zeros((32, 128), F32)
    s, q, ps, pq = lax.fori_loop(0, 8, step, (zero, zero, small, small))
    ones = jnp.ones((8, 128), F32)

    def by_lane(sums):
        twice = jnp.concatenate([sums, sums], axis=0)
        return lax.dot_general(ones, twice, NT, precision=HIGH, preferred_element_type=F32)[0:1]

    stat[...] = jnp.zeros((32, 128), F32)
    put_terms(stat, 0, by_lane(s))
    put_terms(stat, 3, by_lane(q))
    put_terms(stat, 6, jnp.sum(ps, axis=0, keepdims=True))
    put_terms(stat, 9, jnp.sum(pq, axis=0, keepdims=True))
    sums = stat[...].astype(BF16)

    def send(p, _):
        for k in range(2):
            out[p * 5 + k] = faces[jnp.minimum(links[2 * p + k], FACES - 1)]
            out[p * 5 + 2 + k] = pooled[jnp.minimum(csend[2 * p + k], SLOTS - 1)]
        out[p * 5 + 4] = sums
        return 0

    lax.fori_loop(0, DEVS, send, 0)


def border1_kernel(nbr, links, crecv, me, faces, recv, par, o0, o1, o2, o3, inv, tinv, stat):
    invert(links, 2 * DEVS, FACES, inv, FACES)
    invert(crecv, 2 * DEVS, CODES, tinv, CODES)
    y = me[0]

    def add(s, total):
        return total + recv[s * 5 + 4].astype(F32)

    sums = lax.fori_loop(0, DEVS, add, jnp.zeros((32, 128), F32))
    fine = float(DEVS * SLOTS * VOX * GROUP)
    rough = float(DEVS * SLOTS * 64 * GROUP)
    mean1, scale1 = norm_rows(
        group_sum(joined(sums, 0)) * 0.5, group_sum(joined(sums, 3)) * 0.5, fine, par[0:1]
    )
    mean3, scale3 = norm_rows(
        group_sum(joined(sums, 6)), group_sum(joined(sums, 9)), rough, par[2:3]
    )
    bias1, bias3 = par[1:2], par[3:4]
    stat[...] = jnp.zeros((32, 128), F32)
    put_terms(stat, 0, mean1)
    put_terms(stat, 3, scale1)
    put_terms(stat, 6, bias1)
    put_terms(stat, 9, par[4:5])
    told = stat[...].astype(BF16)
    for r, o in enumerate((o0, o1, o2, o3)):
        q = (y + r) & 3

        def face(i, _):
            for f in range(6):
                at = q * 48 + i * 6 + f
                near, far = nbr[at], inv[at]
                link = jnp.maximum(far - 1, 0)
                here = faces[jnp.minimum(near, SLOTS - 1) * 6 + (f ^ 1)].astype(F32)
                there = recv[(link // 2) * 5 + link % 2].astype(F32)
                u = jnp.where(near < SLOTS, here, there)
                v = silu((u - mean1) * scale1 + bias1)
                some = jnp.logical_or(near < SLOTS, far > 0)
                o[i * 6 + f] = jnp.where(some, v, 0.0).astype(BF16)
            return 0

        lax.fori_loop(0, QUART, face, 0)

        def octant(i, _):
            for k in range(4):
                far = tinv[q * 16 + i * 4 + k]
                link = jnp.maximum(far - 1, 0)
                u = recv[(link // 2) * 5 + 2 + link % 2].astype(F32)
                v = silu((u - mean3) * scale3 + bias3)
                o[48 + i * 4 + k] = jnp.where(far > 0, v, 0.0).astype(BF16)
            return 0

        lax.fori_loop(0, 4, octant, 0)
        o[64] = told


def build_taps(act, border, taps, shift):
    wide = act.astype(F32)
    cube = wide.reshape(8, 8, 8, 256)
    taps[:, 0:256] = act
    taps[0:64, 256:512] = border(0).astype(BF16)
    taps[64:512, 256:512] = act[0:448]
    taps[0:448, 512:768] = act[64:512]
    taps[448:512, 512:768] = border(1).astype(BF16)
    low = jnp.concatenate([border(2).reshape(8, 1, 8, 256), cube[:, 0:7]], axis=1)
    taps[:, 768:1024] = low.reshape(512, 256).astype(BF16)
    high = jnp.concatenate([cube[:, 1:8], border(3).reshape(8, 1, 8, 256)], axis=1)
    taps[:, 1024:1280] = high.reshape(512, 256).astype(BF16)
    for f, amount in ((4, 1), (5, 511)):
        turned = pltpu.roll(wide, amount, 0)
        edge = border(f)
        for half in range(2):
            shift[...] = turned[:, 128 * half : 128 * half + 128]
            shift[pl.ds(0 if f == 4 else 7, 64, stride=8), :] = edge[:, 128 * half : 128 * half + 128]
            taps[:, 256 * (f + 1) + 128 * half : 256 * (f + 1) + 128 * half + 128] = shift[
                ...
            ].astype(BF16)


def fill_weights(dst, gathered, which):
    for c in range(4):
        for t in range(7):
            dst[64 * c : 64 * c + 64, 256 * t : 256 * t + 256] = gathered[c, which, t]


def conv1_kernel(
    me, v0, v1, v2, v3, u0, u1, u2, u3, weights, place, place_t,
    hid, o0, o1, o2, o3,
    units, outs, wfine, wrough, rows, taps, shift, cube, stat, sums,
):
    step = pl.program_id(0)
    y = me[0]

    @pl.when(step == 0)
    def _():
        for r, u in enumerate((u0, u1, u2, u3)):
            units[(y - r) & 3] = u[...]
        fill_weights(wfine, weights, 0)
        fill_weights(wrough, weights, 2)
        for k in range(4):
            rows[k : k + 1, :] = gather_row([joined(units[c, 64].astype(F32), 3 * k) for c in range(4)])
        sums[...] = jnp.zeros((8, 256), F32)
        stat[...] = jnp.zeros((4, 32, 128), F32)

    def unit(i):
        return unpack([units[c, i].astype(F32) for c in range(4)])

    @pl.when(step < QUART)
    def _():
        for r, v in enumerate((v0, v1, v2, v3)):
            at = pl.multiple_of(((y - r) & 3) * 64, 64)
            cube[pl.ds(at, 64), :] = v[0].astype(F32)
        x = cube[...].T
        act = silu((x - rows[0:1]) * rows[1:2] + rows[2:3]).astype(BF16)
        build_taps(act, lambda f: unit(step * 6 + f), taps, shift)
        h = lax.dot_general(taps[...], wfine[...], NT, preferred_element_type=F32) + rows[3:4]
        hid[0] = h
        total = jnp.sum(h, axis=0, keepdims=True)
        sums[0:1] += total
        sums[1:2] += jnp.sum(h * h, axis=0, keepdims=True)
        centre = (total * (1.0 / VOX)).astype(BF16).astype(F32)
        for c, part in enumerate(spread_row(centre)):
            stat[c, pl.ds(step, 1), :] = part
        deep = h.reshape(8, 8, 8, 256)
        edges = [[], []]
        for half in range(2):
            shift[...] = h[:, 128 * half : 128 * half + 128]
            for side in range(2):
                edges[side].append(shift[pl.ds(7 * side, 64, stride=8), :])
        for f in range(6):
            if f < 2:
                layer = h[448 * f : 448 * f + 64]
            elif f < 4:
                layer = deep[:, 7 * (f - 2)].reshape(64, 256)
            else:
                layer = jnp.concatenate(edges[f - 4], axis=1)
            for c, part in enumerate(pack(layer - centre)):
                outs[c, step * 6 + f] = part.astype(BF16)

    @pl.when(step >= QUART)
    def _():
        t = step - QUART
        octants = jnp.concatenate([unit(48 + 8 * t + o).astype(BF16) for o in range(8)], axis=0)
        act = lax.dot_general(place[...], octants, NN, preferred_element_type=F32).astype(BF16)
        blank = jnp.zeros((64, 256), F32)
        build_taps(act, lambda f: blank, taps, shift)
        h = lax.dot_general(taps[...], wrough[...], NT, preferred_element_type=F32).astype(BF16)
        pieces = lax.dot_general(place_t[...], h, NN, preferred_element_type=F32)
        for o in range(8):
            for c, part in enumerate(pack(pieces[64 * o : 64 * o + 64])):
                outs[c, 48 + 8 * t + o] = part.astype(BF16)

    @pl.when(step == QUART + TILES - 1)
    def _():
        totals = spread_row(sums[0:1])
        squares = spread_row(sums[1:2])
        for c in range(4):
            for k, part in enumerate(terms(totals[c])):
                stat[c, 8 + k : 9 + k, :] = part
            for k, part in enumerate(terms(squares[c])):
                stat[c, 11 + k : 12 + k, :] = part
            outs[c, 64] = stat[c].astype(BF16)
        for r, o in enumerate((o0, o1, o2, o3)):
            o[...] = outs[(y + r) & 3]


def route2_kernel(links, crecv, me, v0, v1, v2, v3, held, out, cen, stat):
    y = me[0]
    for r, v in enumerate((v0, v1, v2, v3)):
        held[(y - r) & 3] = v[...]
    total = jnp.zeros((32, 128), F32)
    for q in range(4):
        told = held[q, 64].astype(F32)
        cen[8 * q : 8 * q + 8, :] = told[0:8]
        total = total + told
    stat[...] = jnp.zeros((32, 128), F32)
    put_terms(stat, 2, joined(total, 8))
    put_terms(stat, 5, joined(total, 11))

    def send(p, _):
        for k in range(2):
            code = jnp.minimum(links[2 * p + k], FACES - 1)
            slot = code // 6
            q = slot // 8
            out[p * 5 + k] = held[q, code - 48 * q]
            stat[k : k + 1, :] = cen[pl.ds(slot, 1), :]
            place = jnp.minimum(crecv[2 * p + k], CODES - 1)
            q = place // 16
            out[p * 5 + 2 + k] = held[q, 48 + place - 16 * q]
        out[p * 5 + 4] = stat[...].astype(BF16)
        return 0

    lax.fori_loop(0, DEVS, send, 0)


def border2_kernel(
    nbr, links, csend, me, held, recv, par, o0, o1, o2, o3, inv, sinv, cen, far_cen, stat
):
    invert(links, 2 * DEVS, FACES, inv, FACES)
    invert(csend, 2 * DEVS, SLOTS, sinv, SLOTS)
    y = me[0]
    for q in range(4):
        cen[8 * q : 8 * q + 8, :] = held[q, 64].astype(F32)[0:8]

    def add(s, total):
        told = recv[s * 5 + 4].astype(F32)
        far_cen[pl.ds(2 * s, 2), :] = told[0:2]
        return total + told

    sums = lax.fori_loop(0, DEVS, add, jnp.zeros((32, 128), F32))
    fine = float(DEVS * SLOTS * VOX * GROUP)
    mean, scale = norm_rows(
        group_sum(joined(sums, 2)) * 0.5, group_sum(joined(sums, 5)) * 0.5, fine, par[0:1]
    )
    bias = par[1:2]
    stat[...] = jnp.zeros((32, 128), F32)
    put_terms(stat, 0, mean)
    put_terms(stat, 3, scale)
    put_terms(stat, 6, bias)
    told = stat[...].astype(BF16)
    for r, o in enumerate((o0, o1, o2, o3)):
        q = (y + r) & 3

        def face(i, _):
            for f in range(6):
                at = q * 48 + i * 6 + f
                near, far = nbr[at], inv[at]
                link = jnp.maximum(far - 1, 0)
                slot = jnp.minimum(near, SLOTS - 1)
                quarter = slot // 8
                here = held[quarter, (slot - 8 * quarter) * 6 + (f ^ 1)].astype(F32)
                there = recv[(link // 2) * 5 + link % 2].astype(F32)
                u = jnp.where(near < SLOTS, here, there)
                centre = jnp.where(
                    near < SLOTS, cen[pl.ds(slot, 1), :], far_cen[pl.ds(link, 1), :]
                )
                v = silu((u + (centre - mean)) * scale + bias)
                some = jnp.logical_or(near < SLOTS, far > 0)
                o[i * 6 + f] = jnp.where(some, v, 0.0).astype(BF16)
            link = jnp.maximum(sinv[q * 8 + i] - 1, 0)
            o[48 + i] = recv[(link // 2) * 5 + 2 + link % 2]
            return 0

        lax.fori_loop(0, QUART, face, 0)
        o[56] = told


def conv2_kernel(
    me, hid, v0, v1, v2, v3, u0, u1, u2, u3, weights, lift,
    o0, o1, o2, o3,
    units, wfine, rows, taps, shift, cube,
):
    step = pl.program_id(0)
    y = me[0]

    @pl.when(step == 0)
    def _():
        for r, u in enumerate((u0, u1, u2, u3)):
            units[(y - r) & 3] = u[...]
        fill_weights(wfine, weights, 1)
        for k in range(3):
            rows[k : k + 1, :] = gather_row([joined(units[c, 56].astype(F32), 3 * k) for c in range(4)])

    def unit(i):
        return unpack([units[c, i].astype(F32) for c in range(4)])

    act = silu((hid[0] - rows[0:1]) * rows[1:2] + rows[2:3]).astype(BF16)
    build_taps(act, lambda f: unit(step * 6 + f), taps, shift)
    branch = lax.dot_general(taps[...], wfine[...], NT, preferred_element_type=F32)
    lifted = lax.dot_general(
        lift[...], unit(48 + step).astype(BF16), NN, preferred_element_type=F32
    )
    for r, v in enumerate((v0, v1, v2, v3)):
        at = pl.multiple_of(((y - r) & 3) * 64, 64)
        cube[pl.ds(at, 64), :] = v[0].astype(F32)
    cube[...] += (branch + lifted).T
    for r, o in enumerate((o0, o1, o2, o3)):
        at = pl.multiple_of(((y + r) & 3) * 64, 64)
        o[0] = cube[pl.ds(at, 64), :].astype(BF16)


def shape(*dims, dtype=BF16):
    return jax.ShapeDtypeStruct(dims, dtype)


def params(**more):
    return pltpu.CompilerParams(vmem_limit_bytes=LIMIT, **more)


def exchange(parts):
    out = [parts[0]]
    got = {}
    for r in (2, 1, 3):
        got[r] = lax.ppermute(parts[r], "chan", [(i, (i + r) % 4) for i in range(4)])
    return out + [got[1], got[2], got[3]]


def over_blocks(units):
    return lax.all_to_all(units, "blocks", split_axis=0, concat_axis=0, tiled=True)


def local(
    feats,
    conv_weights,
    norm_gain,
    norm_bias,
    time_bias,
    local_nbr,
    face_links,
    coarse_send,
    coarse_recv,
):
    extract_np, lift_np, place_np = tables()
    y = lax.axis_index("chan").astype(jnp.int32)
    me = y[None]
    nbr = local_nbr.reshape(-1)
    links = face_links.reshape(-1)
    csend = coarse_send.reshape(-1)
    crecv = coarse_recv.reshape(-1)

    def twice(rows):
        block = jnp.stack(rows)
        block = jnp.concatenate([block, block], axis=1)
        return jnp.pad(block, ((0, 8 - block.shape[0]), (0, 0)))

    par1 = twice([norm_gain[0], norm_bias[0], norm_gain[2], norm_bias[2], time_bias])
    par2 = twice([norm_gain[1], norm_bias[1]])
    weights = lax.all_gather(conv_weights, "chan", axis=0, tiled=False)

    volumes = exchange(
        [
            lax.dynamic_slice_in_dim(feats, QUART * ((y + r) % 4), QUART, axis=0)
            for r in range(4)
        ]
    )

    faces, outgoing = pl.pallas_call(
        extract_kernel,
        out_shape=(shape(FACES, 32, 128), shape(5 * DEVS, 32, 128)),
        in_specs=[SMEM, SMEM, VMEM, VMEM],
        out_specs=(VMEM, VMEM),
        scratch_shapes=[pltpu.VMEM((SLOTS, 32, 128), BF16), pltpu.VMEM((32, 128), F32)],
        compiler_params=params(),
        name="extract",
    )(links, csend, feats, jnp.asarray(extract_np, BF16))
    arrived = over_blocks(outgoing)

    parts = pl.pallas_call(
        border1_kernel,
        out_shape=(shape(65, 32, 128),) * 4,
        in_specs=[SMEM] * 4 + [VMEM] * 3,
        out_specs=(VMEM,) * 4,
        scratch_shapes=[
            pltpu.SMEM((FACES,), jnp.int32),
            pltpu.SMEM((CODES,), jnp.int32),
            pltpu.VMEM((32, 128), F32),
        ],
        compiler_params=params(),
        name="border1",
    )(nbr, links, crecv, me, faces, arrived, par1)
    units1 = exchange(parts)

    block = pl.BlockSpec((1, 64, VOX), lambda i: (jnp.minimum(i, QUART - 1), 0, 0))
    hidden, *parts = pl.pallas_call(
        conv1_kernel,
        grid=(QUART + TILES,),
        out_shape=(shape(QUART, VOX, 256, dtype=F32),) + (shape(65, 32, 128),) * 4,
        in_specs=[SMEM] + [block] * 4 + [VMEM] * 7,
        out_specs=(pl.BlockSpec((1, VOX, 256), lambda i: (jnp.minimum(i, QUART - 1), 0, 0)),)
        + (VMEM,) * 4,
        scratch_shapes=[
            pltpu.VMEM((4, 65, 32, 128), BF16),
            pltpu.VMEM((4, 65, 32, 128), BF16),
            pltpu.VMEM((256, 1792), BF16),
            pltpu.VMEM((256, 1792), BF16),
            pltpu.VMEM((8, 256), F32),
            pltpu.VMEM((VOX, 1792), BF16),
            pltpu.VMEM((VOX, 128), F32),
            pltpu.VMEM((256, VOX), F32),
            pltpu.VMEM((4, 32, 128), F32),
            pltpu.VMEM((8, 256), F32),
        ],
        compiler_params=params(),
        name="conv1",
    )(
        me, *volumes, *units1, weights, jnp.asarray(place_np, BF16), jnp.asarray(place_np.T, BF16)
    )
    parts = exchange(parts)

    held, outgoing = pl.pallas_call(
        route2_kernel,
        out_shape=(shape(4, 65, 32, 128), shape(5 * DEVS, 32, 128)),
        in_specs=[SMEM] * 3 + [VMEM] * 4,
        out_specs=(VMEM, VMEM),
        scratch_shapes=[pltpu.VMEM((SLOTS, 128), F32), pltpu.VMEM((32, 128), F32)],
        compiler_params=params(),
        name="route2",
    )(links, crecv, me, *parts)
    arrived = over_blocks(outgoing)

    parts = pl.pallas_call(
        border2_kernel,
        out_shape=(shape(57, 32, 128),) * 4,
        in_specs=[SMEM] * 4 + [VMEM] * 3,
        out_specs=(VMEM,) * 4,
        scratch_shapes=[
            pltpu.SMEM((FACES,), jnp.int32),
            pltpu.SMEM((SLOTS,), jnp.int32),
            pltpu.VMEM((SLOTS, 128), F32),
            pltpu.VMEM((2 * DEVS, 128), F32),
            pltpu.VMEM((32, 128), F32),
        ],
        compiler_params=params(),
        name="border2",
    )(nbr, links, csend, me, held, arrived, par2)
    units2 = exchange(parts)

    block = pl.BlockSpec((1, 64, VOX), lambda i: (i, 0, 0))
    parts = pl.pallas_call(
        conv2_kernel,
        grid=(QUART,),
        out_shape=(shape(QUART, 64, VOX),) * 4,
        in_specs=[SMEM, pl.BlockSpec((1, VOX, 256), lambda i: (i, 0, 0))]
        + [block] * 4
        + [VMEM] * 6,
        out_specs=(block,) * 4,
        scratch_shapes=[
            pltpu.VMEM((4, 57, 32, 128), BF16),
            pltpu.VMEM((256, 1792), BF16),
            pltpu.VMEM((8, 256), F32),
            pltpu.VMEM((VOX, 1792), BF16),
            pltpu.VMEM((VOX, 128), F32),
            pltpu.VMEM((256, VOX), F32),
        ],
        compiler_params=params(),
        name="conv2",
    )(me, hidden, *volumes, *units2, weights, jnp.asarray(lift_np, BF16))
    parts = exchange(parts)

    out = jnp.zeros(feats.shape, feats.dtype)
    for r in range(4):
        out = lax.dynamic_update_slice_in_dim(out, parts[r], QUART * ((y - r) % 4), axis=0)
    return out


def solution(mesh):
    in_specs = (
        P("blocks", "chan", None),
        P(None, None, "chan", None),
        P(None, "chan"),
        P(None, "chan"),
        P("chan"),
        P("blocks", None),
        P("blocks", None, None),
        P("blocks", None, None),
        P("blocks", None, None),
    )
    out_specs = P("blocks", "chan", None)
    return jax.shard_map(local, mesh=mesh, in_specs=in_specs, out_specs=out_specs, check_vma=False)
```

```python
import functools

import jax
import jax.numpy as jnp
import numpy as np
from jax import lax
from jax.experimental import pallas as pl
from jax.experimental.pallas import tpu as pltpu
from jax.sharding import PartitionSpec as P

GROUP = 8
SIDE = 8
VOX = 512
SLOTS = 32
DEVS = 32
QUART = 8
TILES = 2
FACES = 6 * SLOTS
CODES = 64
EPS = 1e-05
F32 = jnp.float32
BF16 = jnp.bfloat16
HIGH = lax.Precision.HIGHEST
NT = (((1,), (1,)), ((), ()))
NN = (((1,), (0,)), ((), ()))
VMEM = pl.BlockSpec(memory_space=pltpu.VMEM)
ANY = pl.BlockSpec(memory_space=pl.ANY)
HBM = pl.BlockSpec(memory_space=pltpu.HBM)
SMEM = pl.BlockSpec(memory_space=pltpu.SMEM)
MIB = 1024 * 1024
ROWS = 144


def tables():
    places = np.arange(VOX)
    coords = (places // 64, places // 8 % 8, places % 8)
    extract = np.zeros((7 * 64, VOX), np.float32)
    for face in range(6):
        along = face // 2
        others = [coords[k] for k in range(3) if k != along]
        chosen = coords[along] == (0 if face % 2 == 0 else SIDE - 1)
        extract[face * 64 + (8 * others[0] + others[1])[chosen], places[chosen]] = 1.0
    x, y, z = coords
    extract[384 + x // 2 * 16 + y // 2 * 4 + z // 2, places] = 0.125
    return extract


def lanes(rows):
    return lax.broadcasted_iota(jnp.int32, (rows, 128), 1)


def terms(value):
    high = value.astype(BF16).astype(F32)
    rest = value - high
    middle = rest.astype(BF16).astype(F32)
    return high, middle, rest - middle


def joined(block, row):
    return (block[row + 2 : row + 3] + block[row + 1 : row + 2]) + block[row : row + 1]


def put_terms(ref, row, value):
    for k, part in enumerate(terms(value)):
        ref[row + k : row + k + 1, :] = part


def silu(u):
    half = 0.5 * u
    return half + half * jnp.tanh(half)


def group_matrix(period):
    row = lax.broadcasted_iota(jnp.int32, (128, 128), 0) % period // GROUP
    col = lax.broadcasted_iota(jnp.int32, (128, 128), 1) % period // GROUP
    return (row == col).astype(F32)


def group_sum(row, groups=None):
    wide = jnp.broadcast_to(row, (8, 128))
    groups = group_matrix(64) if groups is None else groups
    return lax.dot_general(wide, groups, NN, precision=HIGH, preferred_element_type=F32)[0:1]


def norm_rows(total, square, entries, gain):
    mean = total * (1.0 / entries)
    spread = square * (1.0 / entries) - mean * mean
    return mean, lax.rsqrt(spread + EPS) * gain


def unpack(parts):
    left = lanes(32) < 64
    low, high = [], []
    for a, b in ((parts[0], parts[1]), (parts[2], parts[3])):
        low.append(jnp.where(left, a, pltpu.roll(b, 64, 1)))
        high.append(jnp.where(left, pltpu.roll(a, 64, 1), b))
    return jnp.concatenate(
        [jnp.concatenate(low, axis=1), jnp.concatenate(high, axis=1)], axis=0
    )


def pack(cells):
    left = lanes(32) < 64
    parts = []
    for half in range(2):
        low = cells[0:32, 128 * half : 128 * half + 128]
        high = cells[32:64, 128 * half : 128 * half + 128]
        parts.append(jnp.where(left, low, pltpu.roll(high, 64, 1)))
        parts.append(jnp.where(left, pltpu.roll(low, 64, 1), high))
    return parts


def spread_row(row):
    left = lanes(1) < 64
    parts = []
    for half in range(2):
        part = row[:, 128 * half : 128 * half + 128]
        turned = pltpu.roll(jnp.broadcast_to(part, (8, 128)), 64, 1)[0:1]
        parts.append(jnp.where(left, part, turned))
        parts.append(jnp.where(left, turned, part))
    return parts


def gather_row(rows):
    left = lanes(1) < 64
    return jnp.concatenate(
        [jnp.where(left, rows[0], rows[1]), jnp.where(left, rows[2], rows[3])], axis=1
    )


def extract_kernel(links, csend, feats, table, faces, out, held, pooled, acc, stat, send_buf, sem):
    step = pl.program_id(0)
    left = lanes(32) < 64

    @pl.when(step == 0)
    def _():
        acc[...] = jnp.zeros((192, 128), F32)

    rows = []
    s = jnp.zeros((64, 128), F32)
    q = jnp.zeros((64, 128), F32)
    ps = jnp.zeros((32, 128), F32)
    pq = jnp.zeros((32, 128), F32)
    for k in range(4):
        x = feats[k]
        rows += [x, x]
        wide = x.astype(F32)
        for v in range(4):
            piece = wide[:, 128 * v : 128 * v + 128]
            s = s + piece
            q = q + piece * piece
    layers = lax.dot_general(
        table[...], jnp.concatenate(rows, axis=0), NT, preferred_element_type=F32
    )
    for k in range(4):
        for f in range(7):
            low = layers[64 * f : 64 * f + 32, 128 * k : 128 * k + 128]
            high = layers[64 * f + 32 : 64 * f + 64, 128 * k : 128 * k + 128]
            unit = jnp.where(left, low, high).astype(BF16)
            if f < 6:
                held[(4 * step + k) * 6 + f] = unit
            else:
                pooled[4 * step + k] = unit
                wide = unit.astype(F32)
                ps = ps + wide
                pq = pq + wide * wide
    acc[0:64, :] += s
    acc[64:128, :] += q
    acc[128:160, :] += ps
    acc[160:192, :] += pq

    @pl.when(step == pl.num_programs(0) - 1)
    def _():
        keep = pltpu.make_async_copy(held, faces, sem.at[0])
        keep.start()
        ones = jnp.ones((8, 128), F32)

        def by_lane(sums):
            twice = jnp.concatenate([sums, sums], axis=0)
            return lax.dot_general(ones, twice, NT, precision=HIGH, preferred_element_type=F32)[0:1]

        stat[...] = jnp.zeros((16, 128), F32)
        put_terms(stat, 0, by_lane(acc[0:64, :]))
        put_terms(stat, 3, by_lane(acc[64:128, :]))
        put_terms(stat, 6, jnp.sum(acc[128:160, :], axis=0, keepdims=True))
        put_terms(stat, 9, jnp.sum(acc[160:192, :], axis=0, keepdims=True))
        sums = stat[...].astype(BF16)

        def send(p, _):
            for k in range(2):
                send_buf[p, 32 * k : 32 * k + 32] = held[jnp.minimum(links[k, p], FACES - 1)]
                send_buf[p, 64 + 32 * k : 96 + 32 * k] = pooled[
                    jnp.minimum(csend[k, p], SLOTS - 1)
                ]
            send_buf[p, 128:144] = sums
            return 0

        lax.fori_loop(0, DEVS, send, 0, unroll=4)
        give = pltpu.make_async_copy(send_buf, out, sem.at[1])
        give.start()
        keep.wait()
        give.wait()


def plan_kernel(nbr, links, csend, crecv, sel, tsel, ssel):
    def slot_of(n, _):
        for f in range(6):
            near = nbr[f, n]
            sel[n * 6 + f] = jnp.where(near < SLOTS, near * 6 + (f ^ 1), FACES + 2 * DEVS)
        return 0

    lax.fori_loop(0, SLOTS, slot_of, 0)

    def empty(i, _):
        tsel[i] = 2 * DEVS
        return 0

    lax.fori_loop(0, CODES, empty, 0)

    def mark(p, _):
        for k in range(2):
            code = links[k, p]

            @pl.when(code < FACES)
            def _():
                sel[code] = FACES + 2 * p + k

            place = crecv[k, p]

            @pl.when(place < CODES)
            def _():
                tsel[place] = 2 * p + k

            slot = csend[k, p]

            @pl.when(slot < SLOTS)
            def _():
                ssel[slot] = 2 * p + k

        return 0

    lax.fori_loop(0, DEVS, mark, 0)


def octant1_kernel(tsel, me, recv, par, x1, x2, x3, o0, o1, o2, o3, own, buf, stat, sem):
    y = me[0]

    def add(s, total):
        return total + recv[s, 128:144].astype(F32)

    sums = lax.fori_loop(0, DEVS, add, jnp.zeros((16, 128), F32), unroll=8)
    fine = float(DEVS * SLOTS * VOX * GROUP)
    rough = float(DEVS * SLOTS * 64 * GROUP)
    mean1, scale1 = norm_rows(
        group_sum(joined(sums, 0)) * 0.5, group_sum(joined(sums, 3)) * 0.5, fine, par[0:1]
    )
    mean3, scale3 = norm_rows(
        group_sum(joined(sums, 6)), group_sum(joined(sums, 9)), rough, par[2:3]
    )
    bias1, bias3 = par[1:2], par[3:4]
    own[0:1, :] = mean1
    own[1:2, :] = scale1
    own[2:3, :] = bias1
    stat[...] = jnp.zeros((32, 128), F32)
    put_terms(stat, 0, mean1)
    put_terms(stat, 3, scale1)
    put_terms(stat, 6, bias1)
    put_terms(stat, 9, par[4:5])
    put_terms(stat, 12, par[5:6])
    put_terms(stat, 15, par[6:7])
    told = stat[...].astype(BF16)
    copies = []
    for r, o in enumerate((o0, o1, o2, o3)):
        q = (y + r) & 3
        buf[r, 16] = told

        def octant(i, _):
            for k in range(4):
                far = tsel[q * 16 + i * 4 + k]
                link = jnp.minimum(far, 2 * DEVS - 1)
                at = pl.multiple_of(64 + 32 * (link & 1), 32)
                u = recv[link >> 1, pl.ds(at, 32)].astype(F32)
                v = silu((u - mean3) * scale3 + bias3)
                buf[r, i * 4 + k] = (v * (far < 2 * DEVS).astype(F32)).astype(BF16)
            return 0

        lax.fori_loop(0, 4, octant, 0)
        copies.append(pltpu.make_async_copy(buf.at[r], o, sem.at[r]))
        copies[-1].start()
    for copy in copies:
        copy.wait()


def border1_kernel(sel, me, own, faces, recv, o0, o1, o2, o3, src, buf, sem, load):
    y = me[0]
    fetch = pltpu.make_async_copy(faces, src.at[pl.ds(0, FACES)], load)
    fetch.start()

    def place(s, _):
        src[FACES + 2 * s] = recv[s, 0:32]
        src[FACES + 2 * s + 1] = recv[s, 32:64]
        return 0

    lax.fori_loop(0, DEVS, place, 0, unroll=4)
    src[FACES + 2 * DEVS] = jnp.zeros((32, 128), BF16)
    mean, scale, bias = own[0:1], own[1:2], own[2:3]
    fetch.wait()
    copies = []
    for r, o in enumerate((o0, o1, o2, o3)):
        q = (y + r) & 3

        def face(i, _):
            for f in range(6):
                at = sel[q * 48 + i * 6 + f]
                u = src[at].astype(F32)
                v = silu((u - mean) * scale + bias)
                buf[r, i * 6 + f] = (v * (at < FACES + 2 * DEVS).astype(F32)).astype(BF16)
            return 0

        lax.fori_loop(0, QUART, face, 0)
        copies.append(pltpu.make_async_copy(buf.at[r], o, sem.at[r]))
        copies[-1].start()
    for copy in copies:
        copy.wait()


def interior_taps(act, taps):
    wide = act.astype(F32)
    cube = wide.reshape(8, 8, 8, 256)
    none = jnp.zeros((64, 256), BF16)
    wall = jnp.zeros((8, 1, 8, 256), F32)
    taps[:, 0:256] = act
    taps[0:64, 256:512] = none
    taps[64:512, 256:512] = act[0:448]
    taps[0:448, 512:768] = act[64:512]
    taps[448:512, 512:768] = none
    low = jnp.concatenate([wall, cube[:, 0:7]], axis=1)
    taps[:, 768:1024] = low.reshape(512, 256).astype(BF16)
    high = jnp.concatenate([cube[:, 1:8], wall], axis=1)
    taps[:, 1024:1280] = high.reshape(512, 256).astype(BF16)
    depth = lax.broadcasted_iota(jnp.int32, (512, 256), 0) % 8
    low = jnp.where(depth == 0, 0.0, pltpu.roll(wide, 1, 0))
    taps[:, 1280:1536] = low.astype(BF16)
    high = jnp.where(depth == 7, 0.0, pltpu.roll(wide, 511, 0))
    taps[:, 1536:1792] = high.astype(BF16)


def halves(first, second, core, which):
    def pieces(c, t):
        for side, part in enumerate((first, second)):
            yield pl.multiple_of(64 * c + 32 * (core ^ side), 32), part[c, which, t]

    return pieces


def fill_weights(dst, pieces):
    for c in range(4):
        for t in range(7):
            for at, rows in pieces(c, t):
                dst[pl.ds(at, rows.shape[0]), 256 * t : 256 * t + 256] = rows


def fill_tap_weights(dst, pieces):
    for c in range(4):
        for f in range(6):
            for at, rows in pieces(c, 1 + f):
                dst[f, pl.ds(at, rows.shape[0]), :] = rows


def fill_cube(cube, volumes, y):
    for r, v in enumerate(volumes):
        at = pl.multiple_of(((y - r) & 3) * 64, 64)
        cube[pl.ds(at, 64), :] = v[0].astype(F32)


def place_rows(rows, told, y, stat):
    rows[...] = jnp.zeros((8, 256), F32)
    for r, t in enumerate(told):
        stat[(y - r) & 3] = t[0].astype(F32)
    for k in range(6):
        rows[k : k + 1, :] = gather_row([joined(stat[c], 3 * k) for c in range(4)])


def inner1_kernel(
    me, t0, t1, t2, t3, v0, v1, v2, v3, wa, wb, part, rows, weights, stat, taps, cube
):
    y = me[0]

    @pl.when(pl.program_id(0) == 0)
    def _():
        place_rows(rows, (t0, t1, t2, t3), y, stat)
        fill_weights(weights, halves(wa, wb, me[1], 0))

    fill_cube(cube, (v0, v1, v2, v3), y)
    x = cube[...].T
    act = silu((x - rows[0:1]) * rows[1:2] + rows[2:3]).astype(BF16)
    interior_taps(act, taps)
    part[0] = lax.dot_general(taps[...], weights[...], NT, preferred_element_type=F32)


def inner2_kernel(me, rows, hid, wa, wb, part, weights, taps, cells, sem):
    step = pl.program_id(0)

    def fetch_cells(n):
        return pltpu.make_async_copy(hid.at[n], cells.at[n], sem.at[n])

    @pl.when(step == 0)
    def _():
        for n in range(QUART):
            fetch_cells(n).start()
        fill_weights(weights, halves(wa, wb, me[1], 1))

    fetch_cells(step).wait()
    act = silu((cells[step] - rows[0:1]) * rows[1:2] + rows[2:3]).astype(BF16)
    interior_taps(act, taps)
    part[0] = lax.dot_general(taps[...], weights[...], NT, preferred_element_type=F32)


def border_terms(units, tap_weights, parts, y, across):
    for r, u in enumerate(parts):
        units[(y - r) & 3] = u[...]
    for f in range(6):
        layer = jnp.concatenate(
            [
                unpack([units[c, 6 * n + f].astype(F32) for c in range(4)]).astype(BF16)
                for n in range(QUART)
            ],
            axis=0,
        )
        across[f] = lax.dot_general(layer, tap_weights[f], NT, preferred_element_type=F32)


def add_borders(h, across, step, shift):
    at = pl.multiple_of(step * 64, 64)
    h = jnp.concatenate(
        [h[0:64] + across[0, pl.ds(at, 64), :], h[64:448], h[448:512] + across[1, pl.ds(at, 64), :]],
        axis=0,
    )
    deep = h.reshape(8, 8, 8, 256)
    low = across[2, pl.ds(at, 64), :].reshape(8, 1, 8, 256)
    high = across[3, pl.ds(at, 64), :].reshape(8, 1, 8, 256)
    h = jnp.concatenate([deep[:, 0:1] + low, deep[:, 1:7], deep[:, 7:8] + high], axis=1)
    h = h.reshape(512, 256)
    halves, edges = [], [[], []]
    for half in range(2):
        cut = slice(128 * half, 128 * half + 128)
        shift[half] = h[:, cut]
        for side in range(2):
            layer = shift[half, pl.ds(7 * side, 64, stride=8), :]
            layer = layer + across[4 + side, pl.ds(at, 64), cut]
            shift[half, pl.ds(7 * side, 64, stride=8), :] = layer
            edges[side].append(layer)
        halves.append(shift[half])
    h = jnp.concatenate(halves, axis=1)
    return h, [jnp.concatenate(pair, axis=1) for pair in edges]


def outer1_kernel(
    me, rows, part, u0, u1, u2, u3, tiles, wa, wb,
    hid, o0, o1, o2, o3,
    units, outs, weights, across, shift, stat, sums, cells, sem,
):
    step = pl.program_id(0)
    y = me[0]

    def keep_cells(n):
        return pltpu.make_async_copy(cells.at[n], hid.at[n], sem.at[n])

    @pl.when(step == 0)
    def _():
        fill_tap_weights(weights, halves(wa, wb, me[1], 0))
        border_terms(units, weights, (u0, u1, u2, u3), y, across)
        sums[...] = jnp.zeros((8, 256), F32)
        stat[...] = jnp.zeros((4, 32, 128), F32)

    h, edges = add_borders(part[0] + rows[3:4], across, step, shift)
    cells[step] = h
    keep_cells(step).start()
    total = jnp.sum(h, axis=0, keepdims=True)
    sums[0:1] += total
    sums[1:2] += jnp.sum(h * h, axis=0, keepdims=True)
    centre = (total * (1.0 / VOX)).astype(BF16).astype(F32)
    for c, row in enumerate(spread_row(centre)):
        stat[c, pl.ds(step, 1), :] = row
    deep = h.reshape(8, 8, 8, 256)
    for f in range(6):
        if f < 2:
            layer = h[448 * f : 448 * f + 64]
        elif f < 4:
            layer = deep[:, 7 * (f - 2)].reshape(64, 256)
        else:
            layer = edges[f - 4]
        for c, unit in enumerate(pack(layer - centre)):
            outs[c, step * 6 + f] = unit.astype(BF16)

    @pl.when(step == QUART - 1)
    def _():
        at = 8
        for k in range(2):
            for half in range(2):
                for row in terms(sums[k : k + 1, 128 * half : 128 * half + 128]):
                    for c in range(4):
                        stat[c, at : at + 1, :] = row
                    at += 1
        for c in range(4):
            outs[c, 48] = stat[c].astype(BF16)
        for r, o in enumerate((o0, o1, o2, o3)):
            o[0:49] = outs[(y + r) & 3]
            o[49:65] = tiles[(y + r) & 3]
        for n in range(QUART):
            keep_cells(n).wait()


def placement(rows, columns, code):
    row = lax.broadcasted_iota(jnp.int32, (rows, columns), 0)
    column = lax.broadcasted_iota(jnp.int32, (rows, columns), 1)
    return (code(row) == column).astype(F32).astype(BF16)


def octant_code(v):
    x, y, z = v >> 6, (v >> 3) & 7, v & 7
    octant = (x >> 2) * 4 + (y >> 2) * 2 + (z >> 2)
    return octant * 64 + (x & 3) * 16 + (y & 3) * 4 + (z & 3)


def voxel_code(w):
    octant, x, y, z = w >> 6, (w >> 4) & 3, (w >> 2) & 3, w & 3
    x, y, z = x + 4 * (octant >> 2), y + 4 * ((octant >> 1) & 1), z + 4 * (octant & 1)
    return x * 64 + y * 8 + z


def coarse_code(v):
    return ((v >> 7) & 3) * 16 + ((v >> 4) & 3) * 4 + ((v >> 1) & 3)


def tile_kernel(me, u0, u1, u2, u3, wa, wb, out, units, weights, taps, place, place_t):
    t = pl.program_id(0)
    y = me[0]

    @pl.when(t == 0)
    def _():
        place[...] = placement(VOX, VOX, octant_code)
        place_t[...] = placement(VOX, VOX, voxel_code)
        fill_weights(weights, halves(wa, wb, me[1], 2))

    for r, u in enumerate((u0, u1, u2, u3)):
        units[(y - r) & 3] = u[...]
    octants = jnp.concatenate(
        [unpack([units[c, o].astype(F32) for c in range(4)]).astype(BF16) for o in range(8)], axis=0
    )
    act = lax.dot_general(place[...], octants, NN, preferred_element_type=F32).astype(BF16)
    interior_taps(act, taps)
    h = lax.dot_general(taps[...], weights[...], NT, preferred_element_type=F32).astype(BF16)
    pieces = lax.dot_general(place_t[...], h, NN, preferred_element_type=F32)
    for o in range(8):
        for c, unit in enumerate(pack(pieces[64 * o : 64 * o + 64])):
            out[c, o] = unit.astype(BF16)


def route2_kernel(
    links, crecv, me, v0, v1, v2, v3, keep, out, held, cen, stat, send_buf, sem
):
    y = me[0]
    for r, v in enumerate((v0, v1, v2, v3)):
        held[(y - r) & 3] = v[...]
    kept = pltpu.make_async_copy(held, keep, sem.at[0])
    kept.start()
    total = jnp.zeros((32, 128), F32)
    for q in range(4):
        told = held[q, 48].astype(F32)
        cen[8 * q : 8 * q + 8, :] = told[0:8]
        total = total + told
    stat[...] = jnp.zeros((16, 128), F32)
    for k in range(4):
        put_terms(stat, 2 + 3 * k, joined(total, 8 + 3 * k))

    def send(p, _):
        for k in range(2):
            code = jnp.minimum(links[k, p], FACES - 1)
            slot = lax.div(code, 6)
            q = slot >> 3
            send_buf[p, 32 * k : 32 * k + 32] = held[q, code - 48 * q]
            stat[k : k + 1, :] = cen[pl.ds(slot, 1), :]
            place = jnp.minimum(crecv[k, p], CODES - 1)
            send_buf[p, 64 + 32 * k : 96 + 32 * k] = held[place >> 4, 49 + (place & 15)]
        send_buf[p, 128:144] = stat[...].astype(BF16)
        return 0

    lax.fori_loop(0, DEVS, send, 0, unroll=4)
    give = pltpu.make_async_copy(send_buf, out, sem.at[1])
    give.start()
    kept.wait()
    give.wait()


def own_row(row, y):
    wide = jnp.broadcast_to(jnp.where(y >= 2, row[:, 128:256], row[:, 0:128]), (8, 128))
    turned = pltpu.roll(wide, 64, 1)
    left = lanes(8) < 64
    odd = (y & 1) == 1
    return jnp.where(left, jnp.where(odd, turned, wide), jnp.where(odd, wide, turned))[0:1]


def border2_kernel(
    sel, ssel, me, rows, held, recv, o0, o1, o2, o3, norm, src, cen, buf, sem, load
):
    y = me[0]
    fetches = []
    for q in range(4):
        fetches.append(
            pltpu.make_async_copy(held.at[q, pl.ds(0, 48)], src.at[pl.ds(48 * q, 48)], load.at[q])
        )
        fetches.append(pltpu.make_async_copy(held.at[q, 48], buf.at[q, 0], load.at[4 + q]))
    for fetch in fetches:
        fetch.start()

    def add(s, total):
        src[FACES + 2 * s] = recv[s, 0:32]
        src[FACES + 2 * s + 1] = recv[s, 32:64]
        told = recv[s, 128:144].astype(F32)
        cen[pl.ds(SLOTS + 2 * s, 2), :] = told[0:2]
        return total + told

    sums = lax.fori_loop(0, DEVS, add, jnp.zeros((16, 128), F32), unroll=8)
    src[FACES + 2 * DEVS] = jnp.zeros((32, 128), BF16)
    cen[pl.ds(SLOTS + 2 * DEVS, 8), :] = jnp.zeros((8, 128), F32)
    fine = float(DEVS * SLOTS * VOX * GROUP)
    groups = group_matrix(128)
    norm[...] = jnp.zeros((8, 256), F32)
    for half in range(2):
        cut = slice(128 * half, 128 * half + 128)
        mean, scale = norm_rows(
            group_sum(joined(sums, 2 + 3 * half), groups),
            group_sum(joined(sums, 8 + 3 * half), groups),
            fine,
            rows[4:5, cut],
        )
        norm[0:1, cut] = mean
        norm[1:2, cut] = scale
        norm[2:3, cut] = rows[5:6, cut]
    mean, scale, bias = (own_row(norm[k : k + 1, :], y) for k in range(3))
    for fetch in fetches:
        fetch.wait()
    for q in range(4):
        cen[8 * q : 8 * q + 8, :] = buf[q, 0].astype(F32)[0:8]
    copies = []
    for r, o in enumerate((o0, o1, o2, o3)):
        q = (y + r) & 3

        def face(i, _):
            for f in range(6):
                at = sel[q * 48 + i * 6 + f]
                owner = jnp.where(at < FACES, lax.div(at, 6), at - (FACES - SLOTS))
                u = src[at].astype(F32) + (cen[pl.ds(owner, 1), :] - mean)
                v = silu(u * scale + bias)
                buf[r, i * 6 + f] = (v * (at < FACES + 2 * DEVS).astype(F32)).astype(BF16)
            link = ssel[q * 8 + i]
            at = pl.multiple_of(64 + 32 * (link & 1), 32)
            buf[r, 48 + i] = recv[link >> 1, pl.ds(at, 32)]
            return 0

        lax.fori_loop(0, QUART, face, 0)
        copies.append(pltpu.make_async_copy(buf.at[r], o, sem.at[r]))
        copies[-1].start()
    for copy in copies:
        copy.wait()


def outer2_kernel(
    me, part, v0, v1, v2, v3, u0, u1, u2, u3, wa, wb,
    o0, o1, o2, o3,
    units, weights, across, shift, cube, lift,
):
    step = pl.program_id(0)
    y = me[0]

    @pl.when(step == 0)
    def _():
        lift[...] = placement(VOX, 64, coarse_code)
        fill_tap_weights(weights, halves(wa, wb, me[1], 1))
        border_terms(units, weights, (u0, u1, u2, u3), y, across)

    raised = unpack([units[c, 48 + step].astype(F32) for c in range(4)]).astype(BF16)
    lifted = lax.dot_general(lift[...], raised, NN, preferred_element_type=F32)
    h, _ = add_borders(part[0] + lifted, across, step, shift)
    fill_cube(cube, (v0, v1, v2, v3), y)
    cube[...] += h.T
    for r, o in enumerate((o0, o1, o2, o3)):
        at = pl.multiple_of(((y + r) & 3) * 64, 64)
        o[0] = cube[pl.ds(at, 64), :].astype(BF16)


def gather_kernel(me, p0, p1, p2, p3, out, sem):
    y = me[0]
    copies = []
    for r, p in enumerate((p0, p1, p2, p3)):
        at = pl.multiple_of(((y - r) & 3) * QUART, QUART)
        copies.append(pltpu.make_async_copy(p, out.at[pl.ds(at, QUART)], sem.at[r]))
        copies[-1].start()
    for copy in copies:
        copy.wait()


def shape(*dims, dtype=BF16):
    return jax.ShapeDtypeStruct(dims, dtype)


def call(kernel, name, mib, micros=1, **more):
    return pl.pallas_call(
        kernel,
        cost_estimate=pl.CostEstimate(
            flops=micros * 10**9, bytes_accessed=micros * 3 * 10**6, transcendentals=0
        ),
        compiler_params=pltpu.CompilerParams(vmem_limit_bytes=mib * MIB),
        name=name,
        **more,
    )


def exchange(parts, order=(0, 1, 2, 3)):
    got = {
        r: lax.ppermute(parts[r], "chan", [(i, (i + r) % 4) for i in order]) for r in (2, 1, 3)
    }
    return [parts[0], got[1], got[2], got[3]]


def over_blocks(units):
    return lax.all_to_all(units, "blocks", split_axis=0, concat_axis=0, tiled=True)


def local(
    feats,
    conv_weights,
    norm_gain,
    norm_bias,
    time_bias,
    local_nbr,
    face_links,
    coarse_send,
    coarse_recv,
):
    extract_np = tables()
    y = lax.axis_index("chan").astype(jnp.int32)
    core = (lax.axis_index("blocks") % 2).astype(jnp.int32)
    me = jnp.stack([y, core])
    nbr = local_nbr.T
    links = face_links[0].T
    csend = coarse_send[0].T
    crecv = coarse_recv[0].T

    def twice(rows):
        block = jnp.stack(rows)
        block = jnp.concatenate([block, block], axis=1)
        return jnp.pad(block, ((0, 8 - block.shape[0]), (0, 0)))

    par = twice(
        [norm_gain[0], norm_bias[0], norm_gain[2], norm_bias[2], time_bias]
        + [norm_gain[1], norm_bias[1]]
    )
    half = lax.dynamic_slice_in_dim(conv_weights, 32 * core, 32, axis=2)
    wa = lax.all_gather(half, "chan", axis=0, tiled=False)

    faces, outgoing = call(
        extract_kernel,
        "extract",
        60,
        grid=(8,),
        out_shape=(shape(FACES, 32, 128), shape(DEVS, ROWS, 128)),
        in_specs=[SMEM, SMEM, pl.BlockSpec((4, 64, VOX), lambda i: (i, 0, 0)), VMEM],
        out_specs=(HBM, HBM),
        scratch_shapes=[
            pltpu.VMEM((FACES, 32, 128), BF16),
            pltpu.VMEM((SLOTS, 32, 128), BF16),
            pltpu.VMEM((192, 128), F32),
            pltpu.VMEM((16, 128), F32),
            pltpu.VMEM((DEVS, ROWS, 128), BF16),
            pltpu.SemaphoreType.DMA((2,)),
        ],
    )(links, csend, feats, jnp.asarray(extract_np, BF16))
    arrived = over_blocks(outgoing)
    volumes = exchange(
        [
            lax.dynamic_slice_in_dim(feats, QUART * ((y + r) % 4), QUART, axis=0)
            for r in range(4)
        ]
    )
    sel, tsel, ssel = call(
        plan_kernel,
        "plan",
        4,
        20,
        out_shape=(
            shape(FACES, dtype=jnp.int32),
            shape(CODES, dtype=jnp.int32),
            shape(SLOTS, dtype=jnp.int32),
        ),
        in_specs=[SMEM] * 4,
        out_specs=(SMEM,) * 3,
    )(nbr, links, csend, crecv)

    *parts, own = call(
        octant1_kernel,
        "octant1",
        8,
        out_shape=(shape(17, 32, 128),) * 4 + (shape(8, 128, dtype=F32),),
        in_specs=[SMEM] * 2 + [VMEM] * 2 + [HBM] * 3,
        out_specs=(ANY,) * 4 + (VMEM,),
        scratch_shapes=[
            pltpu.VMEM((4, 17, 32, 128), BF16),
            pltpu.VMEM((32, 128), F32),
            pltpu.SemaphoreType.DMA((4,)),
        ],
    )(tsel, me, arrived, par, *volumes[1:])
    tiles1 = exchange(parts, (3, 2, 1, 0))
    wa, _ = lax.optimization_barrier((wa, own))
    wb = lax.ppermute(wa, "blocks", [(i, i ^ 1) for i in range(DEVS)])
    parts = call(
        border1_kernel,
        "border1",
        12,
        out_shape=(shape(48, 32, 128),) * 4,
        in_specs=[SMEM] * 2 + [VMEM, HBM, VMEM],
        out_specs=(ANY,) * 4,
        scratch_shapes=[
            pltpu.VMEM((FACES + 2 * DEVS + 1, 32, 128), BF16),
            pltpu.VMEM((4, 48, 32, 128), BF16),
            pltpu.SemaphoreType.DMA((4,)),
            pltpu.SemaphoreType.DMA,
        ],
    )(sel, me, own, faces, arrived)
    units1 = exchange(parts)

    slots = pl.BlockSpec((1, 64, VOX), lambda i: (i, 0, 0))
    cells = pl.BlockSpec((1, VOX, 256), lambda i: (i, 0, 0))
    last = pl.BlockSpec((1, 32, 128), lambda i: (16, 0, 0))
    part1, rows = call(
        inner1_kernel,
        "inner1",
        24,
        8,
        grid=(QUART,),
        out_shape=(shape(QUART, VOX, 256, dtype=F32), shape(8, 256, dtype=F32)),
        in_specs=[SMEM] + [last] * 4 + [slots] * 4 + [VMEM] * 2,
        out_specs=(cells, VMEM),
        scratch_shapes=[
            pltpu.VMEM((256, 1792), BF16),
            pltpu.VMEM((4, 32, 128), F32),
            pltpu.VMEM((VOX, 1792), BF16),
            pltpu.VMEM((256, VOX), F32),
        ],
    )(me, *tiles1, *volumes, wa, wb)
    eight = pl.BlockSpec((8, 32, 128), lambda t: (t, 0, 0))
    coarse = call(
        tile_kernel,
        "tiles",
        24,
        4,
        grid=(TILES,),
        out_shape=shape(4, 16, 32, 128),
        in_specs=[SMEM] + [eight] * 4 + [VMEM] * 2,
        out_specs=pl.BlockSpec((4, 8, 32, 128), lambda t: (0, t, 0, 0)),
        scratch_shapes=[
            pltpu.VMEM((4, 8, 32, 128), BF16),
            pltpu.VMEM((256, 1792), BF16),
            pltpu.VMEM((VOX, 1792), BF16),
            pltpu.VMEM((VOX, VOX), BF16),
            pltpu.VMEM((VOX, VOX), BF16),
        ],
    )(me, *tiles1, wa, wb)
    hidden, *parts = call(
        outer1_kernel,
        "outer1",
        32,
        5,
        grid=(QUART,),
        out_shape=(shape(QUART, VOX, 256, dtype=F32),) + (shape(65, 32, 128),) * 4,
        in_specs=[SMEM, VMEM, cells] + [VMEM] * 7,
        out_specs=(HBM,) + (VMEM,) * 4,
        scratch_shapes=[
            pltpu.VMEM((4, 48, 32, 128), BF16),
            pltpu.VMEM((4, 49, 32, 128), BF16),
            pltpu.VMEM((6, 256, 256), BF16),
            pltpu.VMEM((6, VOX, 256), F32),
            pltpu.VMEM((2, VOX, 128), F32),
            pltpu.VMEM((4, 32, 128), F32),
            pltpu.VMEM((8, 256), F32),
            pltpu.VMEM((QUART, VOX, 256), F32),
            pltpu.SemaphoreType.DMA((QUART,)),
        ],
    )(me, rows, part1, *units1, coarse, wa, wb)
    units = exchange(parts)

    held, outgoing = call(
        route2_kernel,
        "route2",
        12,
        out_shape=(shape(4, 65, 32, 128), shape(DEVS, ROWS, 128)),
        in_specs=[SMEM] * 3 + [VMEM] * 4,
        out_specs=(HBM, HBM),
        scratch_shapes=[
            pltpu.VMEM((4, 65, 32, 128), BF16),
            pltpu.VMEM((SLOTS, 128), F32),
            pltpu.VMEM((16, 128), F32),
            pltpu.VMEM((DEVS, ROWS, 128), BF16),
            pltpu.SemaphoreType.DMA((2,)),
        ],
    )(links, crecv, me, *units)
    arrived = over_blocks(outgoing)

    *parts, norm = call(
        border2_kernel,
        "border2",
        12,
        out_shape=(shape(56, 32, 128),) * 4 + (shape(8, 256, dtype=F32),),
        in_specs=[SMEM] * 3 + [VMEM, HBM, VMEM],
        out_specs=(ANY,) * 4 + (VMEM,),
        scratch_shapes=[
            pltpu.VMEM((FACES + 2 * DEVS + 1, 32, 128), BF16),
            pltpu.VMEM((SLOTS + 2 * DEVS + 8, 128), F32),
            pltpu.VMEM((4, 56, 32, 128), BF16),
            pltpu.SemaphoreType.DMA((4,)),
            pltpu.SemaphoreType.DMA((8,)),
        ],
    )(sel, ssel, me, rows, held, arrived)
    units2 = exchange(parts)
    part2 = call(
        inner2_kernel,
        "inner2",
        24,
        8,
        grid=(QUART,),
        out_shape=shape(QUART, VOX, 256, dtype=F32),
        in_specs=[SMEM, VMEM, HBM, VMEM, VMEM],
        out_specs=cells,
        scratch_shapes=[
            pltpu.VMEM((256, 1792), BF16),
            pltpu.VMEM((VOX, 1792), BF16),
            pltpu.VMEM((QUART, VOX, 256), F32),
            pltpu.SemaphoreType.DMA((QUART,)),
        ],
    )(me, norm, hidden, wa, wb)
    parts = call(
        outer2_kernel,
        "outer2",
        32,
        5,
        grid=(QUART,),
        out_shape=(shape(QUART, 64, VOX),) * 4,
        in_specs=[SMEM, cells] + [slots] * 4 + [VMEM] * 6,
        out_specs=(slots,) * 4,
        scratch_shapes=[
            pltpu.VMEM((4, 56, 32, 128), BF16),
            pltpu.VMEM((6, 256, 256), BF16),
            pltpu.VMEM((6, VOX, 256), F32),
            pltpu.VMEM((2, VOX, 128), F32),
            pltpu.VMEM((256, VOX), F32),
            pltpu.VMEM((VOX, 64), BF16),
        ],
    )(me, part2, *volumes, *units2, wa, wb)
    parts = exchange(parts)
    return call(
        gather_kernel,
        "gather",
        4,
        out_shape=shape(SLOTS, 64, VOX),
        in_specs=[SMEM] + [ANY] * 4,
        out_specs=HBM,
        scratch_shapes=[pltpu.SemaphoreType.DMA((4,))],
    )(me, *parts)


def solution(mesh):
    in_specs = (
        P("blocks", "chan", None),
        P(None, None, "chan", None),
        P(None, "chan"),
        P(None, "chan"),
        P("chan"),
        P("blocks", None),
        P("blocks", None, None),
        P("blocks", None, None),
        P("blocks", None, None),
    )
    out_specs = P("blocks", "chan", None)
    return jax.shard_map(local, mesh=mesh, in_specs=in_specs, out_specs=out_specs, check_vma=False)
```

```python
import functools

import jax
import jax.numpy as jnp
import numpy as np
from jax import lax
from jax.experimental import pallas as pl
from jax.experimental.pallas import tpu as pltpu
from jax.sharding import PartitionSpec as P

GROUP = 8
SIDE = 8
VOX = 512
SLOTS = 32
DEVS = 32
QUART = 8
HALF = 4
TILES = 2
FACES = 6 * SLOTS
CODES = 64
EPS = 1e-05
ORDER = (0, 2, 1, 3)
F32 = jnp.float32
BF16 = jnp.bfloat16
HIGH = lax.Precision.HIGHEST
NT = (((1,), (1,)), ((), ()))
NN = (((1,), (0,)), ((), ()))
VMEM = pl.BlockSpec(memory_space=pltpu.VMEM)
ANY = pl.BlockSpec(memory_space=pl.ANY)
HBM = pl.BlockSpec(memory_space=pltpu.HBM)
SMEM = pl.BlockSpec(memory_space=pltpu.SMEM)
MIB = 1024 * 1024
ROWS = 144


def tables():
    places = np.arange(VOX)
    coords = (places // 64, places // 8 % 8, places % 8)
    extract = np.zeros((7 * 64, VOX), np.float32)
    for face in range(6):
        along = face // 2
        others = [coords[k] for k in range(3) if k != along]
        chosen = coords[along] == (0 if face % 2 == 0 else SIDE - 1)
        extract[face * 64 + (8 * others[0] + others[1])[chosen], places[chosen]] = 1.0
    x, y, z = coords
    extract[384 + x // 2 * 16 + y // 2 * 4 + z // 2, places] = 0.125
    return extract


def lanes(rows):
    return lax.broadcasted_iota(jnp.int32, (rows, 128), 1)


def terms(value):
    high = value.astype(BF16).astype(F32)
    rest = value - high
    middle = rest.astype(BF16).astype(F32)
    return high, middle, rest - middle


def joined(block, row):
    return (block[row + 2 : row + 3] + block[row + 1 : row + 2]) + block[row : row + 1]


def put_terms(ref, row, value):
    for k, part in enumerate(terms(value)):
        ref[row + k : row + k + 1, :] = part


def silu(u):
    half = 0.5 * u
    return half + half * jnp.tanh(half)


def group_matrix(period):
    row = lax.broadcasted_iota(jnp.int32, (128, 128), 0) % period // GROUP
    col = lax.broadcasted_iota(jnp.int32, (128, 128), 1) % period // GROUP
    return (row == col).astype(F32)


def group_sum(row, groups=None):
    wide = jnp.broadcast_to(row, (8, 128))
    groups = group_matrix(64) if groups is None else groups
    return lax.dot_general(wide, groups, NN, precision=HIGH, preferred_element_type=F32)[0:1]


def norm_rows(total, square, entries, gain):
    mean = total * (1.0 / entries)
    spread = square * (1.0 / entries) - mean * mean
    return mean, lax.rsqrt(spread + EPS) * gain


def unpack(parts):
    left = lanes(32) < 64
    low, high = [], []
    for a, b in ((parts[0], parts[1]), (parts[2], parts[3])):
        low.append(jnp.where(left, a, pltpu.roll(b, 64, 1)))
        high.append(jnp.where(left, pltpu.roll(a, 64, 1), b))
    return jnp.concatenate(
        [jnp.concatenate(low, axis=1), jnp.concatenate(high, axis=1)], axis=0
    )


def pack(cells):
    left = lanes(32) < 64
    parts = []
    for half in range(2):
        low = cells[0:32, 128 * half : 128 * half + 128]
        high = cells[32:64, 128 * half : 128 * half + 128]
        parts.append(jnp.where(left, low, pltpu.roll(high, 64, 1)))
        parts.append(jnp.where(left, pltpu.roll(low, 64, 1), high))
    return parts


def spread_row(row):
    left = lanes(1) < 64
    parts = []
    for half in range(2):
        part = row[:, 128 * half : 128 * half + 128]
        turned = pltpu.roll(jnp.broadcast_to(part, (8, 128)), 64, 1)[0:1]
        parts.append(jnp.where(left, part, turned))
        parts.append(jnp.where(left, turned, part))
    return parts


def gather_row(rows):
    left = lanes(1) < 64
    return jnp.concatenate(
        [jnp.where(left, rows[0], rows[1]), jnp.where(left, rows[2], rows[3])], axis=1
    )


def extract_kernel(
    links, csend, feats, table, faces, out,
    slots, codes, held, pooled, stat, send_buf, sem, load,
):
    left = lanes(32) < 64

    def fetch(n):
        here = pl.ds(4 * n, 4)
        return pltpu.make_async_copy(feats.at[here], slots.at[here], load.at[n])

    def keep(n):
        here = pl.ds(12 * n, 12)
        return pltpu.make_async_copy(held.at[here], faces.at[here], sem.at[n])

    get_codes = pltpu.make_async_copy(table, codes, load.at[8])
    fetch(0).start()
    get_codes.start()
    for n in range(1, 8):
        fetch(n).start()
    get_codes.wait()

    def step(n, carry):
        s, q, ps, pq = carry
        fetch(n).wait()
        x = slots[pl.ds(4 * n, 4)]
        layers = lax.dot_general(
            codes[...], x.reshape(256, VOX), NT, preferred_element_type=F32
        )
        wide = x.astype(F32)
        for k in range(4):
            for v in range(4):
                piece = wide[k, :, 128 * v : 128 * v + 128]
                s = s + piece
                q = q + piece * piece
        for j in range(2):
            for f in range(7):
                low = layers[64 * f : 64 * f + 32, 128 * j : 128 * j + 128]
                high = layers[64 * f + 32 : 64 * f + 64, 128 * j : 128 * j + 128]
                pair = (
                    jnp.where(left, low, pltpu.roll(high, 64, 1)),
                    jnp.where(left, pltpu.roll(low, 64, 1), high),
                )
                for k in range(2):
                    unit = pair[k].astype(BF16)
                    slot = 4 * n + 2 * j + k
                    if f < 6:
                        held[slot * 3 + f // 2, 32 * (f % 2) : 32 * (f % 2) + 32] = unit
                    else:
                        pooled[slot] = unit
                        wide = unit.astype(F32)
                        ps = ps + wide
                        pq = pq + wide * wide
        keep(n).start()
        return s, q, ps, pq

    zero = jnp.zeros((64, 128), F32)
    small = jnp.zeros((32, 128), F32)
    s, q, ps, pq = lax.fori_loop(0, 8, step, (zero, zero, small, small), unroll=2)
    ones = jnp.ones((8, 128), F32)
    both = jnp.concatenate([s, q], axis=0)
    rows = lax.dot_general(ones, both, NT, precision=HIGH, preferred_element_type=F32)
    turned = pltpu.roll(rows, 64, 1)
    first = lanes(8) < 64
    stat[...] = jnp.zeros((16, 128), F32)
    put_terms(stat, 0, jnp.where(first, rows, turned)[0:1])
    put_terms(stat, 3, jnp.where(first, turned, rows)[0:1])
    put_terms(stat, 6, jnp.sum(ps, axis=0, keepdims=True))
    put_terms(stat, 9, jnp.sum(pq, axis=0, keepdims=True))
    sums = stat[...].astype(BF16)

    def send(p, _):
        for k in range(2):
            code = jnp.minimum(links[k, p], FACES - 1)
            at = pl.multiple_of(32 * (code & 1), 32)
            send_buf[p, 32 * k : 32 * k + 32] = held[code >> 1, pl.ds(at, 32)]
            send_buf[p, 64 + 32 * k : 96 + 32 * k] = pooled[jnp.minimum(csend[k, p], SLOTS - 1)]
        send_buf[p, 128:144] = sums
        return 0

    lax.fori_loop(0, DEVS, send, 0, unroll=8)
    give = pltpu.make_async_copy(send_buf, out, sem.at[8])
    give.start()
    for n in range(8):
        keep(n).wait()
    give.wait()


def plan_kernel(nbr, links, csend, crecv, sel, tsel, ssel):
    def slot_of(n, _):
        for f in range(6):
            near = nbr[f, n]
            sel[n * 6 + f] = jnp.where(near < SLOTS, near * 6 + (f ^ 1), FACES + 2 * DEVS)
        return 0

    lax.fori_loop(0, SLOTS, slot_of, 0)

    def empty(i, _):
        tsel[i] = 2 * DEVS
        return 0

    lax.fori_loop(0, CODES, empty, 0)

    def mark(p, _):
        for k in range(2):
            code = links[k, p]

            @pl.when(code < FACES)
            def _():
                sel[code] = FACES + 2 * p + k

            place = crecv[k, p]

            @pl.when(place < CODES)
            def _():
                tsel[place] = 2 * p + k

            slot = csend[k, p]

            @pl.when(slot < SLOTS)
            def _():
                ssel[slot] = 2 * p + k

        return 0

    lax.fori_loop(0, DEVS, mark, 0)


def border1_kernel(
    sel, tsel, me, par, faces, recv, x1, x2, x3,
    p0, p1, p2, p3, o0, o1, o2, o3,
    told_in, rough_in, src, first, buf, stat, psem, sem, load,
):
    y = me[0]
    fetches = [
        pltpu.make_async_copy(recv.at[:, pl.ds(128, 16)], told_in, load.at[0]),
        pltpu.make_async_copy(recv.at[:, pl.ds(64, 64)], rough_in, load.at[1]),
        pltpu.make_async_copy(recv.at[:, pl.ds(0, 64)], src.at[pl.ds(96, DEVS)], load.at[2]),
        pltpu.make_async_copy(faces, src.at[pl.ds(0, 96)], load.at[3]),
    ]
    for fetch in fetches:
        fetch.start()
    src[96 + DEVS] = jnp.zeros((64, 128), BF16)
    fetches[0].wait()

    def add(s, total):
        return total + told_in[s].astype(F32)

    sums = lax.fori_loop(0, DEVS, add, jnp.zeros((16, 128), F32), unroll=8)
    fine = float(DEVS * SLOTS * VOX * GROUP)
    rough = float(DEVS * SLOTS * 64 * GROUP)
    groups = group_matrix(64)
    mean1, scale1 = norm_rows(
        group_sum(joined(sums, 0), groups) * 0.5,
        group_sum(joined(sums, 3), groups) * 0.5,
        fine,
        par[0:1],
    )
    mean3, scale3 = norm_rows(
        group_sum(joined(sums, 6), groups), group_sum(joined(sums, 9), groups), rough, par[2:3]
    )
    bias1, bias3 = par[1:2], par[3:4]
    stat[...] = jnp.zeros((32, 128), F32)
    for k, row in enumerate((mean1, scale1, bias1, par[4:5], par[5:6], par[6:7])):
        put_terms(stat, 3 * k, row)
    told = stat[...].astype(BF16)
    fetches[1].wait()
    copies = []
    for r, p in enumerate((p0, p1, p2, p3)):
        q = (y + r) & 3
        first[r, 16] = told

        def octant(i, _):
            for k in range(8):
                far = tsel[q * 16 + i * 8 + k]
                link = jnp.minimum(far, 2 * DEVS - 1)
                at = pl.multiple_of(32 * (link & 1), 32)
                u = rough_in[link >> 1, pl.ds(at, 32)].astype(F32)
                v = silu((u - mean3) * scale3 + bias3)
                first[r, i * 8 + k] = (v * (far < 2 * DEVS).astype(F32)).astype(BF16)
            return 0

        lax.fori_loop(0, 2, octant, 0)
        copies.append(pltpu.make_async_copy(first.at[r], p, psem.at[r]))
        copies[-1].start()
    for fetch in fetches[2:]:
        fetch.wait()
    for r, o in enumerate((o0, o1, o2, o3)):
        q = (y + r) & 3

        def face(i, _):
            for f in range(6):
                at = sel[q * 48 + i * 6 + f]
                u = src[at >> 1, pl.ds(pl.multiple_of(32 * (at & 1), 32), 32)].astype(F32)
                v = silu((u - mean1) * scale1 + bias1)
                buf[r, i * 6 + f] = (v * (at < FACES + 2 * DEVS).astype(F32)).astype(BF16)
            return 0

        lax.fori_loop(0, QUART, face, 0)
        copies.append(pltpu.make_async_copy(buf.at[r], o, sem.at[r]))
        copies[-1].start()
    for copy in copies:
        copy.wait()


def interior_taps(act, taps):
    wide = act.astype(F32)
    cube = wide.reshape(8, 8, 8, 256)
    none = jnp.zeros((64, 256), BF16)
    wall = jnp.zeros((8, 1, 8, 256), F32)
    taps[:, 0:256] = act
    taps[0:64, 256:512] = none
    taps[64:512, 256:512] = act[0:448]
    taps[0:448, 512:768] = act[64:512]
    taps[448:512, 512:768] = none
    low = jnp.concatenate([wall, cube[:, 0:7]], axis=1)
    taps[:, 768:1024] = low.reshape(512, 256).astype(BF16)
    high = jnp.concatenate([cube[:, 1:8], wall], axis=1)
    taps[:, 1024:1280] = high.reshape(512, 256).astype(BF16)
    depth = lax.broadcasted_iota(jnp.int32, (512, 256), 0) % 8
    low = jnp.where(depth == 0, 0.0, pltpu.roll(wide, 1, 0))
    taps[:, 1280:1536] = low.astype(BF16)
    high = jnp.where(depth == 7, 0.0, pltpu.roll(wide, 511, 0))
    taps[:, 1536:1792] = high.astype(BF16)


def fill_weights(dst, first, second, core, which):
    for c in range(4):
        for side, part in enumerate((first, second)):
            at = pl.multiple_of(64 * c + 32 * (core ^ side), 32)
            for t in range(7):
                dst[pl.ds(at, 32), 256 * t : 256 * t + 256] = part[c, which, t]


def fill_tap_weights(dst, first, second, core, which):
    for c in range(4):
        for side, part in enumerate((first, second)):
            at = pl.multiple_of(64 * c + 32 * (core ^ side), 32)
            for f in range(6):
                dst[f, pl.ds(at, 32), :] = part[c, which, 1 + f]


def fill_cube(cube, volumes, y):
    for r, v in zip(ORDER, volumes):
        at = pl.multiple_of(((y - r) & 3) * 64, 64)
        cube[pl.ds(at, 64), :] = v[0].astype(F32)


def place_rows(rows, told, y, stat):
    rows[...] = jnp.zeros((8, 256), F32)
    for r, t in zip(ORDER, told):
        stat[(y - r) & 3] = t[0].astype(F32)
    for k in range(6):
        rows[k : k + 1, :] = gather_row([joined(stat[c], 3 * k) for c in range(4)])


def inner1_kernel(
    me, t0, t1, t2, t3, v0, v1, v2, v3, wa, wb, part, rows, weights, stat, taps, cube
):
    y = me[0]

    @pl.when(pl.program_id(0) == 0)
    def _():
        place_rows(rows, (t0, t1, t2, t3), y, stat)
        fill_weights(weights, wa, wb, me[1], 0)

    fill_cube(cube, (v0, v1, v2, v3), y)
    x = cube[...].T
    act = silu((x - rows[0:1]) * rows[1:2] + rows[2:3]).astype(BF16)
    interior_taps(act, taps)
    part[0] = lax.dot_general(taps[...], weights[...], NT, preferred_element_type=F32)


def inner2_kernel(me, rows, hid, wa, wb, part, weights, taps, cells, sem):
    step = pl.program_id(0)

    def fetch_cells(n):
        return pltpu.make_async_copy(hid.at[n], cells.at[n], sem.at[n])

    @pl.when(step == 0)
    def _():
        for n in range(QUART):
            fetch_cells(n).start()
        fill_weights(weights, wa, wb, me[1], 1)

    fetch_cells(step).wait()
    act = silu((cells[step] - rows[0:1]) * rows[1:2] + rows[2:3]).astype(BF16)
    interior_taps(act, taps)
    part[0] = lax.dot_general(taps[...], weights[...], NT, preferred_element_type=F32)


def border_terms(units, tap_weights, parts, y, across, start, count):
    for r, u in zip(ORDER, parts):
        units[(y - r) & 3] = u[...]
    for f in range(6):
        layer = jnp.concatenate(
            [
                unpack([units[c, 6 * n + f].astype(F32) for c in range(4)]).astype(BF16)
                for n in range(start, start + count)
            ],
            axis=0,
        )
        across[f] = lax.dot_general(layer, tap_weights[f], NT, preferred_element_type=F32)


def add_borders(h, across, step, shift):
    at = pl.multiple_of(step * 64, 64)
    h = jnp.concatenate(
        [h[0:64] + across[0, pl.ds(at, 64), :], h[64:448], h[448:512] + across[1, pl.ds(at, 64), :]],
        axis=0,
    )
    deep = h.reshape(8, 8, 8, 256)
    low = across[2, pl.ds(at, 64), :].reshape(8, 1, 8, 256)
    high = across[3, pl.ds(at, 64), :].reshape(8, 1, 8, 256)
    h = jnp.concatenate([deep[:, 0:1] + low, deep[:, 1:7], deep[:, 7:8] + high], axis=1)
    h = h.reshape(512, 256)
    halves, edges = [], [[], []]
    for half in range(2):
        cut = slice(128 * half, 128 * half + 128)
        shift[half] = h[:, cut]
        for side in range(2):
            layer = shift[half, pl.ds(7 * side, 64, stride=8), :]
            layer = layer + across[4 + side, pl.ds(at, 64), cut]
            shift[half, pl.ds(7 * side, 64, stride=8), :] = layer
            edges[side].append(layer)
        halves.append(shift[half])
    h = jnp.concatenate(halves, axis=1)
    return h, [jnp.concatenate(pair, axis=1) for pair in edges]


def outer1_kernel(
    me, rows, part, u0, u1, u2, u3, tiles, wa, wb,
    hid, o0, o1, o2, o3,
    units, outs, weights, across, shift, stat, cells, sem,
):
    y = me[0]
    fill_tap_weights(weights, wa, wb, me[1], 0)
    border_terms(units, weights, (u0, u1, u2, u3), y, across, 0, QUART)
    stat[...] = jnp.zeros((4, 32, 128), F32)

    def keep_cells(n):
        return pltpu.make_async_copy(cells.at[n], hid.at[n], sem.at[n])

    def slot(n, carry):
        all_total, all_square = carry
        h, edges = add_borders(part[n] + rows[3:4], across, n, shift)
        cells[n] = h
        keep_cells(n).start()
        total = jnp.sum(h, axis=0, keepdims=True)
        square = jnp.sum(h * h, axis=0, keepdims=True)
        centre = (total * (1.0 / VOX)).astype(BF16).astype(F32)
        for c, row in enumerate(spread_row(centre)):
            stat[c, pl.ds(n, 1), :] = row
        deep = h.reshape(8, 8, 8, 256)
        for f in range(6):
            if f < 2:
                layer = h[448 * f : 448 * f + 64]
            elif f < 4:
                layer = deep[:, 7 * (f - 2)].reshape(64, 256)
            else:
                layer = edges[f - 4]
            for c, unit in enumerate(pack(layer - centre)):
                outs[c, n * 6 + f] = unit.astype(BF16)
        return all_total + total, all_square + square

    nothing = jnp.zeros((1, 256), F32)
    sums = lax.fori_loop(0, QUART, slot, (nothing, nothing))
    at = 8
    for k in range(2):
        for half in range(2):
            for row in terms(sums[k][:, 128 * half : 128 * half + 128]):
                for c in range(4):
                    stat[c, at : at + 1, :] = row
                at += 1
    for c in range(4):
        outs[c, 48] = stat[c].astype(BF16)
    for r, o in enumerate((o0, o1, o2, o3)):
        o[0:49] = outs[(y + r) & 3]
        o[49:65] = tiles[(y + r) & 3]
    for n in range(QUART):
        keep_cells(n).wait()


def placement(rows, columns, code):
    row = lax.broadcasted_iota(jnp.int32, (rows, columns), 0)
    column = lax.broadcasted_iota(jnp.int32, (rows, columns), 1)
    return (code(row) == column).astype(F32).astype(BF16)


def octant_code(v):
    x, y, z = v >> 6, (v >> 3) & 7, v & 7
    octant = (x >> 2) * 4 + (y >> 2) * 2 + (z >> 2)
    return octant * 64 + (x & 3) * 16 + (y & 3) * 4 + (z & 3)


def voxel_code(w):
    octant, x, y, z = w >> 6, (w >> 4) & 3, (w >> 2) & 3, w & 3
    x, y, z = x + 4 * (octant >> 2), y + 4 * ((octant >> 1) & 1), z + 4 * (octant & 1)
    return x * 64 + y * 8 + z


def coarse_code(v):
    return ((v >> 7) & 3) * 16 + ((v >> 4) & 3) * 4 + ((v >> 1) & 3)


def tile_kernel(me, u0, u1, u2, u3, wa, wb, out, units, weights, taps, place, place_t):
    t = pl.program_id(0)
    y = me[0]

    @pl.when(t == 0)
    def _():
        place[...] = placement(VOX, VOX, octant_code)
        place_t[...] = placement(VOX, VOX, voxel_code)
        fill_weights(weights, wa, wb, me[1], 2)

    for r, u in zip(ORDER, (u0, u1, u2, u3)):
        units[(y - r) & 3] = u[...]
    octants = jnp.concatenate(
        [unpack([units[c, o].astype(F32) for c in range(4)]).astype(BF16) for o in range(8)], axis=0
    )
    act = lax.dot_general(place[...], octants, NN, preferred_element_type=F32).astype(BF16)
    interior_taps(act, taps)
    h = lax.dot_general(taps[...], weights[...], NT, preferred_element_type=F32).astype(BF16)
    pieces = lax.dot_general(place_t[...], h, NN, preferred_element_type=F32)
    for o in range(8):
        for c, unit in enumerate(pack(pieces[64 * o : 64 * o + 64])):
            out[c, o] = unit.astype(BF16)


def route2_kernel(
    links, crecv, me, v0, v1, v2, v3, keep, out, held, cen, stat, send_buf, sem
):
    y = me[0]
    for r, v in zip(ORDER, (v0, v1, v2, v3)):
        held[(y - r) & 3] = v[...]
    kept = pltpu.make_async_copy(held, keep, sem.at[0])
    kept.start()
    total = jnp.zeros((32, 128), F32)
    for q in range(4):
        told = held[q, 48].astype(F32)
        cen[8 * q : 8 * q + 8, :] = told[0:8]
        total = total + told
    stat[...] = jnp.zeros((16, 128), F32)
    for k in range(4):
        put_terms(stat, 2 + 3 * k, joined(total, 8 + 3 * k))

    def send(p, _):
        for k in range(2):
            code = jnp.minimum(links[k, p], FACES - 1)
            slot = lax.div(code, 6)
            q = slot >> 3
            send_buf[p, 32 * k : 32 * k + 32] = held[q, code - 48 * q]
            stat[k : k + 1, :] = cen[pl.ds(slot, 1), :]
            place = jnp.minimum(crecv[k, p], CODES - 1)
            send_buf[p, 64 + 32 * k : 96 + 32 * k] = held[place >> 4, 49 + (place & 15)]
        send_buf[p, 128:144] = stat[...].astype(BF16)
        return 0

    lax.fori_loop(0, DEVS, send, 0, unroll=4)
    give = pltpu.make_async_copy(send_buf, out, sem.at[1])
    give.start()
    kept.wait()
    give.wait()


def own_row(row, y):
    wide = jnp.broadcast_to(jnp.where(y >= 2, row[:, 128:256], row[:, 0:128]), (8, 128))
    turned = pltpu.roll(wide, 64, 1)
    left = lanes(8) < 64
    odd = (y & 1) == 1
    return jnp.where(left, jnp.where(odd, turned, wide), jnp.where(odd, wide, turned))[0:1]


def border2_kernel(
    sel, ssel, me, rows, held, recv, o0, o1, o2, o3, norm, src, cen, buf, sem, load
):
    y = me[0]
    fetches = []
    for q in range(4):
        fetches.append(
            pltpu.make_async_copy(held.at[q, pl.ds(0, 48)], src.at[pl.ds(48 * q, 48)], load.at[q])
        )
        fetches.append(pltpu.make_async_copy(held.at[q, 48], buf.at[q, 0], load.at[4 + q]))
    for fetch in fetches:
        fetch.start()

    def add(s, total):
        src[FACES + 2 * s] = recv[s, 0:32]
        src[FACES + 2 * s + 1] = recv[s, 32:64]
        told = recv[s, 128:144].astype(F32)
        cen[pl.ds(SLOTS + 2 * s, 2), :] = told[0:2]
        return total + told

    sums = lax.fori_loop(0, DEVS, add, jnp.zeros((16, 128), F32), unroll=8)
    src[FACES + 2 * DEVS] = jnp.zeros((32, 128), BF16)
    cen[pl.ds(SLOTS + 2 * DEVS, 8), :] = jnp.zeros((8, 128), F32)
    fine = float(DEVS * SLOTS * VOX * GROUP)
    groups = group_matrix(128)
    norm[...] = jnp.zeros((8, 256), F32)
    for half in range(2):
        cut = slice(128 * half, 128 * half + 128)
        mean, scale = norm_rows(
            group_sum(joined(sums, 2 + 3 * half), groups),
            group_sum(joined(sums, 8 + 3 * half), groups),
            fine,
            rows[4:5, cut],
        )
        norm[0:1, cut] = mean
        norm[1:2, cut] = scale
        norm[2:3, cut] = rows[5:6, cut]
    mean, scale, bias = (own_row(norm[k : k + 1, :], y) for k in range(3))
    for fetch in fetches:
        fetch.wait()
    for q in range(4):
        cen[8 * q : 8 * q + 8, :] = buf[q, 0].astype(F32)[0:8]
    copies = []
    for r, o in enumerate((o0, o1, o2, o3)):
        q = (y + r) & 3

        def face(i, _):
            for f in range(6):
                at = sel[q * 48 + i * 6 + f]
                owner = jnp.where(at < FACES, lax.div(at, 6), at - (FACES - SLOTS))
                u = src[at].astype(F32) + (cen[pl.ds(owner, 1), :] - mean)
                v = silu(u * scale + bias)
                buf[r, i * 6 + f] = (v * (at < FACES + 2 * DEVS).astype(F32)).astype(BF16)
            link = ssel[q * 8 + i]
            at = pl.multiple_of(64 + 32 * (link & 1), 32)
            buf[r, 48 + i] = recv[link >> 1, pl.ds(at, 32)]
            return 0

        lax.fori_loop(0, QUART, face, 0)
        copies.append(pltpu.make_async_copy(buf.at[r], o, sem.at[r]))
        copies[-1].start()
    for copy in copies:
        copy.wait()


def outer2_kernel(
    me, part, v0, v1, v2, v3, u0, u1, u2, u3, wa, wb,
    o0, o1, o2, o3,
    units, weights, across, shift, cube, lift,
    *, start,
):
    y = me[0]
    lift[...] = placement(VOX, 64, coarse_code)
    fill_tap_weights(weights, wa, wb, me[1], 1)
    border_terms(units, weights, (u0, u1, u2, u3), y, across, start, HALF)

    def slot(n, _):
        m = start + n
        raised = unpack([units[c, 48 + m].astype(F32) for c in range(4)]).astype(BF16)
        lifted = lax.dot_general(lift[...], raised, NN, preferred_element_type=F32)
        h, _ = add_borders(part[m] + lifted, across, n, shift)
        for r, v in zip(ORDER, (v0, v1, v2, v3)):
            at = pl.multiple_of(((y - r) & 3) * 64, 64)
            cube[pl.ds(at, 64), :] = v[QUART * y + m if r == 0 else m].astype(F32)
        cube[...] += h.T
        for r, o in enumerate((o0, o1, o2, o3)):
            at = pl.multiple_of(((y + r) & 3) * 64, 64)
            o[n] = cube[pl.ds(at, 64), :].astype(BF16)
        return 0

    lax.fori_loop(0, HALF, slot, 0)


def gather_kernel(me, *refs):
    *parts, out, sem = refs
    y = me[0]
    copies = []
    for k, p in enumerate(parts):
        at = ((y - ORDER[k % 4]) & 3) * QUART + HALF * (k // 4)
        copies.append(pltpu.make_async_copy(p, out.at[pl.ds(at, HALF)], sem.at[k]))
        copies[-1].start()
    for copy in copies:
        copy.wait()


def shape(*dims, dtype=BF16):
    return jax.ShapeDtypeStruct(dims, dtype)


def call(kernel, name, mib, micros=1, **more):
    return pl.pallas_call(
        kernel,
        cost_estimate=pl.CostEstimate(
            flops=micros * 10**9, bytes_accessed=micros * 3 * 10**6, transcendentals=0
        ),
        compiler_params=pltpu.CompilerParams(vmem_limit_bytes=mib * MIB),
        name=name,
        **more,
    )


def exchange(parts, order=(0, 1, 2, 3)):
    got = {
        r: lax.ppermute(parts[r], "chan", [(i, (i + r) % 4) for i in order]) for r in ORDER[1:]
    }
    return [parts[0]] + [got[r] for r in ORDER[1:]]


def over_blocks(units):
    return lax.all_to_all(units, "blocks", split_axis=0, concat_axis=0, tiled=True)


def local(
    feats,
    conv_weights,
    norm_gain,
    norm_bias,
    time_bias,
    local_nbr,
    face_links,
    coarse_send,
    coarse_recv,
):
    extract_np = tables()
    y = lax.axis_index("chan").astype(jnp.int32)
    core = (lax.axis_index("blocks") % 2).astype(jnp.int32)
    me = jnp.stack([y, core])
    nbr = local_nbr.T
    links = face_links[0].T
    csend = coarse_send[0].T
    crecv = coarse_recv[0].T

    def twice(rows):
        block = jnp.stack(rows)
        block = jnp.concatenate([block, block], axis=1)
        return jnp.pad(block, ((0, 8 - block.shape[0]), (0, 0)))

    par = twice(
        [norm_gain[0], norm_bias[0], norm_gain[2], norm_bias[2], time_bias]
        + [norm_gain[1], norm_bias[1]]
    )
    faces, outgoing = call(
        extract_kernel,
        "extract",
        60,
        out_shape=(shape(FACES // 2, 64, 128), shape(DEVS, ROWS, 128)),
        in_specs=[SMEM] * 2 + [HBM] * 2,
        out_specs=(HBM,) * 2,
        scratch_shapes=[
            pltpu.VMEM((SLOTS, 64, VOX), BF16),
            pltpu.VMEM((448, VOX), BF16),
            pltpu.VMEM((FACES // 2, 64, 128), BF16),
            pltpu.VMEM((SLOTS, 32, 128), BF16),
            pltpu.VMEM((16, 128), F32),
            pltpu.VMEM((DEVS, ROWS, 128), BF16),
            pltpu.SemaphoreType.DMA((9,)),
            pltpu.SemaphoreType.DMA((9,)),
        ],
    )(links, csend, feats, jnp.asarray(extract_np, BF16))
    arrived = over_blocks(outgoing)
    half = lax.dynamic_slice_in_dim(conv_weights, 32 * core, 32, axis=2)
    wa = lax.all_gather(half, "chan", axis=0, tiled=False)
    volumes = exchange(
        [feats]
        + [
            lax.dynamic_slice_in_dim(feats, QUART * ((y + r) % 4), QUART, axis=0)
            for r in range(1, 4)
        ]
    )
    sel, tsel, ssel = call(
        plan_kernel,
        "plan",
        4,
        20,
        out_shape=(
            shape(FACES, dtype=jnp.int32),
            shape(CODES, dtype=jnp.int32),
            shape(SLOTS, dtype=jnp.int32),
        ),
        in_specs=[SMEM] * 4,
        out_specs=(SMEM,) * 3,
    )(nbr, links, csend, crecv)

    parts = call(
        border1_kernel,
        "border1",
        60,
        out_shape=(shape(17, 32, 128),) * 4 + (shape(48, 32, 128),) * 4,
        in_specs=[SMEM] * 3 + [VMEM] + [HBM] * 5,
        out_specs=(HBM,) * 8,
        scratch_shapes=[
            pltpu.VMEM((DEVS, 16, 128), BF16),
            pltpu.VMEM((DEVS, 64, 128), BF16),
            pltpu.VMEM((FACES // 2 + DEVS + 1, 64, 128), BF16),
            pltpu.VMEM((4, 17, 32, 128), BF16),
            pltpu.VMEM((4, 48, 32, 128), BF16),
            pltpu.VMEM((32, 128), F32),
            pltpu.SemaphoreType.DMA((4,)),
            pltpu.SemaphoreType.DMA((4,)),
            pltpu.SemaphoreType.DMA((4,)),
        ],
    )(sel, tsel, me, par, faces, arrived, *volumes[1:])
    tiles1 = exchange(parts[:4], (3, 2, 1, 0))
    units1 = exchange(parts[4:])
    wa, _ = lax.optimization_barrier((wa, parts[0]))
    wb = lax.ppermute(wa, "blocks", [(i, i ^ 1) for i in range(DEVS)])

    cells = pl.BlockSpec((1, VOX, 256), lambda i: (i, 0, 0))

    def prefetched(count, in_specs, out_specs, scratch_shapes):
        return pltpu.PrefetchScalarGridSpec(
            num_scalar_prefetch=1,
            grid=(count,),
            in_specs=in_specs,
            out_specs=out_specs,
            scratch_shapes=scratch_shapes,
        )

    def slot_specs(start):
        first = pl.BlockSpec((1, 64, VOX), lambda i, me: (QUART * me[0] + start + i, 0, 0))
        return [first] + [pl.BlockSpec((1, 64, VOX), lambda i, me: (start + i, 0, 0))] * 3

    def cell_spec(start):
        return pl.BlockSpec((1, VOX, 256), lambda i, me: (start + i, 0, 0))

    last = pl.BlockSpec((1, 32, 128), lambda i, me: (16, 0, 0))
    part1, rows = call(
        inner1_kernel,
        "inner1",
        24,
        8,
        grid_spec=prefetched(
            QUART,
            [last] * 4 + slot_specs(0) + [VMEM] * 2,
            (cell_spec(0), VMEM),
            [
                pltpu.VMEM((256, 1792), BF16),
                pltpu.VMEM((4, 32, 128), F32),
                pltpu.VMEM((VOX, 1792), BF16),
                pltpu.VMEM((256, VOX), F32),
            ],
        ),
        out_shape=(shape(QUART, VOX, 256, dtype=F32), shape(8, 256, dtype=F32)),
    )(me, *tiles1, *volumes, wa, wb)
    eight = pl.BlockSpec((8, 32, 128), lambda t: (t, 0, 0))
    coarse = call(
        tile_kernel,
        "tiles",
        24,
        4,
        grid=(TILES,),
        out_shape=shape(4, 16, 32, 128),
        in_specs=[SMEM] + [eight] * 4 + [VMEM] * 2,
        out_specs=pl.BlockSpec((4, 8, 32, 128), lambda t: (0, t, 0, 0)),
        scratch_shapes=[
            pltpu.VMEM((4, 8, 32, 128), BF16),
            pltpu.VMEM((256, 1792), BF16),
            pltpu.VMEM((VOX, 1792), BF16),
            pltpu.VMEM((VOX, VOX), BF16),
            pltpu.VMEM((VOX, VOX), BF16),
        ],
    )(me, *tiles1, wa, wb)
    hidden, *parts = call(
        outer1_kernel,
        "outer1",
        32,
        5,
        out_shape=(shape(QUART, VOX, 256, dtype=F32),) + (shape(65, 32, 128),) * 4,
        in_specs=[SMEM] + [VMEM] * 9,
        out_specs=(HBM,) + (VMEM,) * 4,
        scratch_shapes=[
            pltpu.VMEM((4, 48, 32, 128), BF16),
            pltpu.VMEM((4, 49, 32, 128), BF16),
            pltpu.VMEM((6, 256, 256), BF16),
            pltpu.VMEM((6, VOX, 256), F32),
            pltpu.VMEM((2, VOX, 128), F32),
            pltpu.VMEM((4, 32, 128), F32),
            pltpu.VMEM((QUART, VOX, 256), F32),
            pltpu.SemaphoreType.DMA((QUART,)),
        ],
    )(me, rows, part1, *units1, coarse, wa, wb)
    units = exchange(parts)

    held, outgoing = call(
        route2_kernel,
        "route2",
        12,
        out_shape=(shape(4, 65, 32, 128), shape(DEVS, ROWS, 128)),
        in_specs=[SMEM] * 3 + [VMEM] * 4,
        out_specs=(HBM, HBM),
        scratch_shapes=[
            pltpu.VMEM((4, 65, 32, 128), BF16),
            pltpu.VMEM((SLOTS, 128), F32),
            pltpu.VMEM((16, 128), F32),
            pltpu.VMEM((DEVS, ROWS, 128), BF16),
            pltpu.SemaphoreType.DMA((2,)),
        ],
    )(links, crecv, me, *units)
    arrived = over_blocks(outgoing)

    *parts, norm = call(
        border2_kernel,
        "border2",
        12,
        out_shape=(shape(56, 32, 128),) * 4 + (shape(8, 256, dtype=F32),),
        in_specs=[SMEM] * 3 + [VMEM, HBM, VMEM],
        out_specs=(ANY,) * 4 + (VMEM,),
        scratch_shapes=[
            pltpu.VMEM((FACES + 2 * DEVS + 1, 32, 128), BF16),
            pltpu.VMEM((SLOTS + 2 * DEVS + 8, 128), F32),
            pltpu.VMEM((4, 56, 32, 128), BF16),
            pltpu.SemaphoreType.DMA((4,)),
            pltpu.SemaphoreType.DMA((8,)),
        ],
    )(sel, ssel, me, rows, held, arrived)
    units2 = exchange(parts)
    part2 = call(
        inner2_kernel,
        "inner2",
        24,
        8,
        grid=(QUART,),
        out_shape=shape(QUART, VOX, 256, dtype=F32),
        in_specs=[SMEM, VMEM, HBM, VMEM, VMEM],
        out_specs=cells,
        scratch_shapes=[
            pltpu.VMEM((256, 1792), BF16),
            pltpu.VMEM((VOX, 1792), BF16),
            pltpu.VMEM((QUART, VOX, 256), F32),
            pltpu.SemaphoreType.DMA((QUART,)),
        ],
    )(me, norm, hidden, wa, wb)
    pieces = []
    for start in (0, HALF):
        parts = call(
            functools.partial(outer2_kernel, start=start),
            "outer2",
            32,
            5,
            in_specs=[SMEM] + [VMEM] * 11,
            out_specs=(VMEM,) * 4,
            scratch_shapes=[
                pltpu.VMEM((4, 56, 32, 128), BF16),
                pltpu.VMEM((6, 256, 256), BF16),
                pltpu.VMEM((6, 64 * HALF, 256), F32),
                pltpu.VMEM((2, VOX, 128), F32),
                pltpu.VMEM((256, VOX), F32),
                pltpu.VMEM((VOX, 64), BF16),
            ],
            out_shape=(shape(HALF, 64, VOX),) * 4,
        )(me, part2, *volumes, *units2, wa, wb)
        pieces += exchange(parts, (0, 1, 2, 3) if start == 0 else (3, 2, 1, 0))
    return call(
        gather_kernel,
        "gather",
        4,
        out_shape=shape(SLOTS, 64, VOX),
        in_specs=[SMEM] + [ANY] * 8,
        out_specs=HBM,
        scratch_shapes=[pltpu.SemaphoreType.DMA((8,))],
    )(me, *pieces)


def solution(mesh):
    in_specs = (
        P("blocks", "chan", None),
        P(None, None, "chan", None),
        P(None, "chan"),
        P(None, "chan"),
        P("chan"),
        P("blocks", None),
        P("blocks", None, None),
        P("blocks", None, None),
        P("blocks", None, None),
    )
    out_specs = P("blocks", "chan", None)
    return jax.shard_map(local, mesh=mesh, in_specs=in_specs, out_specs=out_specs, check_vma=False)
```

```python
import functools

import jax
import jax.numpy as jnp
import numpy as np
from jax import lax
from jax.experimental import pallas as pl
from jax.experimental.pallas import tpu as pltpu
from jax.sharding import PartitionSpec as P

GROUP = 8
SIDE = 8
VOX = 512
SLOTS = 32
DEVS = 32
QUART = 8
HALF = 4
TILES = 2
FACES = 6 * SLOTS
CODES = 64
EPS = 1e-05
ORDER = (0, 2, 1, 3)
F32 = jnp.float32
BF16 = jnp.bfloat16
HIGH = lax.Precision.HIGHEST
NT = (((1,), (1,)), ((), ()))
NN = (((1,), (0,)), ((), ()))
VMEM = pl.BlockSpec(memory_space=pltpu.VMEM)
ANY = pl.BlockSpec(memory_space=pl.ANY)
HBM = pl.BlockSpec(memory_space=pltpu.HBM)
SMEM = pl.BlockSpec(memory_space=pltpu.SMEM)
MIB = 1024 * 1024
ROWS = 144


def tables():
    places = np.arange(VOX)
    coords = (places // 64, places // 8 % 8, places % 8)
    extract = np.zeros((7 * 64, VOX), np.float32)
    for face in range(6):
        along = face // 2
        others = [coords[k] for k in range(3) if k != along]
        chosen = coords[along] == (0 if face % 2 == 0 else SIDE - 1)
        extract[face * 64 + (8 * others[0] + others[1])[chosen], places[chosen]] = 1.0
    x, y, z = coords
    extract[384 + x // 2 * 16 + y // 2 * 4 + z // 2, places] = 0.125
    return extract


def lanes(rows):
    return lax.broadcasted_iota(jnp.int32, (rows, 128), 1)


def terms(value):
    high = value.astype(BF16).astype(F32)
    rest = value - high
    middle = rest.astype(BF16).astype(F32)
    return high, middle, rest - middle


def joined(block, row):
    return (block[row + 2 : row + 3] + block[row + 1 : row + 2]) + block[row : row + 1]


def put_terms(ref, row, value):
    for k, part in enumerate(terms(value)):
        ref[row + k : row + k + 1, :] = part


def silu(u):
    half = 0.5 * u
    return half + half * jnp.tanh(half)


def group_matrix(period):
    row = lax.broadcasted_iota(jnp.int32, (128, 128), 0) % period // GROUP
    col = lax.broadcasted_iota(jnp.int32, (128, 128), 1) % period // GROUP
    return (row == col).astype(F32)


def group_sum(row, groups=None):
    wide = jnp.broadcast_to(row, (8, 128))
    groups = group_matrix(64) if groups is None else groups
    return lax.dot_general(wide, groups, NN, precision=HIGH, preferred_element_type=F32)[0:1]


def norm_rows(total, square, entries, gain):
    mean = total * (1.0 / entries)
    spread = square * (1.0 / entries) - mean * mean
    return mean, lax.rsqrt(spread + EPS) * gain


def unpack(parts):
    left = lanes(32) < 64
    low, high = [], []
    for a, b in ((parts[0], parts[1]), (parts[2], parts[3])):
        low.append(jnp.where(left, a, pltpu.roll(b, 64, 1)))
        high.append(jnp.where(left, pltpu.roll(a, 64, 1), b))
    return jnp.concatenate(
        [jnp.concatenate(low, axis=1), jnp.concatenate(high, axis=1)], axis=0
    )


def pack(cells):
    left = lanes(32) < 64
    parts = []
    for half in range(2):
        low = cells[0:32, 128 * half : 128 * half + 128]
        high = cells[32:64, 128 * half : 128 * half + 128]
        parts.append(jnp.where(left, low, pltpu.roll(high, 64, 1)))
        parts.append(jnp.where(left, pltpu.roll(low, 64, 1), high))
    return parts


def spread_row(row):
    left = lanes(1) < 64
    parts = []
    for half in range(2):
        part = row[:, 128 * half : 128 * half + 128]
        turned = pltpu.roll(jnp.broadcast_to(part, (8, 128)), 64, 1)[0:1]
        parts.append(jnp.where(left, part, turned))
        parts.append(jnp.where(left, turned, part))
    return parts


def gather_row(rows):
    left = lanes(1) < 64
    return jnp.concatenate(
        [jnp.where(left, rows[0], rows[1]), jnp.where(left, rows[2], rows[3])], axis=1
    )


def extract_kernel(
    links, csend, me, feats, table, kernels, faces, out, half,
    slots, codes, held, pooled, stat, send_buf, cut, sem, load,
):
    left = lanes(32) < 64
    at = pl.multiple_of(32 * me[1], 32)
    cut_in = pltpu.make_async_copy(kernels.at[:, :, pl.ds(at, 32)], cut, load.at[9])
    cut_out = pltpu.make_async_copy(cut, half, sem.at[9])

    def fetch(n):
        here = pl.ds(4 * n, 4)
        return pltpu.make_async_copy(feats.at[here], slots.at[here], load.at[n])

    def keep(n):
        here = pl.ds(12 * n, 12)
        return pltpu.make_async_copy(held.at[here], faces.at[here], sem.at[n])

    get_codes = pltpu.make_async_copy(table, codes, load.at[8])
    fetch(0).start()
    get_codes.start()
    for n in range(1, 8):
        fetch(n).start()
    cut_in.start()
    get_codes.wait()

    def step(n, carry):
        s, q, ps, pq = carry
        fetch(n).wait()
        x = slots[pl.ds(4 * n, 4)]
        layers = lax.dot_general(
            codes[...], x.reshape(256, VOX), NT, preferred_element_type=F32
        )
        wide = x.astype(F32)
        for k in range(4):
            for v in range(4):
                piece = wide[k, :, 128 * v : 128 * v + 128]
                s = s + piece
                q = q + piece * piece
        for j in range(2):
            for f in range(7):
                low = layers[64 * f : 64 * f + 32, 128 * j : 128 * j + 128]
                high = layers[64 * f + 32 : 64 * f + 64, 128 * j : 128 * j + 128]
                pair = (
                    jnp.where(left, low, pltpu.roll(high, 64, 1)),
                    jnp.where(left, pltpu.roll(low, 64, 1), high),
                )
                for k in range(2):
                    unit = pair[k].astype(BF16)
                    slot = 4 * n + 2 * j + k
                    if f < 6:
                        held[slot * 3 + f // 2, 32 * (f % 2) : 32 * (f % 2) + 32] = unit
                    else:
                        pooled[slot] = unit
                        wide = unit.astype(F32)
                        ps = ps + wide
                        pq = pq + wide * wide
        keep(n).start()
        return s, q, ps, pq

    zero = jnp.zeros((64, 128), F32)
    small = jnp.zeros((32, 128), F32)
    s, q, ps, pq = lax.fori_loop(0, 8, step, (zero, zero, small, small), unroll=2)
    cut_in.wait()
    cut_out.start()
    ones = jnp.ones((8, 128), F32)
    both = jnp.concatenate([s, q], axis=0)
    rows = lax.dot_general(ones, both, NT, precision=HIGH, preferred_element_type=F32)
    turned = pltpu.roll(rows, 64, 1)
    first = lanes(8) < 64
    stat[...] = jnp.zeros((16, 128), F32)
    put_terms(stat, 0, jnp.where(first, rows, turned)[0:1])
    put_terms(stat, 3, jnp.where(first, turned, rows)[0:1])
    put_terms(stat, 6, jnp.sum(ps, axis=0, keepdims=True))
    put_terms(stat, 9, jnp.sum(pq, axis=0, keepdims=True))
    sums = stat[...].astype(BF16)

    def send(p, _):
        for k in range(2):
            code = jnp.minimum(links[k, p], FACES - 1)
            at = pl.multiple_of(32 * (code & 1), 32)
            send_buf[p, 32 * k : 32 * k + 32] = held[code >> 1, pl.ds(at, 32)]
            send_buf[p, 64 + 32 * k : 96 + 32 * k] = pooled[jnp.minimum(csend[k, p], SLOTS - 1)]
        send_buf[p, 128:144] = sums
        return 0

    lax.fori_loop(0, DEVS, send, 0, unroll=8)
    give = pltpu.make_async_copy(send_buf, out, sem.at[8])
    give.start()
    for n in range(8):
        keep(n).wait()
    cut_out.wait()
    give.wait()


def plan_kernel(nbr, links, csend, crecv, sel, tsel, ssel, owner, lslot):
    def slot_of(n, _):
        for f in range(6):
            near = nbr[f, n]
            sel[n * 6 + f] = jnp.where(near < SLOTS, near * 6 + (f ^ 1), FACES + 2 * DEVS)
            owner[n * 6 + f] = jnp.where(near < SLOTS, near, SLOTS + 2 * DEVS)
        return 0

    lax.fori_loop(0, SLOTS, slot_of, 0)

    def empty(i, _):
        tsel[i] = 2 * DEVS
        return 0

    lax.fori_loop(0, CODES, empty, 0)

    def mark(p, _):
        for k in range(2):
            code = links[k, p]
            lslot[2 * p + k] = lax.div(jnp.minimum(code, FACES - 1), 6)

            @pl.when(code < FACES)
            def _():
                sel[code] = FACES + 2 * p + k
                owner[code] = SLOTS + 2 * p + k

            place = crecv[k, p]

            @pl.when(place < CODES)
            def _():
                tsel[place] = 2 * p + k

            slot = csend[k, p]

            @pl.when(slot < SLOTS)
            def _():
                ssel[slot] = 2 * p + k

        return 0

    lax.fori_loop(0, DEVS, mark, 0)


def border1_kernel(
    sel, tsel, me, par, faces, recv, x1, x2, x3,
    p0, p1, p2, p3, o0, o1, o2, o3,
    told_in, rough_in, src, first, buf, stat, psem, sem, load,
):
    y = me[0]
    fetches = [
        pltpu.make_async_copy(recv.at[:, pl.ds(128, 16)], told_in, load.at[0]),
        pltpu.make_async_copy(recv.at[:, pl.ds(64, 64)], rough_in, load.at[1]),
        pltpu.make_async_copy(recv.at[:, pl.ds(0, 64)], src.at[pl.ds(96, DEVS)], load.at[2]),
        pltpu.make_async_copy(faces, src.at[pl.ds(0, 96)], load.at[3]),
    ]
    for fetch in fetches:
        fetch.start()
    src[96 + DEVS] = jnp.zeros((64, 128), BF16)
    fetches[0].wait()

    def add(s, total):
        return total + told_in[s].astype(F32)

    sums = lax.fori_loop(0, DEVS, add, jnp.zeros((16, 128), F32), unroll=8)
    fine = float(DEVS * SLOTS * VOX * GROUP)
    rough = float(DEVS * SLOTS * 64 * GROUP)
    groups = group_matrix(64)
    mean1, scale1 = norm_rows(
        group_sum(joined(sums, 0), groups) * 0.5,
        group_sum(joined(sums, 3), groups) * 0.5,
        fine,
        par[0:1],
    )
    mean3, scale3 = norm_rows(
        group_sum(joined(sums, 6), groups), group_sum(joined(sums, 9), groups), rough, par[2:3]
    )
    bias1, bias3 = par[1:2], par[3:4]
    stat[...] = jnp.zeros((32, 128), F32)
    for k, row in enumerate((mean1, scale1, bias1, par[4:5], par[5:6], par[6:7])):
        put_terms(stat, 3 * k, row)
    told = stat[...].astype(BF16)
    fetches[1].wait()
    copies = []
    for r, p in enumerate((p0, p1, p2, p3)):
        q = (y + r) & 3
        first[r, 16] = told

        def octant(i, _):
            for k in range(8):
                far = tsel[q * 16 + i * 8 + k]
                link = jnp.minimum(far, 2 * DEVS - 1)
                at = pl.multiple_of(32 * (link & 1), 32)
                u = rough_in[link >> 1, pl.ds(at, 32)].astype(F32)
                v = silu((u - mean3) * scale3 + bias3)
                first[r, i * 8 + k] = (v * (far < 2 * DEVS).astype(F32)).astype(BF16)
            return 0

        lax.fori_loop(0, 2, octant, 0)
        copies.append(pltpu.make_async_copy(first.at[r], p, psem.at[r]))
        copies[-1].start()
    for fetch in fetches[2:]:
        fetch.wait()
    for r, o in enumerate((o0, o1, o2, o3)):
        q = (y + r) & 3

        def face(i, _):
            for f in range(6):
                at = sel[q * 48 + i * 6 + f]
                u = src[at >> 1, pl.ds(pl.multiple_of(32 * (at & 1), 32), 32)].astype(F32)
                v = silu((u - mean1) * scale1 + bias1)
                buf[r, i * 6 + f] = (v * (at < FACES + 2 * DEVS).astype(F32)).astype(BF16)
            return 0

        lax.fori_loop(0, QUART, face, 0)
        copies.append(pltpu.make_async_copy(buf.at[r], o, sem.at[r]))
        copies[-1].start()
    for copy in copies:
        copy.wait()


def interior_taps(act, taps):
    wide = act.astype(F32)
    cube = wide.reshape(8, 8, 8, 256)
    none = jnp.zeros((64, 256), BF16)
    wall = jnp.zeros((8, 1, 8, 256), F32)
    taps[:, 0:256] = act
    taps[0:64, 256:512] = none
    taps[64:512, 256:512] = act[0:448]
    taps[0:448, 512:768] = act[64:512]
    taps[448:512, 512:768] = none
    low = jnp.concatenate([wall, cube[:, 0:7]], axis=1)
    taps[:, 768:1024] = low.reshape(512, 256).astype(BF16)
    high = jnp.concatenate([cube[:, 1:8], wall], axis=1)
    taps[:, 1024:1280] = high.reshape(512, 256).astype(BF16)
    depth = lax.broadcasted_iota(jnp.int32, (512, 256), 0) % 8
    low = jnp.where(depth == 0, 0.0, pltpu.roll(wide, 1, 0))
    taps[:, 1280:1536] = low.astype(BF16)
    high = jnp.where(depth == 7, 0.0, pltpu.roll(wide, 511, 0))
    taps[:, 1536:1792] = high.astype(BF16)


def fill_weights(dst, first, second, core, which):
    for c in range(4):
        for side, part in enumerate((first, second)):
            at = pl.multiple_of(64 * c + 32 * (core ^ side), 32)
            for t in range(7):
                dst[pl.ds(at, 32), 256 * t : 256 * t + 256] = part[c, which, t]


def fill_cube(cube, volumes, y):
    for r, v in zip(ORDER, volumes):
        at = pl.multiple_of(((y - r) & 3) * 64, 64)
        cube[pl.ds(at, 64), :] = v[0].astype(F32)


def place_rows(rows, told, y, stat):
    rows[...] = jnp.zeros((8, 256), F32)
    for r, t in zip(ORDER, told):
        stat[(y - r) & 3] = t[0].astype(F32)
    for k in range(6):
        rows[k : k + 1, :] = gather_row([joined(stat[c], 3 * k) for c in range(4)])


def inner1_kernel(
    me, t0, t1, t2, t3, v0, v1, v2, v3, wa, wb, part, rows, weights, stat, taps, cube
):
    y = me[0]

    @pl.when(pl.program_id(0) == 0)
    def _():
        place_rows(rows, (t0, t1, t2, t3), y, stat)
        fill_weights(weights, wa, wb, me[1], 0)

    fill_cube(cube, (v0, v1, v2, v3), y)
    x = cube[...].T
    act = silu((x - rows[0:1]) * rows[1:2] + rows[2:3]).astype(BF16)
    interior_taps(act, taps)
    part[0] = lax.dot_general(taps[...], weights[...], NT, preferred_element_type=F32)


def inner2_kernel(me, rows, hid, wa, wb, part, weights, taps, cells, sem):
    step = pl.program_id(0)

    def fetch_cells(n):
        return pltpu.make_async_copy(hid.at[n], cells.at[n], sem.at[n])

    @pl.when(step == 0)
    def _():
        for n in range(QUART):
            fetch_cells(n).start()
        fill_weights(weights, wa, wb, me[1], 1)

    fetch_cells(step).wait()
    act = silu((cells[step] - rows[0:1]) * rows[1:2] + rows[2:3]).astype(BF16)
    interior_taps(act, taps)
    part[0] = lax.dot_general(taps[...], weights[...], NT, preferred_element_type=F32)


def border_terms(units, tap_weights, parts, y, across, start, count):
    for r, u in zip(ORDER, parts):
        units[(y - r) & 3] = u[...]
    for f in range(6):
        layer = jnp.concatenate(
            [
                unpack([units[c, 6 * n + f].astype(F32) for c in range(4)]).astype(BF16)
                for n in range(start, start + count)
            ],
            axis=0,
        )
        across[f] = lax.dot_general(
            layer,
            tap_weights[:, 256 * (f + 1) : 256 * (f + 2)],
            NT,
            preferred_element_type=F32,
        )


def add_borders(h, across, step, shift):
    at = pl.multiple_of(step * 64, 64)
    h = jnp.concatenate(
        [h[0:64] + across[0, pl.ds(at, 64), :], h[64:448], h[448:512] + across[1, pl.ds(at, 64), :]],
        axis=0,
    )
    deep = h.reshape(8, 8, 8, 256)
    low = across[2, pl.ds(at, 64), :].reshape(8, 1, 8, 256)
    high = across[3, pl.ds(at, 64), :].reshape(8, 1, 8, 256)
    h = jnp.concatenate([deep[:, 0:1] + low, deep[:, 1:7], deep[:, 7:8] + high], axis=1)
    h = h.reshape(512, 256)
    halves, edges = [], [[], []]
    for half in range(2):
        cut = slice(128 * half, 128 * half + 128)
        shift[half] = h[:, cut]
        for side in range(2):
            layer = shift[half, pl.ds(7 * side, 64, stride=8), :]
            layer = layer + across[4 + side, pl.ds(at, 64), cut]
            shift[half, pl.ds(7 * side, 64, stride=8), :] = layer
            edges[side].append(layer)
        halves.append(shift[half])
    h = jnp.concatenate(halves, axis=1)
    return h, [jnp.concatenate(pair, axis=1) for pair in edges]


def outer1_kernel(
    me, rows, part, u0, u1, u2, u3, tiles, weights,
    hid, o0, o1, o2, o3,
    units, outs, across, shift, stat, cells, sem,
):
    y = me[0]
    border_terms(units, weights, (u0, u1, u2, u3), y, across, 0, QUART)
    stat[...] = jnp.zeros((4, 32, 128), F32)

    def keep_cells(n):
        return pltpu.make_async_copy(cells.at[n], hid.at[n], sem.at[n])

    def slot(n, carry):
        all_total, all_square = carry
        h, edges = add_borders(part[n] + rows[3:4], across, n, shift)
        cells[n] = h
        keep_cells(n).start()
        total = jnp.sum(h, axis=0, keepdims=True)
        square = jnp.sum(h * h, axis=0, keepdims=True)
        centre = (total * (1.0 / VOX)).astype(BF16).astype(F32)
        for c, row in enumerate(spread_row(centre)):
            stat[c, pl.ds(n, 1), :] = row
        deep = h.reshape(8, 8, 8, 256)
        for f in range(6):
            if f < 2:
                layer = h[448 * f : 448 * f + 64]
            elif f < 4:
                layer = deep[:, 7 * (f - 2)].reshape(64, 256)
            else:
                layer = edges[f - 4]
            for c, unit in enumerate(pack(layer - centre)):
                outs[c, n * 6 + f] = unit.astype(BF16)
        return all_total + total, all_square + square

    nothing = jnp.zeros((1, 256), F32)
    sums = lax.fori_loop(0, QUART, slot, (nothing, nothing))
    at = 8
    for k in range(2):
        for half in range(2):
            for row in terms(sums[k][:, 128 * half : 128 * half + 128]):
                for c in range(4):
                    stat[c, at : at + 1, :] = row
                at += 1
    for c in range(4):
        outs[c, 48] = stat[c].astype(BF16)
    for r, o in enumerate((o0, o1, o2, o3)):
        o[0:49] = outs[(y + r) & 3]
        o[49:65] = tiles[(y + r) & 3]
    for n in range(QUART):
        keep_cells(n).wait()


def placement(rows, columns, code):
    row = lax.broadcasted_iota(jnp.int32, (rows, columns), 0)
    column = lax.broadcasted_iota(jnp.int32, (rows, columns), 1)
    return (code(row) == column).astype(F32).astype(BF16)


def octant_code(v):
    x, y, z = v >> 6, (v >> 3) & 7, v & 7
    octant = (x >> 2) * 4 + (y >> 2) * 2 + (z >> 2)
    return octant * 64 + (x & 3) * 16 + (y & 3) * 4 + (z & 3)


def voxel_code(w):
    octant, x, y, z = w >> 6, (w >> 4) & 3, (w >> 2) & 3, w & 3
    x, y, z = x + 4 * (octant >> 2), y + 4 * ((octant >> 1) & 1), z + 4 * (octant & 1)
    return x * 64 + y * 8 + z


def coarse_code(v):
    return ((v >> 7) & 3) * 16 + ((v >> 4) & 3) * 4 + ((v >> 1) & 3)


def tile_kernel(me, u0, u1, u2, u3, wa, wb, out, units, weights, taps, place, place_t):
    t = pl.program_id(0)
    y = me[0]

    @pl.when(t == 0)
    def _():
        place[...] = placement(VOX, VOX, octant_code)
        place_t[...] = placement(VOX, VOX, voxel_code)
        fill_weights(weights, wa, wb, me[1], 2)

    for r, u in zip(ORDER, (u0, u1, u2, u3)):
        units[(y - r) & 3] = u[...]
    octants = jnp.concatenate(
        [unpack([units[c, o].astype(F32) for c in range(4)]).astype(BF16) for o in range(8)], axis=0
    )
    act = lax.dot_general(place[...], octants, NN, preferred_element_type=F32).astype(BF16)
    interior_taps(act, taps)
    h = lax.dot_general(taps[...], weights[...], NT, preferred_element_type=F32).astype(BF16)
    pieces = lax.dot_general(place_t[...], h, NN, preferred_element_type=F32)
    for o in range(8):
        for c, unit in enumerate(pack(pieces[64 * o : 64 * o + 64])):
            out[c, o] = unit.astype(BF16)


def route2_kernel(
    links, lslot, crecv, me, v0, v1, v2, v3, keep, out, held, cen, stat, send_buf, sem
):
    y = me[0]
    for r, v in zip(ORDER, (v0, v1, v2, v3)):
        held[(y - r) & 3] = v[...]
    kept = pltpu.make_async_copy(held, keep, sem.at[0])
    kept.start()
    total = jnp.zeros((32, 128), F32)
    for q in range(4):
        told = held[q, 48].astype(F32)
        cen[8 * q : 8 * q + 8, :] = told[0:8]
        total = total + told
    stat[...] = jnp.zeros((16, 128), F32)
    for k in range(4):
        put_terms(stat, 2 + 3 * k, joined(total, 8 + 3 * k))

    def send(p, _):
        for k in range(2):
            code = jnp.minimum(links[k, p], FACES - 1)
            slot = lslot[2 * p + k]
            q = slot >> 3
            send_buf[p, 32 * k : 32 * k + 32] = held[q, code - 48 * q]
            stat[k : k + 1, :] = cen[pl.ds(slot, 1), :]
            place = jnp.minimum(crecv[k, p], CODES - 1)
            send_buf[p, 64 + 32 * k : 96 + 32 * k] = held[place >> 4, 49 + (place & 15)]
        send_buf[p, 128:144] = stat[...].astype(BF16)
        return 0

    lax.fori_loop(0, DEVS, send, 0, unroll=4)
    give = pltpu.make_async_copy(send_buf, out, sem.at[1])
    give.start()
    kept.wait()
    give.wait()


def own_row(row, y):
    wide = jnp.broadcast_to(jnp.where(y >= 2, row[:, 128:256], row[:, 0:128]), (8, 128))
    turned = pltpu.roll(wide, 64, 1)
    left = lanes(8) < 64
    odd = (y & 1) == 1
    return jnp.where(left, jnp.where(odd, turned, wide), jnp.where(odd, wide, turned))[0:1]


def border2_kernel(
    sel, ssel, owner, me, rows, held, recv, o0, o1, o2, o3, norm, src, cen, buf, sem, load
):
    y = me[0]
    fetches = []
    for q in range(4):
        fetches.append(
            pltpu.make_async_copy(held.at[q, pl.ds(0, 48)], src.at[pl.ds(48 * q, 48)], load.at[q])
        )
        fetches.append(pltpu.make_async_copy(held.at[q, 48], buf.at[q, 0], load.at[4 + q]))
    for fetch in fetches:
        fetch.start()

    def add(s, total):
        src[FACES + 2 * s] = recv[s, 0:32]
        src[FACES + 2 * s + 1] = recv[s, 32:64]
        told = recv[s, 128:144].astype(F32)
        cen[pl.ds(SLOTS + 2 * s, 2), :] = told[0:2]
        return total + told

    sums = lax.fori_loop(0, DEVS, add, jnp.zeros((16, 128), F32), unroll=8)
    src[FACES + 2 * DEVS] = jnp.zeros((32, 128), BF16)
    cen[pl.ds(SLOTS + 2 * DEVS, 8), :] = jnp.zeros((8, 128), F32)
    fine = float(DEVS * SLOTS * VOX * GROUP)
    groups = group_matrix(128)
    norm[...] = jnp.zeros((8, 256), F32)
    for half in range(2):
        cut = slice(128 * half, 128 * half + 128)
        mean, scale = norm_rows(
            group_sum(joined(sums, 2 + 3 * half), groups),
            group_sum(joined(sums, 8 + 3 * half), groups),
            fine,
            rows[4:5, cut],
        )
        norm[0:1, cut] = mean
        norm[1:2, cut] = scale
        norm[2:3, cut] = rows[5:6, cut]
    mean, scale, bias = (own_row(norm[k : k + 1, :], y) for k in range(3))
    for fetch in fetches:
        fetch.wait()
    for q in range(4):
        cen[8 * q : 8 * q + 8, :] = buf[q, 0].astype(F32)[0:8]
    copies = []
    for r, o in enumerate((o0, o1, o2, o3)):
        q = (y + r) & 3

        def face(i, _):
            for f in range(6):
                at = sel[q * 48 + i * 6 + f]
                whose = owner[q * 48 + i * 6 + f]
                u = src[at].astype(F32) + (cen[pl.ds(whose, 1), :] - mean)
                v = silu(u * scale + bias)
                buf[r, i * 6 + f] = (v * (at < FACES + 2 * DEVS).astype(F32)).astype(BF16)
            link = ssel[q * 8 + i]
            at = pl.multiple_of(64 + 32 * (link & 1), 32)
            buf[r, 48 + i] = recv[link >> 1, pl.ds(at, 32)]
            return 0

        lax.fori_loop(0, QUART, face, 0)
        copies.append(pltpu.make_async_copy(buf.at[r], o, sem.at[r]))
        copies[-1].start()
    for copy in copies:
        copy.wait()


def outer2_kernel(
    me, part, v0, v1, v2, v3, u0, u1, u2, u3, weights,
    o0, o1, o2, o3,
    units, across, shift, cube, lift,
    *, start,
):
    y = me[0]
    lift[...] = placement(VOX, 64, coarse_code)
    border_terms(units, weights, (u0, u1, u2, u3), y, across, start, HALF)

    def slot(n, _):
        m = start + n
        raised = unpack([units[c, 48 + m].astype(F32) for c in range(4)]).astype(BF16)
        lifted = lax.dot_general(lift[...], raised, NN, preferred_element_type=F32)
        h, _ = add_borders(part[m] + lifted, across, n, shift)
        for r, v in zip(ORDER, (v0, v1, v2, v3)):
            at = pl.multiple_of(((y - r) & 3) * 64, 64)
            cube[pl.ds(at, 64), :] = v[QUART * y + m if r == 0 else m].astype(F32)
        cube[...] += h.T
        for r, o in enumerate((o0, o1, o2, o3)):
            at = pl.multiple_of(((y + r) & 3) * 64, 64)
            o[n] = cube[pl.ds(at, 64), :].astype(BF16)
        return 0

    lax.fori_loop(0, HALF, slot, 0)


def gather_kernel(me, *refs):
    *parts, out, sem = refs
    y = me[0]
    copies = []
    for k, p in enumerate(parts):
        at = ((y - ORDER[k % 4]) & 3) * QUART + HALF * (k // 4)
        copies.append(pltpu.make_async_copy(p, out.at[pl.ds(at, HALF)], sem.at[k]))
        copies[-1].start()
    for copy in copies:
        copy.wait()


def shape(*dims, dtype=BF16):
    return jax.ShapeDtypeStruct(dims, dtype)


def call(kernel, name, mib, micros=1, **more):
    return pl.pallas_call(
        kernel,
        cost_estimate=pl.CostEstimate(
            flops=micros * 10**9, bytes_accessed=micros * 3 * 10**6, transcendentals=0
        ),
        compiler_params=pltpu.CompilerParams(vmem_limit_bytes=mib * MIB),
        name=name,
        **more,
    )


def exchange(parts, order=(0, 1, 2, 3)):
    got = {
        r: lax.ppermute(parts[r], "chan", [(i, (i + r) % 4) for i in order]) for r in ORDER[1:]
    }
    return [parts[0]] + [got[r] for r in ORDER[1:]]


def over_blocks(units):
    return lax.all_to_all(units, "blocks", split_axis=0, concat_axis=0, tiled=True)


def local(
    feats,
    conv_weights,
    norm_gain,
    norm_bias,
    time_bias,
    local_nbr,
    face_links,
    coarse_send,
    coarse_recv,
):
    extract_np = tables()
    y = lax.axis_index("chan").astype(jnp.int32)
    core = (lax.axis_index("blocks") % 2).astype(jnp.int32)
    me = jnp.stack([y, core])
    nbr = local_nbr.T
    links = face_links[0].T
    csend = coarse_send[0].T
    crecv = coarse_recv[0].T

    def twice(rows):
        block = jnp.stack(rows)
        block = jnp.concatenate([block, block], axis=1)
        return jnp.pad(block, ((0, 8 - block.shape[0]), (0, 0)))

    par = twice(
        [norm_gain[0], norm_bias[0], norm_gain[2], norm_bias[2], time_bias]
        + [norm_gain[1], norm_bias[1]]
    )
    faces, outgoing, half = call(
        extract_kernel,
        "extract",
        60,
        out_shape=(
            shape(FACES // 2, 64, 128),
            shape(DEVS, ROWS, 128),
            shape(3, 7, 32, 256),
        ),
        in_specs=[SMEM] * 3 + [HBM] * 3,
        out_specs=(HBM,) * 3,
        scratch_shapes=[
            pltpu.VMEM((SLOTS, 64, VOX), BF16),
            pltpu.VMEM((448, VOX), BF16),
            pltpu.VMEM((FACES // 2, 64, 128), BF16),
            pltpu.VMEM((SLOTS, 32, 128), BF16),
            pltpu.VMEM((16, 128), F32),
            pltpu.VMEM((DEVS, ROWS, 128), BF16),
            pltpu.VMEM((3, 7, 32, 256), BF16),
            pltpu.SemaphoreType.DMA((10,)),
            pltpu.SemaphoreType.DMA((10,)),
        ],
    )(links, csend, me, feats, jnp.asarray(extract_np, BF16), conv_weights)
    wa = lax.all_gather(half, "chan", axis=0, tiled=False)
    arrived = over_blocks(outgoing)
    volumes = exchange(
        [feats]
        + [
            lax.dynamic_slice_in_dim(feats, QUART * ((y + r) % 4), QUART, axis=0)
            for r in range(1, 4)
        ]
    )
    sel, tsel, ssel, owner, lslot = call(
        plan_kernel,
        "plan",
        4,
        20,
        out_shape=(
            shape(FACES, dtype=jnp.int32),
            shape(CODES, dtype=jnp.int32),
            shape(SLOTS, dtype=jnp.int32),
            shape(FACES, dtype=jnp.int32),
            shape(2 * DEVS, dtype=jnp.int32),
        ),
        in_specs=[SMEM] * 4,
        out_specs=(SMEM,) * 5,
    )(nbr, links, csend, crecv)

    parts = call(
        border1_kernel,
        "border1",
        60,
        out_shape=(shape(17, 32, 128),) * 4 + (shape(48, 32, 128),) * 4,
        in_specs=[SMEM] * 3 + [VMEM] + [HBM] * 5,
        out_specs=(HBM,) * 8,
        scratch_shapes=[
            pltpu.VMEM((DEVS, 16, 128), BF16),
            pltpu.VMEM((DEVS, 64, 128), BF16),
            pltpu.VMEM((FACES // 2 + DEVS + 1, 64, 128), BF16),
            pltpu.VMEM((4, 17, 32, 128), BF16),
            pltpu.VMEM((4, 48, 32, 128), BF16),
            pltpu.VMEM((32, 128), F32),
            pltpu.SemaphoreType.DMA((4,)),
            pltpu.SemaphoreType.DMA((4,)),
            pltpu.SemaphoreType.DMA((4,)),
        ],
    )(sel, tsel, me, par, faces, arrived, *volumes[1:])
    tiles1 = exchange(parts[:4], (3, 2, 1, 0))
    units1 = exchange(parts[4:])
    wa, _ = lax.optimization_barrier((wa, parts[0]))
    wb = lax.ppermute(wa, "blocks", [(i, i ^ 1) for i in range(DEVS)])

    cells = pl.BlockSpec((1, VOX, 256), lambda i: (i, 0, 0))

    def prefetched(count, in_specs, out_specs, scratch_shapes):
        return pltpu.PrefetchScalarGridSpec(
            num_scalar_prefetch=1,
            grid=(count,),
            in_specs=in_specs,
            out_specs=out_specs,
            scratch_shapes=scratch_shapes,
        )

    def slot_specs(start):
        first = pl.BlockSpec((1, 64, VOX), lambda i, me: (QUART * me[0] + start + i, 0, 0))
        return [first] + [pl.BlockSpec((1, 64, VOX), lambda i, me: (start + i, 0, 0))] * 3

    def cell_spec(start):
        return pl.BlockSpec((1, VOX, 256), lambda i, me: (start + i, 0, 0))

    last = pl.BlockSpec((1, 32, 128), lambda i, me: (16, 0, 0))
    part1, rows, weights = call(
        inner1_kernel,
        "inner1",
        24,
        8,
        grid_spec=prefetched(
            QUART,
            [last] * 4 + slot_specs(0) + [VMEM] * 2,
            (cell_spec(0), VMEM, VMEM),
            [
                pltpu.VMEM((4, 32, 128), F32),
                pltpu.VMEM((VOX, 1792), BF16),
                pltpu.VMEM((256, VOX), F32),
            ],
        ),
        out_shape=(
            shape(QUART, VOX, 256, dtype=F32),
            shape(8, 256, dtype=F32),
            shape(256, 1792),
        ),
    )(me, *tiles1, *volumes, wa, wb)
    eight = pl.BlockSpec((8, 32, 128), lambda t: (t, 0, 0))
    coarse = call(
        tile_kernel,
        "tiles",
        24,
        4,
        grid=(TILES,),
        out_shape=shape(4, 16, 32, 128),
        in_specs=[SMEM] + [eight] * 4 + [VMEM] * 2,
        out_specs=pl.BlockSpec((4, 8, 32, 128), lambda t: (0, t, 0, 0)),
        scratch_shapes=[
            pltpu.VMEM((4, 8, 32, 128), BF16),
            pltpu.VMEM((256, 1792), BF16),
            pltpu.VMEM((VOX, 1792), BF16),
            pltpu.VMEM((VOX, VOX), BF16),
            pltpu.VMEM((VOX, VOX), BF16),
        ],
    )(me, *tiles1, wa, wb)
    hidden, *parts = call(
        outer1_kernel,
        "outer1",
        32,
        5,
        out_shape=(shape(QUART, VOX, 256, dtype=F32),) + (shape(65, 32, 128),) * 4,
        in_specs=[SMEM] + [VMEM] * 8,
        out_specs=(HBM,) + (VMEM,) * 4,
        scratch_shapes=[
            pltpu.VMEM((4, 48, 32, 128), BF16),
            pltpu.VMEM((4, 49, 32, 128), BF16),
            pltpu.VMEM((6, VOX, 256), F32),
            pltpu.VMEM((2, VOX, 128), F32),
            pltpu.VMEM((4, 32, 128), F32),
            pltpu.VMEM((QUART, VOX, 256), F32),
            pltpu.SemaphoreType.DMA((QUART,)),
        ],
    )(me, rows, part1, *units1, coarse, weights)
    units = exchange(parts)

    held, outgoing = call(
        route2_kernel,
        "route2",
        12,
        out_shape=(shape(4, 65, 32, 128), shape(DEVS, ROWS, 128)),
        in_specs=[SMEM] * 4 + [VMEM] * 4,
        out_specs=(HBM, HBM),
        scratch_shapes=[
            pltpu.VMEM((4, 65, 32, 128), BF16),
            pltpu.VMEM((SLOTS, 128), F32),
            pltpu.VMEM((16, 128), F32),
            pltpu.VMEM((DEVS, ROWS, 128), BF16),
            pltpu.SemaphoreType.DMA((2,)),
        ],
    )(links, lslot, crecv, me, *units)
    arrived = over_blocks(outgoing)

    *parts, norm = call(
        border2_kernel,
        "border2",
        12,
        out_shape=(shape(56, 32, 128),) * 4 + (shape(8, 256, dtype=F32),),
        in_specs=[SMEM] * 4 + [VMEM, HBM, VMEM],
        out_specs=(ANY,) * 4 + (VMEM,),
        scratch_shapes=[
            pltpu.VMEM((FACES + 2 * DEVS + 1, 32, 128), BF16),
            pltpu.VMEM((SLOTS + 2 * DEVS + 8, 128), F32),
            pltpu.VMEM((4, 56, 32, 128), BF16),
            pltpu.SemaphoreType.DMA((4,)),
            pltpu.SemaphoreType.DMA((8,)),
        ],
    )(sel, ssel, owner, me, rows, held, arrived)
    units2 = exchange(parts)
    part2, weights = call(
        inner2_kernel,
        "inner2",
        24,
        8,
        grid=(QUART,),
        out_shape=(shape(QUART, VOX, 256, dtype=F32), shape(256, 1792)),
        in_specs=[SMEM, VMEM, HBM, VMEM, VMEM],
        out_specs=(cells, VMEM),
        scratch_shapes=[
            pltpu.VMEM((VOX, 1792), BF16),
            pltpu.VMEM((QUART, VOX, 256), F32),
            pltpu.SemaphoreType.DMA((QUART,)),
        ],
    )(me, norm, hidden, wa, wb)
    pieces = []
    for start in (0, HALF):
        parts = call(
            functools.partial(outer2_kernel, start=start),
            "outer2",
            32,
            5,
            in_specs=[SMEM] + [VMEM] * 10,
            out_specs=(VMEM,) * 4,
            scratch_shapes=[
                pltpu.VMEM((4, 56, 32, 128), BF16),
                pltpu.VMEM((6, 64 * HALF, 256), F32),
                pltpu.VMEM((2, VOX, 128), F32),
                pltpu.VMEM((256, VOX), F32),
                pltpu.VMEM((VOX, 64), BF16),
            ],
            out_shape=(shape(HALF, 64, VOX),) * 4,
        )(me, part2, *volumes, *units2, weights)
        pieces += exchange(parts, (0, 1, 2, 3) if start == 0 else (3, 2, 1, 0))
    return call(
        gather_kernel,
        "gather",
        4,
        out_shape=shape(SLOTS, 64, VOX),
        in_specs=[SMEM] + [ANY] * 8,
        out_specs=HBM,
        scratch_shapes=[pltpu.SemaphoreType.DMA((8,))],
    )(me, *pieces)


def solution(mesh):
    in_specs = (
        P("blocks", "chan", None),
        P(None, None, "chan", None),
        P(None, "chan"),
        P(None, "chan"),
        P("chan"),
        P("blocks", None),
        P("blocks", None, None),
        P("blocks", None, None),
        P("blocks", None, None),
    )
    out_specs = P("blocks", "chan", None)
    return jax.shard_map(local, mesh=mesh, in_specs=in_specs, out_specs=out_specs, check_vma=False)
```

```python
import functools

import jax
import jax.numpy as jnp
import numpy as np
from jax import lax
from jax.experimental import pallas as pl
from jax.experimental.pallas import tpu as pltpu
from jax.sharding import PartitionSpec as P

GROUP = 8
SIDE = 8
VOX = 512
SLOTS = 32
DEVS = 32
QUART = 8
HALF = 4
TILES = 2
FACES = 6 * SLOTS
CODES = 64
EPS = 1e-05
ORDER = (0, 2, 1, 3)
F32 = jnp.float32
BF16 = jnp.bfloat16
HIGH = lax.Precision.HIGHEST
NT = (((1,), (1,)), ((), ()))
NN = (((1,), (0,)), ((), ()))
VMEM = pl.BlockSpec(memory_space=pltpu.VMEM)
ANY = pl.BlockSpec(memory_space=pl.ANY)
HBM = pl.BlockSpec(memory_space=pltpu.HBM)
SMEM = pl.BlockSpec(memory_space=pltpu.SMEM)
MIB = 1024 * 1024
ROWS = 144


def tables():
    places = np.arange(VOX)
    coords = (places // 64, places // 8 % 8, places % 8)
    extract = np.zeros((7 * 64, VOX), np.float32)
    for face in range(6):
        along = face // 2
        others = [coords[k] for k in range(3) if k != along]
        chosen = coords[along] == (0 if face % 2 == 0 else SIDE - 1)
        extract[face * 64 + (8 * others[0] + others[1])[chosen], places[chosen]] = 1.0
    x, y, z = coords
    extract[384 + x // 2 * 16 + y // 2 * 4 + z // 2, places] = 0.125
    return extract


def lanes(rows):
    return lax.broadcasted_iota(jnp.int32, (rows, 128), 1)


def terms(value):
    high = value.astype(BF16).astype(F32)
    rest = value - high
    middle = rest.astype(BF16).astype(F32)
    return high, middle, rest - middle


def joined(block, row):
    return (block[row + 2 : row + 3] + block[row + 1 : row + 2]) + block[row : row + 1]


def put_terms(ref, row, value):
    for k, part in enumerate(terms(value)):
        ref[row + k : row + k + 1, :] = part


def silu(u):
    half = 0.5 * u
    return half + half * jnp.tanh(half)


def group_matrix(period):
    row = lax.broadcasted_iota(jnp.int32, (128, 128), 0) % period // GROUP
    col = lax.broadcasted_iota(jnp.int32, (128, 128), 1) % period // GROUP
    return (row == col).astype(F32)


def group_sum(row, groups=None):
    wide = jnp.broadcast_to(row, (8, 128))
    groups = group_matrix(64) if groups is None else groups
    return lax.dot_general(wide, groups, NN, precision=HIGH, preferred_element_type=F32)[0:1]


def norm_rows(total, square, entries, gain):
    mean = total * (1.0 / entries)
    spread = square * (1.0 / entries) - mean * mean
    return mean, lax.rsqrt(spread + EPS) * gain


def unpack(parts):
    left = lanes(32) < 64
    low, high = [], []
    for a, b in ((parts[0], parts[1]), (parts[2], parts[3])):
        low.append(jnp.where(left, a, pltpu.roll(b, 64, 1)))
        high.append(jnp.where(left, pltpu.roll(a, 64, 1), b))
    return jnp.concatenate(
        [jnp.concatenate(low, axis=1), jnp.concatenate(high, axis=1)], axis=0
    )


def pack(cells):
    left = lanes(32) < 64
    parts = []
    for half in range(2):
        low = cells[0:32, 128 * half : 128 * half + 128]
        high = cells[32:64, 128 * half : 128 * half + 128]
        parts.append(jnp.where(left, low, pltpu.roll(high, 64, 1)))
        parts.append(jnp.where(left, pltpu.roll(low, 64, 1), high))
    return parts


def spread_row(row):
    left = lanes(1) < 64
    parts = []
    for half in range(2):
        part = row[:, 128 * half : 128 * half + 128]
        turned = pltpu.roll(jnp.broadcast_to(part, (8, 128)), 64, 1)[0:1]
        parts.append(jnp.where(left, part, turned))
        parts.append(jnp.where(left, turned, part))
    return parts


def gather_row(rows):
    left = lanes(1) < 64
    return jnp.concatenate(
        [jnp.where(left, rows[0], rows[1]), jnp.where(left, rows[2], rows[3])], axis=1
    )


def extract_kernel(
    links, csend, me, feats, table, kernels, faces, out, half,
    slots, codes, held, pooled, stat, send_buf, cut, sem, load,
):
    left = lanes(32) < 64
    at = pl.multiple_of(32 * me[1], 32)
    cut_in = pltpu.make_async_copy(kernels.at[:, :, pl.ds(at, 32)], cut, load.at[9])
    cut_out = pltpu.make_async_copy(cut, half, sem.at[9])

    def fetch(n):
        here = pl.ds(4 * n, 4)
        return pltpu.make_async_copy(feats.at[here], slots.at[here], load.at[n])

    def keep(n):
        here = pl.ds(12 * n, 12)
        return pltpu.make_async_copy(held.at[here], faces.at[here], sem.at[n])

    get_codes = pltpu.make_async_copy(table, codes, load.at[8])
    fetch(0).start()
    get_codes.start()
    for n in range(1, 8):
        fetch(n).start()
    cut_in.start()
    get_codes.wait()

    def step(n, carry):
        s, q, ps, pq = carry
        fetch(n).wait()
        x = slots[pl.ds(4 * n, 4)]
        layers = lax.dot_general(
            codes[...], x.reshape(256, VOX), NT, preferred_element_type=F32
        )
        wide = x.astype(F32)
        for k in range(4):
            for v in range(4):
                piece = wide[k, :, 128 * v : 128 * v + 128]
                s = s + piece
                q = q + piece * piece
        for j in range(2):
            for f in range(7):
                low = layers[64 * f : 64 * f + 32, 128 * j : 128 * j + 128]
                high = layers[64 * f + 32 : 64 * f + 64, 128 * j : 128 * j + 128]
                pair = (
                    jnp.where(left, low, pltpu.roll(high, 64, 1)),
                    jnp.where(left, pltpu.roll(low, 64, 1), high),
                )
                for k in range(2):
                    unit = pair[k].astype(BF16)
                    slot = 4 * n + 2 * j + k
                    if f < 6:
                        held[slot * 3 + f // 2, 32 * (f % 2) : 32 * (f % 2) + 32] = unit
                    else:
                        pooled[slot] = unit
                        wide = unit.astype(F32)
                        ps = ps + wide
                        pq = pq + wide * wide
        keep(n).start()
        return s, q, ps, pq

    zero = jnp.zeros((64, 128), F32)
    small = jnp.zeros((32, 128), F32)
    s, q, ps, pq = lax.fori_loop(0, 8, step, (zero, zero, small, small), unroll=2)
    cut_in.wait()
    cut_out.start()
    ones = jnp.ones((8, 128), F32)
    both = jnp.concatenate([s, q], axis=0)
    rows = lax.dot_general(ones, both, NT, precision=HIGH, preferred_element_type=F32)
    turned = pltpu.roll(rows, 64, 1)
    first = lanes(8) < 64
    stat[...] = jnp.zeros((16, 128), F32)
    put_terms(stat, 0, jnp.where(first, rows, turned)[0:1])
    put_terms(stat, 3, jnp.where(first, turned, rows)[0:1])
    put_terms(stat, 6, jnp.sum(ps, axis=0, keepdims=True))
    put_terms(stat, 9, jnp.sum(pq, axis=0, keepdims=True))
    sums = stat[...].astype(BF16)

    def send(p, _):
        for k in range(2):
            code = jnp.minimum(links[k, p], FACES - 1)
            at = pl.multiple_of(32 * (code & 1), 32)
            send_buf[p, 32 * k : 32 * k + 32] = held[code >> 1, pl.ds(at, 32)]
            send_buf[p, 64 + 32 * k : 96 + 32 * k] = pooled[jnp.minimum(csend[k, p], SLOTS - 1)]
        send_buf[p, 128:144] = sums
        return 0

    lax.fori_loop(0, DEVS, send, 0, unroll=8)
    give = pltpu.make_async_copy(send_buf, out, sem.at[8])
    give.start()
    for n in range(8):
        keep(n).wait()
    cut_out.wait()
    give.wait()


def plan_kernel(nbr, links, csend, crecv, sel, tsel, ssel, owner, lslot):
    def slot_of(n, _):
        for f in range(6):
            near = nbr[f, n]
            sel[n * 6 + f] = jnp.where(near < SLOTS, near * 6 + (f ^ 1), FACES + 2 * DEVS)
            owner[n * 6 + f] = jnp.where(near < SLOTS, near, SLOTS + 2 * DEVS)
        return 0

    lax.fori_loop(0, SLOTS, slot_of, 0)

    def empty(i, _):
        tsel[i] = 2 * DEVS
        return 0

    lax.fori_loop(0, CODES, empty, 0)

    def mark(p, _):
        for k in range(2):
            code = links[k, p]
            lslot[2 * p + k] = lax.div(jnp.minimum(code, FACES - 1), 6)

            @pl.when(code < FACES)
            def _():
                sel[code] = FACES + 2 * p + k
                owner[code] = SLOTS + 2 * p + k

            place = crecv[k, p]

            @pl.when(place < CODES)
            def _():
                tsel[place] = 2 * p + k

            slot = csend[k, p]

            @pl.when(slot < SLOTS)
            def _():
                ssel[slot] = 2 * p + k

        return 0

    lax.fori_loop(0, DEVS, mark, 0)


def border1_kernel(
    sel, tsel, me, par, faces, recv, x1, x2, x3,
    p0, p1, p2, p3, o0, o1, o2, o3,
    told_in, rough_in, src, first, buf, stat, psem, sem, load,
):
    y = me[0]
    fetches = [
        pltpu.make_async_copy(recv.at[:, pl.ds(128, 16)], told_in, load.at[0]),
        pltpu.make_async_copy(recv.at[:, pl.ds(64, 64)], rough_in, load.at[1]),
        pltpu.make_async_copy(recv.at[:, pl.ds(0, 64)], src.at[pl.ds(96, DEVS)], load.at[2]),
        pltpu.make_async_copy(faces, src.at[pl.ds(0, 96)], load.at[3]),
    ]
    for fetch in fetches:
        fetch.start()
    src[96 + DEVS] = jnp.zeros((64, 128), BF16)
    fetches[0].wait()

    def add(s, total):
        return total + told_in[s].astype(F32)

    sums = lax.fori_loop(0, DEVS, add, jnp.zeros((16, 128), F32), unroll=8)
    fine = float(DEVS * SLOTS * VOX * GROUP)
    rough = float(DEVS * SLOTS * 64 * GROUP)
    groups = group_matrix(64)
    mean1, scale1 = norm_rows(
        group_sum(joined(sums, 0), groups) * 0.5,
        group_sum(joined(sums, 3), groups) * 0.5,
        fine,
        par[0:1],
    )
    mean3, scale3 = norm_rows(
        group_sum(joined(sums, 6), groups), group_sum(joined(sums, 9), groups), rough, par[2:3]
    )
    bias1, bias3 = par[1:2], par[3:4]
    stat[...] = jnp.zeros((32, 128), F32)
    for k, row in enumerate((mean1, scale1, bias1, par[4:5], par[5:6], par[6:7])):
        put_terms(stat, 3 * k, row)
    told = stat[...].astype(BF16)
    fetches[1].wait()
    copies = []
    for r, p in enumerate((p0, p1, p2, p3)):
        q = (y + r) & 3
        first[r, 16] = told

        def octant(i, _):
            for k in range(8):
                far = tsel[q * 16 + i * 8 + k]
                link = jnp.minimum(far, 2 * DEVS - 1)
                at = pl.multiple_of(32 * (link & 1), 32)
                u = rough_in[link >> 1, pl.ds(at, 32)].astype(F32)
                v = silu((u - mean3) * scale3 + bias3)
                first[r, i * 8 + k] = (v * (far < 2 * DEVS).astype(F32)).astype(BF16)
            return 0

        lax.fori_loop(0, 2, octant, 0)
        copies.append(pltpu.make_async_copy(first.at[r], p, psem.at[r]))
        copies[-1].start()
    for fetch in fetches[2:]:
        fetch.wait()
    for r, o in enumerate((o0, o1, o2, o3)):
        q = (y + r) & 3

        def face(i, _):
            for f in range(6):
                at = sel[q * 48 + i * 6 + f]
                u = src[at >> 1, pl.ds(pl.multiple_of(32 * (at & 1), 32), 32)].astype(F32)
                v = silu((u - mean1) * scale1 + bias1)
                buf[r, i * 6 + f] = (v * (at < FACES + 2 * DEVS).astype(F32)).astype(BF16)
            return 0

        lax.fori_loop(0, QUART, face, 0)
        copies.append(pltpu.make_async_copy(buf.at[r], o, sem.at[r]))
        copies[-1].start()
    for copy in copies:
        copy.wait()


def interior_taps(act, taps):
    wide = act.astype(F32)
    cube = wide.reshape(8, 8, 8, 256)
    none = jnp.zeros((64, 256), BF16)
    wall = jnp.zeros((8, 1, 8, 256), F32)
    taps[:, 0:256] = act
    taps[0:64, 256:512] = none
    taps[64:512, 256:512] = act[0:448]
    taps[0:448, 512:768] = act[64:512]
    taps[448:512, 512:768] = none
    low = jnp.concatenate([wall, cube[:, 0:7]], axis=1)
    taps[:, 768:1024] = low.reshape(512, 256).astype(BF16)
    high = jnp.concatenate([cube[:, 1:8], wall], axis=1)
    taps[:, 1024:1280] = high.reshape(512, 256).astype(BF16)
    depth = lax.broadcasted_iota(jnp.int32, (512, 256), 0) % 8
    low = jnp.where(depth == 0, 0.0, pltpu.roll(wide, 1, 0))
    taps[:, 1280:1536] = low.astype(BF16)
    high = jnp.where(depth == 7, 0.0, pltpu.roll(wide, 511, 0))
    taps[:, 1536:1792] = high.astype(BF16)


def fill_weights(dst, first, second, core, which):
    for c in range(4):
        for side, part in enumerate((first, second)):
            at = pl.multiple_of(64 * c + 32 * (core ^ side), 32)
            for t in range(7):
                dst[pl.ds(at, 32), 256 * t : 256 * t + 256] = part[c, which, t]


def fill_cube(cube, volumes, y):
    for r, v in zip(ORDER, volumes):
        at = pl.multiple_of(((y - r) & 3) * 64, 64)
        cube[pl.ds(at, 64), :] = v[0].astype(F32)


def place_rows(rows, told, y, stat):
    rows[...] = jnp.zeros((8, 256), F32)
    for r, t in zip(ORDER, told):
        stat[(y - r) & 3] = t[0].astype(F32)
    for k in range(6):
        rows[k : k + 1, :] = gather_row([joined(stat[c], 3 * k) for c in range(4)])


def inner1_kernel(
    me, t0, t1, t2, t3, v0, v1, v2, v3, wa, wb, part, rows, weights, stat, taps, cube
):
    y = me[0]

    @pl.when(pl.program_id(0) == 0)
    def _():
        place_rows(rows, (t0, t1, t2, t3), y, stat)
        fill_weights(weights, wa, wb, me[1], 0)

    fill_cube(cube, (v0, v1, v2, v3), y)
    x = cube[...].T
    act = silu((x - rows[0:1]) * rows[1:2] + rows[2:3]).astype(BF16)
    interior_taps(act, taps)
    part[0] = lax.dot_general(taps[...], weights[...], NT, preferred_element_type=F32)


def inner2_kernel(me, rows, hid, wa, wb, part, weights, taps, cells, sem):
    step = pl.program_id(0)

    def fetch_cells(n):
        return pltpu.make_async_copy(hid.at[n], cells.at[n], sem.at[n])

    @pl.when(step == 0)
    def _():
        for n in range(QUART):
            fetch_cells(n).start()
        fill_weights(weights, wa, wb, me[1], 1)

    fetch_cells(step).wait()
    act = silu((cells[step] - rows[0:1]) * rows[1:2] + rows[2:3]).astype(BF16)
    interior_taps(act, taps)
    part[0] = lax.dot_general(taps[...], weights[...], NT, preferred_element_type=F32)


def border_terms(units, tap_weights, parts, y, across, start, count):
    for r, u in zip(ORDER, parts):
        units[(y - r) & 3] = u[...]
    for f in range(6):
        layer = jnp.concatenate(
            [
                unpack([units[c, 6 * n + f].astype(F32) for c in range(4)]).astype(BF16)
                for n in range(start, start + count)
            ],
            axis=0,
        )
        across[f] = lax.dot_general(
            layer,
            tap_weights[:, 256 * (f + 1) : 256 * (f + 2)],
            NT,
            preferred_element_type=F32,
        )


def add_borders(h, across, step, shift):
    at = pl.multiple_of(step * 64, 64)
    h = jnp.concatenate(
        [h[0:64] + across[0, pl.ds(at, 64), :], h[64:448], h[448:512] + across[1, pl.ds(at, 64), :]],
        axis=0,
    )
    deep = h.reshape(8, 8, 8, 256)
    low = across[2, pl.ds(at, 64), :].reshape(8, 1, 8, 256)
    high = across[3, pl.ds(at, 64), :].reshape(8, 1, 8, 256)
    h = jnp.concatenate([deep[:, 0:1] + low, deep[:, 1:7], deep[:, 7:8] + high], axis=1)
    h = h.reshape(512, 256)
    halves, edges = [], [[], []]
    for half in range(2):
        cut = slice(128 * half, 128 * half + 128)
        shift[half] = h[:, cut]
        for side in range(2):
            layer = shift[half, pl.ds(7 * side, 64, stride=8), :]
            layer = layer + across[4 + side, pl.ds(at, 64), cut]
            shift[half, pl.ds(7 * side, 64, stride=8), :] = layer
            edges[side].append(layer)
        halves.append(shift[half])
    h = jnp.concatenate(halves, axis=1)
    return h, [jnp.concatenate(pair, axis=1) for pair in edges]


def outer1_kernel(
    me, rows, part, u0, u1, u2, u3, tiles, weights,
    hid, o0, o1, o2, o3,
    units, outs, across, shift, stat, cells, sem,
):
    y = me[0]
    border_terms(units, weights, (u0, u1, u2, u3), y, across, 0, QUART)
    stat[...] = jnp.zeros((4, 32, 128), F32)

    def keep_cells(n):
        return pltpu.make_async_copy(cells.at[n], hid.at[n], sem.at[n])

    def slot(n, carry):
        all_total, all_square = carry
        h, edges = add_borders(part[n] + rows[3:4], across, n, shift)
        cells[n] = h
        keep_cells(n).start()
        total = jnp.sum(h, axis=0, keepdims=True)
        square = jnp.sum(h * h, axis=0, keepdims=True)
        centre = (total * (1.0 / VOX)).astype(BF16).astype(F32)
        for c, row in enumerate(spread_row(centre)):
            stat[c, pl.ds(n, 1), :] = row
        deep = h.reshape(8, 8, 8, 256)
        for f in range(6):
            if f < 2:
                layer = h[448 * f : 448 * f + 64]
            elif f < 4:
                layer = deep[:, 7 * (f - 2)].reshape(64, 256)
            else:
                layer = edges[f - 4]
            for c, unit in enumerate(pack(layer - centre)):
                outs[c, n * 6 + f] = unit.astype(BF16)
        return all_total + total, all_square + square

    nothing = jnp.zeros((1, 256), F32)
    sums = lax.fori_loop(0, QUART, slot, (nothing, nothing))
    at = 8
    for k in range(2):
        for half in range(2):
            for row in terms(sums[k][:, 128 * half : 128 * half + 128]):
                for c in range(4):
                    stat[c, at : at + 1, :] = row
                at += 1
    for c in range(4):
        outs[c, 48] = stat[c].astype(BF16)
    for r, o in enumerate((o0, o1, o2, o3)):
        o[0:49] = outs[(y + r) & 3]
        o[49:65] = tiles[(y + r) & 3]
    for n in range(QUART):
        keep_cells(n).wait()


def placement(rows, columns, code):
    row = lax.broadcasted_iota(jnp.int32, (rows, columns), 0)
    column = lax.broadcasted_iota(jnp.int32, (rows, columns), 1)
    return (code(row) == column).astype(F32).astype(BF16)


def octant_code(v):
    x, y, z = v >> 6, (v >> 3) & 7, v & 7
    octant = (x >> 2) * 4 + (y >> 2) * 2 + (z >> 2)
    return octant * 64 + (x & 3) * 16 + (y & 3) * 4 + (z & 3)


def voxel_code(w):
    octant, x, y, z = w >> 6, (w >> 4) & 3, (w >> 2) & 3, w & 3
    x, y, z = x + 4 * (octant >> 2), y + 4 * ((octant >> 1) & 1), z + 4 * (octant & 1)
    return x * 64 + y * 8 + z


def coarse_code(v):
    return ((v >> 7) & 3) * 16 + ((v >> 4) & 3) * 4 + ((v >> 1) & 3)


def tile_kernel(me, u0, u1, u2, u3, wa, wb, out, units, weights, taps, place, place_t):
    t = pl.program_id(0)
    y = me[0]

    @pl.when(t == 0)
    def _():
        place[...] = placement(VOX, VOX, octant_code)
        place_t[...] = placement(VOX, VOX, voxel_code)
        fill_weights(weights, wa, wb, me[1], 2)

    for r, u in zip(ORDER, (u0, u1, u2, u3)):
        units[(y - r) & 3] = u[...]
    octants = jnp.concatenate(
        [unpack([units[c, o].astype(F32) for c in range(4)]).astype(BF16) for o in range(8)], axis=0
    )
    act = lax.dot_general(place[...], octants, NN, preferred_element_type=F32).astype(BF16)
    interior_taps(act, taps)
    h = lax.dot_general(taps[...], weights[...], NT, preferred_element_type=F32).astype(BF16)
    pieces = lax.dot_general(place_t[...], h, NN, preferred_element_type=F32)
    for o in range(8):
        for c, unit in enumerate(pack(pieces[64 * o : 64 * o + 64])):
            out[c, o] = unit.astype(BF16)


def route2_kernel(
    links, lslot, crecv, me, v0, v1, v2, v3, keep, out, held, cen, stat, send_buf, sem
):
    y = me[0]
    for r, v in zip(ORDER, (v0, v1, v2, v3)):
        held[(y - r) & 3] = v[...]
    kept = pltpu.make_async_copy(held, keep, sem.at[0])
    kept.start()
    total = jnp.zeros((32, 128), F32)
    for q in range(4):
        told = held[q, 48].astype(F32)
        cen[8 * q : 8 * q + 8, :] = told[0:8]
        total = total + told
    stat[...] = jnp.zeros((16, 128), F32)
    for k in range(4):
        put_terms(stat, 2 + 3 * k, joined(total, 8 + 3 * k))

    def send(p, _):
        for k in range(2):
            code = jnp.minimum(links[k, p], FACES - 1)
            slot = lslot[2 * p + k]
            q = slot >> 3
            send_buf[p, 32 * k : 32 * k + 32] = held[q, code - 48 * q]
            stat[k : k + 1, :] = cen[pl.ds(slot, 1), :]
            place = jnp.minimum(crecv[k, p], CODES - 1)
            send_buf[p, 64 + 32 * k : 96 + 32 * k] = held[place >> 4, 49 + (place & 15)]
        send_buf[p, 128:144] = stat[...].astype(BF16)
        return 0

    lax.fori_loop(0, DEVS, send, 0, unroll=4)
    give = pltpu.make_async_copy(send_buf, out, sem.at[1])
    give.start()
    kept.wait()
    give.wait()


def own_row(row, y):
    wide = jnp.broadcast_to(jnp.where(y >= 2, row[:, 128:256], row[:, 0:128]), (8, 128))
    turned = pltpu.roll(wide, 64, 1)
    left = lanes(8) < 64
    odd = (y & 1) == 1
    return jnp.where(left, jnp.where(odd, turned, wide), jnp.where(odd, wide, turned))[0:1]


def border2_kernel(
    sel, ssel, owner, me, rows, held, recv, *refs, away
):
    *outs, norm, src, cen, buf, sem, load = refs
    y = me[0]
    fetches = []
    for q in range(4):
        fetches.append(
            pltpu.make_async_copy(held.at[q, pl.ds(0, 48)], src.at[pl.ds(48 * q, 48)], load.at[q])
        )
        fetches.append(pltpu.make_async_copy(held.at[q, 48], buf.at[q, 0], load.at[4 + q]))
    for fetch in fetches:
        fetch.start()

    def add(s, total):
        src[FACES + 2 * s] = recv[s, 0:32]
        src[FACES + 2 * s + 1] = recv[s, 32:64]
        told = recv[s, 128:144].astype(F32)
        cen[pl.ds(SLOTS + 2 * s, 2), :] = told[0:2]
        return total + told

    sums = lax.fori_loop(0, DEVS, add, jnp.zeros((16, 128), F32), unroll=8)
    src[FACES + 2 * DEVS] = jnp.zeros((32, 128), BF16)
    cen[pl.ds(SLOTS + 2 * DEVS, 8), :] = jnp.zeros((8, 128), F32)
    fine = float(DEVS * SLOTS * VOX * GROUP)
    groups = group_matrix(128)
    norm[...] = jnp.zeros((8, 256), F32)
    for half in range(2):
        cut = slice(128 * half, 128 * half + 128)
        mean, scale = norm_rows(
            group_sum(joined(sums, 2 + 3 * half), groups),
            group_sum(joined(sums, 8 + 3 * half), groups),
            fine,
            rows[4:5, cut],
        )
        norm[0:1, cut] = mean
        norm[1:2, cut] = scale
        norm[2:3, cut] = rows[5:6, cut]
    mean, scale, bias = (own_row(norm[k : k + 1, :], y) for k in range(3))
    for fetch in fetches:
        fetch.wait()
    for q in range(4):
        cen[8 * q : 8 * q + 8, :] = buf[q, 0].astype(F32)[0:8]
    copies = []
    for r, o in zip(away, outs):
        q = (y + r) & 3

        def face(i, _):
            for f in range(6):
                at = sel[q * 48 + i * 6 + f]
                whose = owner[q * 48 + i * 6 + f]
                u = src[at].astype(F32) + (cen[pl.ds(whose, 1), :] - mean)
                v = silu(u * scale + bias)
                buf[r, i * 6 + f] = (v * (at < FACES + 2 * DEVS).astype(F32)).astype(BF16)
            link = ssel[q * 8 + i]
            at = pl.multiple_of(64 + 32 * (link & 1), 32)
            buf[r, 48 + i] = recv[link >> 1, pl.ds(at, 32)]
            return 0

        lax.fori_loop(0, QUART, face, 0)
        copies.append(pltpu.make_async_copy(buf.at[r], o, sem.at[r]))
        copies[-1].start()
    for copy in copies:
        copy.wait()


def outer2_kernel(
    me, part, v0, v1, v2, v3, u0, u1, u2, u3, weights,
    o0, o1, o2, o3,
    units, across, shift, cube, lift,
    *, start,
):
    y = me[0]
    lift[...] = placement(VOX, 64, coarse_code)
    border_terms(units, weights, (u0, u1, u2, u3), y, across, start, HALF)

    def slot(n, _):
        m = start + n
        raised = unpack([units[c, 48 + m].astype(F32) for c in range(4)]).astype(BF16)
        lifted = lax.dot_general(lift[...], raised, NN, preferred_element_type=F32)
        h, _ = add_borders(part[m] + lifted, across, n, shift)
        for r, v in zip(ORDER, (v0, v1, v2, v3)):
            at = pl.multiple_of(((y - r) & 3) * 64, 64)
            cube[pl.ds(at, 64), :] = v[QUART * y + m if r == 0 else m].astype(F32)
        cube[...] += h.T
        for r, o in enumerate((o0, o1, o2, o3)):
            at = pl.multiple_of(((y + r) & 3) * 64, 64)
            o[n] = cube[pl.ds(at, 64), :].astype(BF16)
        return 0

    lax.fori_loop(0, HALF, slot, 0)


def gather_kernel(me, *refs):
    *parts, out, sem = refs
    y = me[0]
    copies = []
    for k, p in enumerate(parts):
        at = ((y - ORDER[k % 4]) & 3) * QUART + HALF * (k // 4)
        copies.append(pltpu.make_async_copy(p, out.at[pl.ds(at, HALF)], sem.at[k]))
        copies[-1].start()
    for copy in copies:
        copy.wait()


def shape(*dims, dtype=BF16):
    return jax.ShapeDtypeStruct(dims, dtype)


def call(kernel, name, mib, micros=1, **more):
    return pl.pallas_call(
        kernel,
        cost_estimate=pl.CostEstimate(
            flops=micros * 10**9, bytes_accessed=micros * 3 * 10**6, transcendentals=0
        ),
        compiler_params=pltpu.CompilerParams(vmem_limit_bytes=mib * MIB),
        name=name,
        **more,
    )


def exchange(parts, order=(0, 1, 2, 3)):
    got = {
        r: lax.ppermute(parts[r], "chan", [(i, (i + r) % 4) for i in order]) for r in ORDER[1:]
    }
    return [parts[0]] + [got[r] for r in ORDER[1:]]


def over_blocks(units):
    return lax.all_to_all(units, "blocks", split_axis=0, concat_axis=0, tiled=True)


def local(
    feats,
    conv_weights,
    norm_gain,
    norm_bias,
    time_bias,
    local_nbr,
    face_links,
    coarse_send,
    coarse_recv,
):
    extract_np = tables()
    y = lax.axis_index("chan").astype(jnp.int32)
    core = (lax.axis_index("blocks") % 2).astype(jnp.int32)
    me = jnp.stack([y, core])
    nbr = local_nbr.T
    links = face_links[0].T
    csend = coarse_send[0].T
    crecv = coarse_recv[0].T

    def twice(rows):
        block = jnp.stack(rows)
        block = jnp.concatenate([block, block], axis=1)
        return jnp.pad(block, ((0, 8 - block.shape[0]), (0, 0)))

    par = twice(
        [norm_gain[0], norm_bias[0], norm_gain[2], norm_bias[2], time_bias]
        + [norm_gain[1], norm_bias[1]]
    )
    faces, outgoing, half = call(
        extract_kernel,
        "extract",
        60,
        out_shape=(
            shape(FACES // 2, 64, 128),
            shape(DEVS, ROWS, 128),
            shape(3, 7, 32, 256),
        ),
        in_specs=[SMEM] * 3 + [HBM] * 3,
        out_specs=(HBM,) * 3,
        scratch_shapes=[
            pltpu.VMEM((SLOTS, 64, VOX), BF16),
            pltpu.VMEM((448, VOX), BF16),
            pltpu.VMEM((FACES // 2, 64, 128), BF16),
            pltpu.VMEM((SLOTS, 32, 128), BF16),
            pltpu.VMEM((16, 128), F32),
            pltpu.VMEM((DEVS, ROWS, 128), BF16),
            pltpu.VMEM((3, 7, 32, 256), BF16),
            pltpu.SemaphoreType.DMA((10,)),
            pltpu.SemaphoreType.DMA((10,)),
        ],
    )(links, csend, me, feats, jnp.asarray(extract_np, BF16), conv_weights)
    wa = lax.all_gather(half, "chan", axis=0, tiled=False)
    arrived = over_blocks(outgoing)
    volumes = exchange(
        [feats]
        + [
            lax.dynamic_slice_in_dim(feats, QUART * ((y + r) % 4), QUART, axis=0)
            for r in range(1, 4)
        ]
    )
    sel, tsel, ssel, owner, lslot = call(
        plan_kernel,
        "plan",
        4,
        20,
        out_shape=(
            shape(FACES, dtype=jnp.int32),
            shape(CODES, dtype=jnp.int32),
            shape(SLOTS, dtype=jnp.int32),
            shape(FACES, dtype=jnp.int32),
            shape(2 * DEVS, dtype=jnp.int32),
        ),
        in_specs=[SMEM] * 4,
        out_specs=(SMEM,) * 5,
    )(nbr, links, csend, crecv)

    parts = call(
        border1_kernel,
        "border1",
        60,
        out_shape=(shape(17, 32, 128),) * 4 + (shape(48, 32, 128),) * 4,
        in_specs=[SMEM] * 3 + [VMEM] + [HBM] * 5,
        out_specs=(HBM,) * 8,
        scratch_shapes=[
            pltpu.VMEM((DEVS, 16, 128), BF16),
            pltpu.VMEM((DEVS, 64, 128), BF16),
            pltpu.VMEM((FACES // 2 + DEVS + 1, 64, 128), BF16),
            pltpu.VMEM((4, 17, 32, 128), BF16),
            pltpu.VMEM((4, 48, 32, 128), BF16),
            pltpu.VMEM((32, 128), F32),
            pltpu.SemaphoreType.DMA((4,)),
            pltpu.SemaphoreType.DMA((4,)),
            pltpu.SemaphoreType.DMA((4,)),
        ],
    )(sel, tsel, me, par, faces, arrived, *volumes[1:])
    tiles1 = exchange(parts[:4], (3, 2, 1, 0))
    units1 = exchange(parts[4:])
    wa, _ = lax.optimization_barrier((wa, parts[0]))
    wb = lax.ppermute(wa, "blocks", [(i, i ^ 1) for i in range(DEVS)])

    cells = pl.BlockSpec((1, VOX, 256), lambda i: (i, 0, 0))

    def prefetched(count, in_specs, out_specs, scratch_shapes):
        return pltpu.PrefetchScalarGridSpec(
            num_scalar_prefetch=1,
            grid=(count,),
            in_specs=in_specs,
            out_specs=out_specs,
            scratch_shapes=scratch_shapes,
        )

    def slot_specs(start):
        first = pl.BlockSpec((1, 64, VOX), lambda i, me: (QUART * me[0] + start + i, 0, 0))
        return [first] + [pl.BlockSpec((1, 64, VOX), lambda i, me: (start + i, 0, 0))] * 3

    def cell_spec(start):
        return pl.BlockSpec((1, VOX, 256), lambda i, me: (start + i, 0, 0))

    last = pl.BlockSpec((1, 32, 128), lambda i, me: (16, 0, 0))
    part1, rows, weights = call(
        inner1_kernel,
        "inner1",
        24,
        8,
        grid_spec=prefetched(
            QUART,
            [last] * 4 + slot_specs(0) + [VMEM] * 2,
            (cell_spec(0), VMEM, VMEM),
            [
                pltpu.VMEM((4, 32, 128), F32),
                pltpu.VMEM((VOX, 1792), BF16),
                pltpu.VMEM((256, VOX), F32),
            ],
        ),
        out_shape=(
            shape(QUART, VOX, 256, dtype=F32),
            shape(8, 256, dtype=F32),
            shape(256, 1792),
        ),
    )(me, *tiles1, *volumes, wa, wb)
    eight = pl.BlockSpec((8, 32, 128), lambda t: (t, 0, 0))
    coarse = call(
        tile_kernel,
        "tiles",
        24,
        4,
        grid=(TILES,),
        out_shape=shape(4, 16, 32, 128),
        in_specs=[SMEM] + [eight] * 4 + [VMEM] * 2,
        out_specs=pl.BlockSpec((4, 8, 32, 128), lambda t: (0, t, 0, 0)),
        scratch_shapes=[
            pltpu.VMEM((4, 8, 32, 128), BF16),
            pltpu.VMEM((256, 1792), BF16),
            pltpu.VMEM((VOX, 1792), BF16),
            pltpu.VMEM((VOX, VOX), BF16),
            pltpu.VMEM((VOX, VOX), BF16),
        ],
    )(me, *tiles1, wa, wb)
    hidden, *parts = call(
        outer1_kernel,
        "outer1",
        32,
        5,
        out_shape=(shape(QUART, VOX, 256, dtype=F32),) + (shape(65, 32, 128),) * 4,
        in_specs=[SMEM] + [VMEM] * 8,
        out_specs=(HBM,) + (VMEM,) * 4,
        scratch_shapes=[
            pltpu.VMEM((4, 48, 32, 128), BF16),
            pltpu.VMEM((4, 49, 32, 128), BF16),
            pltpu.VMEM((6, VOX, 256), F32),
            pltpu.VMEM((2, VOX, 128), F32),
            pltpu.VMEM((4, 32, 128), F32),
            pltpu.VMEM((QUART, VOX, 256), F32),
            pltpu.SemaphoreType.DMA((QUART,)),
        ],
    )(me, rows, part1, *units1, coarse, weights)
    units = exchange(parts)

    held, outgoing = call(
        route2_kernel,
        "route2",
        12,
        out_shape=(shape(4, 65, 32, 128), shape(DEVS, ROWS, 128)),
        in_specs=[SMEM] * 4 + [VMEM] * 4,
        out_specs=(HBM, HBM),
        scratch_shapes=[
            pltpu.VMEM((4, 65, 32, 128), BF16),
            pltpu.VMEM((SLOTS, 128), F32),
            pltpu.VMEM((16, 128), F32),
            pltpu.VMEM((DEVS, ROWS, 128), BF16),
            pltpu.SemaphoreType.DMA((2,)),
        ],
    )(links, lslot, crecv, me, *units)
    arrived = over_blocks(outgoing)

    def border2(*away):
        return call(
            functools.partial(border2_kernel, away=away),
            "border2",
            12,
            out_shape=(shape(56, 32, 128),) * len(away) + (shape(8, 256, dtype=F32),),
            in_specs=[SMEM] * 4 + [VMEM, HBM, VMEM],
            out_specs=(ANY,) * len(away) + (VMEM,),
            scratch_shapes=[
                pltpu.VMEM((FACES + 2 * DEVS + 1, 32, 128), BF16),
                pltpu.VMEM((SLOTS + 2 * DEVS + 8, 128), F32),
                pltpu.VMEM((4, 56, 32, 128), BF16),
                pltpu.SemaphoreType.DMA((4,)),
                pltpu.SemaphoreType.DMA((8,)),
            ],
        )(sel, ssel, owner, me, rows, held, arrived)

    first, norm = border2(2)
    own, *rest, _ = border2(0, 1, 3)
    parts = [own, rest[0], first, rest[1]]
    units2 = exchange(parts)
    part2, weights = call(
        inner2_kernel,
        "inner2",
        24,
        8,
        grid=(QUART,),
        out_shape=(shape(QUART, VOX, 256, dtype=F32), shape(256, 1792)),
        in_specs=[SMEM, VMEM, HBM, VMEM, VMEM],
        out_specs=(cells, VMEM),
        scratch_shapes=[
            pltpu.VMEM((VOX, 1792), BF16),
            pltpu.VMEM((QUART, VOX, 256), F32),
            pltpu.SemaphoreType.DMA((QUART,)),
        ],
    )(me, norm, hidden, wa, wb)
    pieces = []
    for start in (0, HALF):
        parts = call(
            functools.partial(outer2_kernel, start=start),
            "outer2",
            32,
            5,
            in_specs=[SMEM] + [VMEM] * 10,
            out_specs=(VMEM,) * 4,
            scratch_shapes=[
                pltpu.VMEM((4, 56, 32, 128), BF16),
                pltpu.VMEM((6, 64 * HALF, 256), F32),
                pltpu.VMEM((2, VOX, 128), F32),
                pltpu.VMEM((256, VOX), F32),
                pltpu.VMEM((VOX, 64), BF16),
            ],
            out_shape=(shape(HALF, 64, VOX),) * 4,
        )(me, part2, *volumes, *units2, weights)
        pieces += exchange(parts, (0, 1, 2, 3) if start == 0 else (3, 2, 1, 0))
    return call(
        gather_kernel,
        "gather",
        4,
        out_shape=shape(SLOTS, 64, VOX),
        in_specs=[SMEM] + [ANY] * 8,
        out_specs=HBM,
        scratch_shapes=[pltpu.SemaphoreType.DMA((8,))],
    )(me, *pieces)


def solution(mesh):
    in_specs = (
        P("blocks", "chan", None),
        P(None, None, "chan", None),
        P(None, "chan"),
        P(None, "chan"),
        P("chan"),
        P("blocks", None),
        P("blocks", None, None),
        P("blocks", None, None),
        P("blocks", None, None),
    )
    out_specs = P("blocks", "chan", None)
    return jax.shard_map(local, mesh=mesh, in_specs=in_specs, out_specs=out_specs, check_vma=False)
```
